32 devices in a mesh: dp: 8 (over y, x, core), seq: 4 (over z).
Axes of the slice: x: 2, y: 2, z: 4, core: 2. Of those that a mesh axis runs over, the one named last changes fastest.
Arguments:
- patches: bfloat16 [96, 196, 768], P('dp', 'seq'), may hold values from -6 to 6
- specials: bfloat16 [96, 2, 768], P('dp'), may hold values from -6 to 6
- keep_mask: int32 [96, 2], P('dp'), may hold values 0 or 1
- ln1_gain: bfloat16 [768], replicated, may hold values from 0.5 to 1.5
- ln1_bias: bfloat16 [768], replicated, may hold values from -1 to 1
- qkv_weight: bfloat16 [768, 2304], replicated, may hold values from -0.21875 to 0.21875
- qv_bias: bfloat16 [2, 768], replicated, may hold values from -1 to 1
- proj_weight: bfloat16 [768, 768], replicated, may hold values from -1.75 to 1.75
- proj_bias: bfloat16 [768], replicated, may hold values from -1 to 1
- ln2_gain: bfloat16 [768], replicated, may hold values from 0.5 to 1.5
- ln2_bias: bfloat16 [768], replicated, may hold values from -1 to 1
- fc1_weight: bfloat16 [768, 3072], replicated, may hold values from -0.21875 to 0.21875
- fc1_bias: bfloat16 [3072], replicated, may hold values from -1 to 1
- fc2_weight: bfloat16 [3072, 768], replicated, may hold values from -0.109375 to 0.109375
- fc2_bias: bfloat16 [768], replicated, may hold values from -1 to 1
- grad_patches: bfloat16 [96, 196, 768], P('dp', 'seq'), may hold values from -6 to 6
- grad_specials: bfloat16 [96, 2, 768], P('dp'), may hold values from -6 to 6
Outputs:
- out_patches: bfloat16 [96, 196, 768], P('dp', 'seq')
- out_specials: bfloat16 [96, 2, 768], P('dp')
- dx_patches: bfloat16 [96, 196, 768], P('dp', 'seq')
- dx_specials: bfloat16 [96, 2, 768], P('dp')
- d_ln1_gain: float32 [768], P('dp')
- d_ln1_bias: float32 [768], P('dp')
- d_qkv_weight: float32 [768, 2304], P('dp')
- d_qv_bias: float32 [2, 768], P(None, 'dp')
- d_proj_weight: float32 [768, 768], P('dp')
- d_proj_bias: float32 [768], P('dp')
- d_ln2_gain: float32 [768], P('dp')
- d_ln2_bias: float32 [768], P('dp')
- d_fc1_weight: float32 [768, 3072], P('dp')
- d_fc1_bias: float32 [3072], P('dp')
- d_fc2_weight: float32 [3072, 768], P('dp')
- d_fc2_bias: float32 [768], P('dp')
The draws below stay inside these ranges and needn't reach their ends.
All inputs are finite; a program needn't handle non-finite values. No bound on the sum of `keep_mask` on one device may be relied on, other than what follows from the above.
Results may differ from the reference program's by a relative error of at most 0.014.
Values may be sent and summed in bfloat16 or wider, within the bound.
No kernel may reach another device: no remote copies, remote signals or barrier semaphores. Data moves between devices by JAX's collectives and lax.ppermute only.
A program may use at most 192 MiB of HBM per device.

```python
import jax
import jax.numpy as jnp
from jax import lax

D = 768
HEAD_DIM = 64
FF = 3072
PATCHES = 196
IMAGES = 96


def place_ends(drawn, key, least, top_value):
    extent = drawn.shape
    spot = [jax.random.randint(jax.random.fold_in(key, axis), (), 0, extent[axis]) for axis in range(len(extent))]
    drawn = drawn.at[tuple(spot)].set(least)
    longest = extent.index(max(extent))
    spot[longest] = (spot[longest] + 1) % extent[longest]
    return drawn.at[tuple(spot)].set(top_value)


def block_levels(rng, dims, shards, least, top_value):
    level, own = 1.0, jax.random.fold_in(rng, 6)
    for dim, blocks in shards:
        heights = jnp.exp(jax.random.uniform(jax.random.fold_in(own, dim), (blocks,), jnp.float32, least / len(shards), top_value / len(shards)))
        level = level * jnp.repeat(heights, dims[dim] // blocks).reshape([-1 if axis == dim else 1 for axis in range(len(dims))])
    return level


def scatter_about(stream_key, shape, width, most, split=(), dtype=jnp.bfloat16):
    values = width * jax.random.normal(stream_key, shape, jnp.float32)
    if split:
        values = values * block_levels(stream_key, shape, split, -0.22, 0.18)
    return jnp.clip(values, -most, most).astype(dtype)


def setup_inputs(seed: int = 0) -> dict:
    key_list = jax.random.split(jax.random.key(seed), 18)
    return {
        "patches": scatter_about(key_list[0], (IMAGES, PATCHES, D), 1.0, 6.0, ((0, 8), (1, 4))),
        "specials": scatter_about(key_list[1], (IMAGES, 2, D), 1.0, 6.0, ((0, 8),)),
        "keep_mask": place_ends((jax.random.randint(key_list[2], (IMAGES, 2), 0, 10) < 9).astype(jnp.int32), jax.random.fold_in(key_list[2], 1), 0, 1),
        "ln1_gain": jnp.clip(1.0 + 0.1 * jax.random.normal(key_list[3], (D,), jnp.float32), 0.5, 1.5).astype(jnp.bfloat16),
        "ln1_bias": scatter_about(key_list[4], (D,), 0.2, 1.0),
        "qkv_weight": scatter_about(key_list[5], (D, 3 * D), D ** -0.5, 0.21875),
        "qv_bias": scatter_about(key_list[6], (2, D), 0.2, 1.0),
        "proj_weight": scatter_about(key_list[7], (D, D), (D // 64) ** -0.5, 1.75),
        "proj_bias": scatter_about(key_list[8], (D,), 0.2, 1.0),
        "ln2_gain": jnp.clip(1.0 + 0.1 * jax.random.normal(key_list[9], (D,), jnp.float32), 0.5, 1.5).astype(jnp.bfloat16),
        "ln2_bias": scatter_about(key_list[10], (D,), 0.2, 1.0),
        "fc1_weight": scatter_about(key_list[11], (D, FF), D ** -0.5, 0.21875),
        "fc1_bias": scatter_about(key_list[12], (FF,), 0.2, 1.0),
        "fc2_weight": scatter_about(key_list[13], (FF, D), FF ** -0.5, 0.109375),
        "fc2_bias": scatter_about(key_list[14], (D,), 0.2, 1.0),
        "grad_patches": scatter_about(key_list[15], (IMAGES, PATCHES, D), 1.0, 6.0, ((0, 8), (1, 4))),
        "grad_specials": scatter_about(key_list[16], (IMAGES, 2, D), 1.0, 6.0, ((0, 8),)),
    }


@jax.custom_vjp
def low(v):
    return lax.optimization_barrier(v.astype(jnp.bfloat16)).astype(jnp.float32)

@jax.custom_vjp
def low_back(v):
    return v

def low_keep(v):
    return (low(v), None)

def low_pass(kept, grad):
    return (grad,)

def back_keep(v):
    return (v, None)

def back_low(kept, grad):
    return (low(grad),)
low.defvjp(low_keep, low_pass)
low_back.defvjp(back_keep, back_low)
keep_rate = 0.9
epsilon = 1e-06
highest_precision = lax.Precision.HIGHEST

def layer_norm(row_block, norm_gain, norm_shift):
    center = row_block - lax.optimization_barrier(jnp.mean(row_block, axis=-1, keepdims=True))
    variance = lax.optimization_barrier(jnp.mean(center * center, axis=-1, keepdims=True))
    return center * lax.rsqrt(variance + epsilon) * norm_gain + norm_shift

def matmul(row_block, weight):
    return jnp.einsum('grd,de->gre', row_block, weight, precision=highest_precision)

def layer_forward(inputs, params, keep_flags):
    gain_one, shift_one, qkv_matrix, qv_shift, proj_matrix, proj_shift, gain_two, shift_two, first_matrix, first_shift, second_matrix, second_shift = params
    image_count, row_count, feature_width = inputs.shape
    head_count = feature_width // HEAD_DIM
    normed_one = low(layer_norm(inputs, gain_one, shift_one))
    qkv_shift = jnp.concatenate([qv_shift[0], jnp.zeros((feature_width,), jnp.float32), qv_shift[1]])
    qkv_rows = low_back(low(matmul(normed_one, qkv_matrix) + qkv_shift))
    queries = qkv_rows[..., :feature_width].reshape(image_count, row_count, head_count, HEAD_DIM)
    key_rows = qkv_rows[..., feature_width:2 * feature_width].reshape(image_count, row_count, head_count, HEAD_DIM)
    value_rows = qkv_rows[..., 2 * feature_width:].reshape(image_count, row_count, head_count, HEAD_DIM)
    scores = low_back(jnp.einsum('glhd,gmhd->ghlm', queries, key_rows, precision=highest_precision) * HEAD_DIM ** (-0.5))
    exponent = jnp.exp(scores - lax.optimization_barrier(jnp.max(scores, axis=-1, keepdims=True)))
    attention = low(exponent / lax.optimization_barrier(jnp.sum(exponent, axis=-1, keepdims=True)))
    context = jnp.einsum('ghlm,gmhd->glhd', attention, value_rows, precision=highest_precision)
    context = low_back(low(context.reshape(image_count, row_count, feature_width)))
    branch = low_back(matmul(context, proj_matrix) + proj_shift)
    attn_keep = (keep_flags[:, 0] / keep_rate)[:, None, None]
    mlp_keep = (keep_flags[:, 1] / keep_rate)[:, None, None]
    middle = inputs + attn_keep * branch
    normed_two = low(layer_norm(middle, gain_two, shift_two))
    hidden = low_back(matmul(normed_two, first_matrix) + first_shift)
    activated = low(jax.nn.gelu(hidden, approximate=False))
    mlp_out = low_back(matmul(activated, second_matrix) + second_shift)
    return middle + mlp_keep * mlp_out

def reference(patches, specials, keep_mask, ln1_gain, ln1_bias, qkv_weight, qv_bias, proj_weight, proj_bias, ln2_gain, ln2_bias, fc1_weight, fc1_bias, fc2_weight, fc2_bias, grad_patches, grad_specials):
    image_group = max([size_try for size_try in range(1, 21) if IMAGES % size_try == 0])
    group_count = IMAGES // image_group
    seq_rows = PATCHES + 2
    inputs = jnp.concatenate([specials, patches], axis=1).astype(jnp.float32)
    inputs = inputs.reshape(group_count, image_group, seq_rows, D)
    cotangent = jnp.concatenate([grad_specials, grad_patches], axis=1).astype(jnp.float32)
    cotangent = cotangent.reshape(group_count, image_group, seq_rows, D)
    keep_flags = keep_mask.astype(jnp.float32).reshape(group_count, image_group, 2)
    params = tuple((weight.astype(jnp.float32) for weight in (ln1_gain, ln1_bias, qkv_weight, qv_bias, proj_weight, proj_bias, ln2_gain, ln2_bias, fc1_weight, fc1_bias, fc2_weight, fc2_bias)))

    def step(totals, pieces):
        block_rows, block_grads, block_flags = pieces

        def inner(rows_in, weights_in):
            return layer_forward(rows_in, weights_in, block_flags)
        result, pullback = jax.vjp(inner, block_rows, params)
        grad_rows, grad_params = pullback(block_grads)
        totals = jax.tree.map(jnp.add, totals, grad_params)
        return (totals, (result.astype(jnp.bfloat16), grad_rows.astype(jnp.bfloat16)))
    zero_totals = jax.tree.map(jnp.zeros_like, params)
    totals, (outputs, gradients) = lax.scan(step, zero_totals, (inputs, cotangent, keep_flags))
    outputs = outputs.reshape(IMAGES, seq_rows, D)
    gradients = gradients.reshape(IMAGES, seq_rows, D)
    return (outputs[:, 2:], outputs[:, :2], gradients[:, 2:], gradients[:, :2], totals[0], totals[1], totals[2], totals[3], totals[4], totals[5], totals[6], totals[7], totals[8], totals[9], totals[10], totals[11])
```

```python
from functools import partial

import jax
import jax.numpy as jnp
from jax import lax
from jax.experimental import pallas as pl
from jax.experimental.pallas import tpu as pltpu
from jax.sharding import PartitionSpec as P

HEAD_DIM = 64
KEEP = 1.0 / 0.9
EPS = 1e-06
BF = jnp.bfloat16
F32 = jnp.float32
OWNERS = 8
VMEM = 60 * 2**20

ERF_P = 0.425
ERF_C = (
    0.2396707695899643,
    0.2419609266760862,
    0.1999560009093125,
    0.2575598334337707,
    -0.1079240365384954,
    0.4126939875393689,
    -0.3161029975019298,
    0.07218539595215835,
)


def dot(a, b):
    return lax.dot_general(a, b, (((1,), (0,)), ((), ())), preferred_element_type=F32)


def dot_nt(a, b):
    return lax.dot_general(a, b, (((1,), (1,)), ((), ())), preferred_element_type=F32)


def dot_tn(a, b):
    return lax.dot_general(a, b, (((0,), (0,)), ((), ())), preferred_element_type=F32)


def gelu_both(u):
    t = 1.0 / (1.0 + (ERF_P * 0.5**0.5) * jnp.abs(u))
    poly = jnp.full_like(t, 0.5 * ERF_C[-1])
    for c in ERF_C[-2::-1]:
        poly = poly * t + 0.5 * c
    bell = jnp.exp(-0.5 * u * u)
    tail = poly * t * bell
    cdf = jnp.where(u >= 0, 1.0 - tail, tail)
    return u * cdf, cdf + u * (bell * 0.3989422804014327)


def normalize(x):
    center = x - jnp.mean(x, axis=-1, keepdims=True)
    inv = lax.rsqrt(jnp.mean(center * center, axis=-1, keepdims=True) + EPS)
    return center * inv, inv


def norm_back(up, hat, inv, gain):
    e = up * gain
    return inv * (
        e
        - jnp.mean(e, axis=-1, keepdims=True)
        - hat * jnp.mean(e * hat, axis=-1, keepdims=True)
    )


def colsum(v):
    return jnp.sum(v, axis=0, keepdims=True)


def place(b):
    return (b & 1) * (OWNERS // 2) + lax.shift_right_logical(b, 1)


def store_relative(ref, lead, value, d):
    n = value.shape[0] // OWNERS
    for b in range(OWNERS):
        spot = pl.multiple_of(place(b ^ d) * n, n)
        ref[lead, pl.ds(spot, n), :] = value[b * n : (b + 1) * n]


def forward_kernel(
    at, keep, x0, x1, x2, x3, sp, g1, b1, wq, bq, wp, bp, g2, b2,
    xs, a1t, qkv, prob, ot, h, a2, a2t, buf, *, rows, heads,
):
    i = pl.program_id(0)
    d = at[1]
    part = x0.shape[1]
    ns = sp.shape[1]
    width = x0.shape[2]
    buf[...] = jnp.zeros_like(buf)
    buf[0:ns, :] = sp[0].astype(F32)
    for k, ref in enumerate((x0, x1, x2, x3)):
        buf[ns + k * part : ns + (k + 1) * part, :] = ref[0].astype(F32)
    x = buf[...]
    xs[0] = x.astype(BF)
    hat, _ = normalize(x)
    a1 = (hat * g1[...].astype(F32) + b1[...].astype(F32)).astype(BF)
    store_relative(a1t, 0, a1.astype(F32).T.astype(BF), d)
    both = (dot(a1, wq[...]) + bq[...]).astype(BF)
    qkv[0] = both
    padded = x.shape[0]
    low = lax.broadcasted_iota(jnp.int32, (padded, 2 * HEAD_DIM), 1) < HEAD_DIM
    seen = lax.broadcasted_iota(jnp.int32, (padded, padded), 1) < rows
    outs = []
    for j in range(heads // 2):
        c = j * 2 * HEAD_DIM
        q = both[:, c : c + 2 * HEAD_DIM] * BF(HEAD_DIM**-0.5)
        k = both[:, width + c : width + c + 2 * HEAD_DIM]
        v = both[:, 2 * width + c : 2 * width + c + 2 * HEAD_DIM]
        pair = []
        for side in range(2):
            mine = low if side == 0 else ~low
            s = dot_nt(jnp.where(mine, q, BF(0)), k)
            s = jnp.where(seen, s, -1e30)
            e = jnp.exp(s - jnp.max(s, axis=-1, keepdims=True))
            p = (e * (1.0 / jnp.sum(e, axis=-1, keepdims=True))).astype(BF)
            prob[0, 2 * j + side] = p
            pair.append(dot(p, v))
        outs.append(jnp.where(low, pair[0], pair[1]))
    o32 = jnp.concatenate(outs, axis=1)
    store_relative(ot, 0, o32.T.astype(BF), d)
    y = dot(o32.astype(BF), wp[...]) + bp[...].astype(F32)
    m1 = keep[at[0] * pl.num_programs(0) + i, 0].astype(F32) * KEEP
    hh = x + m1 * y
    h[0] = hh
    hat2, _ = normalize(hh)
    n2 = hat2 * g2[...].astype(F32) + b2[...].astype(F32)
    a2[0] = n2.astype(BF)
    store_relative(a2t, 0, n2.T.astype(BF), d)


def feed_kernel(
    at, keep, g0, g1, g2, g3, sg, h, a2, a2t, w1, b1, w2, b2, gain,
    o0, o1, o2, o3, dh, dy, w2s, w2k, w1s, w1k, db1, small,
    dout, dz, z, da2, gl, *, images, rows,
):
    t = pl.program_id(0)
    steps = pl.num_programs(0)
    part = g0.shape[1]
    ns = sg.shape[1]
    padded = h.shape[1]

    @pl.when(t == 0)
    def _():
        for i in range(images):
            m2 = keep[at[0] * images + i, 1].astype(F32) * KEEP
            r = i * padded
            dout[r : r + padded, :] = jnp.zeros((padded, dout.shape[1]), F32)
            dout[r : r + ns, :] = sg[i].astype(F32)
            for k, ref in enumerate((g0, g1, g2, g3)):
                lo = r + ns + k * part
                dout[lo : lo + part, :] = ref[i].astype(F32)
            dz[r : r + padded, :] = (dout[r : r + padded, :] * m2).astype(BF)
        z[...] = jnp.zeros_like(z)
        da2[...] = jnp.zeros_like(da2)

    wa = w1[...]
    wb = w2[...]
    bias = b1[...].astype(F32)
    grad1 = None
    db = None
    for i in range(images):
        r = slice(i * padded, (i + 1) * padded)
        u = dot(a2[i], wa) + bias
        dg = dot_nt(dz[r, :], wb)
        act, slope = gelu_both(u)
        act = act.astype(BF)
        du = (slope * dg).astype(BF)
        gl[r, :] = act
        z[r, :] += dot(act, wb)
        da2[r, :] += dot_nt(du, wa)
        g = dot(a2t[i], du)
        s = colsum(du.astype(F32))
        grad1 = g if grad1 is None else grad1 + g
        db = s if db is None else db + s
    db1[...] = db
    half = grad1.shape[0] // 2
    w1k[...] = grad1[:half].astype(BF)
    w1s[...] = grad1[half:].astype(BF)
    grad2 = dot_tn(gl[...], dz[...]).astype(BF)

    @pl.when(t < steps // 2)
    def _():
        w2s[...] = grad2

    @pl.when(t >= steps // 2)
    def _():
        w2k[...] = grad2

    @pl.when(t == steps - 1)
    def _():
        gains = gain[...].astype(F32)
        sums = [jnp.zeros((1, dout.shape[1]), F32) for _ in range(4)]
        for i in range(images):
            n = at[0] * images + i
            m1 = keep[n, 0].astype(F32) * KEEP
            m2 = keep[n, 1].astype(F32) * KEEP
            r = slice(i * padded, (i + 1) * padded)
            x = h[i]
            z[r, :] = x + m2 * (z[r, :] + b2[...].astype(F32))
            hat, inv = normalize(x)
            up = da2[r, :]
            grad = dout[r, :] + norm_back(up, hat, inv, gains)
            dh[i] = grad
            low = (m1 * grad).astype(BF)
            dy[i] = low
            for j, v in enumerate((up * hat, up, dz[r, :].astype(F32), low.astype(F32))):
                sums[j] = sums[j] + colsum(v)
            for k, ref in enumerate((o0, o1, o2, o3)):
                lo = i * padded + ns + k * part
                ref[i] = jnp.concatenate(
                    [z[lo : lo + part, :], z[i * padded : i * padded + ns, :]], axis=0
                ).astype(BF)
        small[...] = jnp.concatenate(sums, axis=0)


def heads_kernel(
    dy, prob, qkv, a1t, ot, wp,
    dqkv, cs, ck, ds_, dk_, flat,
    acc, accp, *, heads,
):
    i = pl.program_id(0)
    width = dy.shape[2]
    padded = dy.shape[1]
    low = lax.broadcasted_iota(jnp.int32, (padded, 2 * HEAD_DIM), 1) < HEAD_DIM
    do = dot_nt(dy[0], wp[...]).astype(BF)
    for j in range(heads // 2):
        c = j * 2 * HEAD_DIM
        pair = slice(c, c + 2 * HEAD_DIM)
        q = qkv[0, :, c : c + 2 * HEAD_DIM]
        k = qkv[0, :, width + c : width + c + 2 * HEAD_DIM]
        v = qkv[0, :, 2 * width + c : 2 * width + c + 2 * HEAD_DIM]
        g = do[:, pair]
        got = []
        for side in range(2):
            mine = low if side == 0 else ~low
            p = prob[0, 2 * j + side]
            p32 = p.astype(F32)
            dp = dot_nt(jnp.where(mine, g, BF(0)), v)
            w = p32 * dp
            ds = (w - p32 * jnp.sum(w, axis=-1, keepdims=True)).astype(BF)
            got.append((dot(ds, k), dot_tn(ds, q), dot_tn(p, g)))
        scale = HEAD_DIM**-0.5
        dqkv[0, :, c : c + 2 * HEAD_DIM] = (jnp.where(low, got[0][0], got[1][0]) * scale).astype(BF)
        dqkv[0, :, width + c : width + c + 2 * HEAD_DIM] = (
            jnp.where(low, got[0][1], got[1][1]) * scale
        ).astype(BF)
        dqkv[0, :, 2 * width + c : 2 * width + c + 2 * HEAD_DIM] = jnp.where(
            low, got[0][2], got[1][2]
        ).astype(BF)
    grads = dqkv[0]
    more = dot(a1t[0], grads)
    morep = dot(ot[0], dy[0])
    tops = colsum(grads.astype(F32))

    @pl.when(i == 0)
    def _():
        acc[...] = more
        accp[...] = morep
        flat[...] = tops

    @pl.when(i > 0)
    def _():
        acc[...] += more
        accp[...] += morep
        flat[...] += tops

    @pl.when(i == pl.num_programs(0) - 1)
    def _():
        half = acc.shape[0] // 2
        for rows, c_ref, d_ref in ((slice(0, half), ck, dk_), (slice(half, 2 * half), cs, ds_)):
            c_ref[...] = acc[rows, : 2 * width].astype(BF)
            d_ref[:, :width] = acc[rows, 2 * width :].astype(BF)
            d_ref[:, width:] = accp[rows, :].astype(BF)


def input_kernel(dqkv, wq, xs, dh, gain, o0, o1, o2, o3, small, buf, *, part, ns):
    i = pl.program_id(0)
    up = dot_nt(dqkv[0], wq[...])
    hat, inv = normalize(xs[0].astype(F32))
    buf[...] = dh[0] + norm_back(up, hat, inv, gain[...].astype(F32))
    for k, ref in enumerate((o0, o1, o2, o3)):
        lo = ns + k * part
        ref[0] = jnp.concatenate([buf[lo : lo + part, :], buf[0:ns, :]], axis=0).astype(BF)
    sums = jnp.concatenate([colsum(up * hat), colsum(up)], axis=0)

    @pl.when(i == 0)
    def _():
        small[...] = sums

    @pl.when(i > 0)
    def _():
        small[...] += sums


def gather_kernel(at, c0, c1, c2, c3, rows, specials):
    k = pl.program_id(0)
    part = rows.shape[1]
    for j, ref in enumerate((c0, c1, c2, c3)):

        @pl.when(k == j)
        def _(ref=ref):
            rows[...] = ref[:, :part, :]
            specials[...] = ref[:, part:, :]


def whole(shape):
    return pl.BlockSpec(shape, lambda *_: (0,) * len(shape))


def params():
    return pltpu.CompilerParams(
        dimension_semantics=("arbitrary",), vmem_limit_bytes=VMEM
    )


def cost(flops, read):
    return pl.CostEstimate(flops=int(flops), bytes_accessed=int(read), transcendentals=0)


def struct(*shape, dtype=BF):
    return jax.ShapeDtypeStruct(shape, dtype)


def send_around(x, groups):
    me = lax.axis_index("seq")
    n = x.shape[0] // groups
    got = []
    for k in range(1, groups):
        block = lax.dynamic_slice_in_dim(x, n * ((me + k) % groups), n)
        got.append(lax.ppermute(block, "seq", [(s, (s + k) % groups) for s in range(groups)]))
    return got


def send_back(chunks, groups):
    return [chunks[0]] + [
        lax.ppermute(c, "seq", [(s, (s - k) % groups) for s in range(groups)])
        for k, c in enumerate(chunks)
        if k
    ]


def settle(chunks, at, groups, part, ns):
    n, _, width = chunks[0].shape
    return pl.pallas_call(
        gather_kernel,
        grid_spec=pltpu.PrefetchScalarGridSpec(
            num_scalar_prefetch=1,
            grid=(groups,),
            in_specs=[whole(c.shape) for c in chunks],
            out_specs=[
                pl.BlockSpec((n, part, width), lambda k, at: ((at[0] + k) % groups, 0, 0)),
                pl.BlockSpec((n, ns, width), lambda k, at: ((at[0] + k) % groups, 0, 0)),
            ],
        ),
        out_shape=[struct(n * groups, part, width), struct(n * groups, ns, width)],
        compiler_params=params(),
        name="settle",
    )(at, *chunks)


def shards(
    patches, specials, keep_mask, ln1_gain, ln1_bias, qkv_weight, qv_bias, proj_weight, proj_bias,
    ln2_gain, ln2_bias, fc1_weight, fc1_bias, fc2_weight, fc2_bias, grad_patches, grad_specials,
):
    images, part, width = patches.shape
    ns = specials.shape[1]
    groups = lax.axis_size("seq")
    replicas = lax.axis_size("dp")
    hidden = fc1_weight.shape[1]
    heads = width // HEAD_DIM
    n = images // groups
    rows = ns + groups * part
    padded = -(-rows // 16) * 16
    chunk = hidden // OWNERS
    half = width // 2
    direct = replicas == OWNERS
    me = lax.axis_index("seq")
    d = lax.axis_index("dp") if direct else jnp.int32(0)
    at = jnp.stack([me, d]).astype(jnp.int32)

    def row(v):
        return v.reshape(1, -1)

    got = send_around(patches, groups)
    got_grad = send_around(grad_patches, groups)
    zero = jnp.zeros((width,), F32)
    qkv_bias = row(jnp.concatenate([qv_bias[0].astype(F32), zero, qv_bias[1].astype(F32)]))

    own = pl.BlockSpec((1, part, width), lambda i, at, keep: (at[0] * n + i, 0, 0))
    block = pl.BlockSpec((1, part, width), lambda i, at, keep: (i, 0, 0))

    def per_image(*shape):
        return pl.BlockSpec((1, *shape), lambda i, *_: (i,) + (0,) * len(shape))

    xs, a1t, qkv, prob, ot, h, a2, a2t = pl.pallas_call(
        partial(forward_kernel, rows=rows, heads=heads),
        grid_spec=pltpu.PrefetchScalarGridSpec(
            num_scalar_prefetch=2,
            grid=(n,),
            in_specs=[
                own, block, block, block,
                pl.BlockSpec((1, ns, width), lambda i, at, keep: (at[0] * n + i, 0, 0)),
                whole((1, width)), whole((1, width)),
                whole(qkv_weight.shape), whole((1, 3 * width)),
                whole(proj_weight.shape), whole((1, width)), whole((1, width)), whole((1, width)),
            ],
            out_specs=[
                per_image(padded, width), per_image(width, padded), per_image(padded, 3 * width),
                per_image(heads, padded, padded), per_image(width, padded),
                per_image(padded, width), per_image(padded, width), per_image(width, padded),
            ],
            scratch_shapes=[pltpu.VMEM((padded, width), F32)],
        ),
        out_shape=[
            struct(n, padded, width), struct(n, width, padded), struct(n, padded, 3 * width),
            struct(n, heads, padded, padded), struct(n, width, padded),
            struct(n, padded, width, dtype=F32), struct(n, padded, width), struct(n, width, padded),
        ],
        compiler_params=params(),
        cost_estimate=cost(2 * n * padded * width * 6 * width, 20e6),
        name="attention_forward",
    )(
        at, keep_mask, patches, *got, specials, row(ln1_gain), row(ln1_bias), qkv_weight, qkv_bias,
        proj_weight, row(proj_bias), row(ln2_gain), row(ln2_bias),
    )

    steps = OWNERS

    def owner(t, at):
        relative = jnp.where(t < steps // 2, 2 * t + 1, 2 * t - steps)
        return relative ^ at[1]

    total = n * padded
    outs = pl.pallas_call(
        partial(feed_kernel, images=n, rows=rows),
        grid_spec=pltpu.PrefetchScalarGridSpec(
            num_scalar_prefetch=2,
            grid=(steps,),
            in_specs=[
                pl.BlockSpec((n, part, width), lambda t, at, keep: (at[0], 0, 0)),
                *[whole((n, part, width))] * 3,
                pl.BlockSpec((n, ns, width), lambda t, at, keep: (at[0], 0, 0)),
                whole(h.shape), whole(a2.shape), whole(a2t.shape),
                pl.BlockSpec((width, chunk), lambda t, at, keep: (0, owner(t, at))),
                pl.BlockSpec((1, chunk), lambda t, at, keep: (0, owner(t, at))),
                pl.BlockSpec((chunk, width), lambda t, at, keep: (owner(t, at), 0)),
                whole((1, width)), whole((1, width)),
            ],
            out_specs=[
                *[whole((n, part + ns, width))] * 4,
                whole((n, padded, width)), whole((n, padded, width)),
                pl.BlockSpec((chunk, width), lambda t, *_: (jnp.minimum(t, steps // 2 - 1), 0)),
                pl.BlockSpec((chunk, width), lambda t, *_: (jnp.maximum(t - steps // 2, 0), 0)),
                pl.BlockSpec((half, chunk), lambda t, at, keep: (0, owner(t, at))),
                pl.BlockSpec((half, chunk), lambda t, at, keep: (0, owner(t, at))),
                pl.BlockSpec((1, chunk), lambda t, at, keep: (0, owner(t, at))),
                whole((4, width)),
            ],
            scratch_shapes=[
                pltpu.VMEM((total, width), F32), pltpu.VMEM((total, width), BF),
                pltpu.VMEM((total, width), F32), pltpu.VMEM((total, width), F32),
                pltpu.VMEM((total, chunk), BF),
            ],
        ),
        out_shape=[
            *[struct(n, part + ns, width)] * 4,
            struct(n, padded, width, dtype=F32), struct(n, padded, width),
            struct(hidden // 2, width), struct(hidden // 2, width),
            struct(half, hidden), struct(half, hidden),
            struct(1, hidden, dtype=F32), struct(4, width, dtype=F32),
        ],
        compiler_params=params(),
        cost_estimate=cost(12 * total * width * hidden, 40e6),
        name="feed_forward",
    )(
        at, keep_mask, grad_patches, *got_grad, grad_specials, h, a2, a2t, fc1_weight, row(fc1_bias),
        fc2_weight, row(fc2_bias), row(ln2_gain),
    )
    out_chunks, (dh, dy, w2s, w2k, w1s, w1k, db1, small2) = outs[:4], outs[4:]
    out_rows, out_specials = settle(send_back(out_chunks, groups), at, groups, part, ns)

    dqkv, cs, ck, ds_, dk_, flat = pl.pallas_call(
        partial(heads_kernel, heads=heads),
        grid=(n,),
        in_specs=[
            per_image(padded, width), per_image(heads, padded, padded), per_image(padded, 3 * width),
            per_image(width, padded), per_image(width, padded), whole(proj_weight.shape),
        ],
        out_specs=[
            per_image(padded, 3 * width), *[whole((half, 2 * width))] * 4, whole((1, 3 * width)),
        ],
        out_shape=[
            struct(n, padded, 3 * width), *[struct(half, 2 * width)] * 4,
            struct(1, 3 * width, dtype=F32),
        ],
        scratch_shapes=[pltpu.VMEM((width, 3 * width), F32), pltpu.VMEM((width, width), F32)],
        compiler_params=params(),
        cost_estimate=cost(2 * total * width * 6 * width, 20e6),
        name="attention_backward",
    )(dy, prob, qkv, a1t, ot, proj_weight)

    outs = pl.pallas_call(
        partial(input_kernel, part=part, ns=ns),
        grid=(n,),
        in_specs=[
            per_image(padded, 3 * width), whole(qkv_weight.shape), per_image(padded, width),
            per_image(padded, width), whole((1, width)),
        ],
        out_specs=[*[per_image(part + ns, width)] * 4, whole((2, width))],
        out_shape=[*[struct(n, part + ns, width)] * 4, struct(2, width, dtype=F32)],
        scratch_shapes=[pltpu.VMEM((padded, width), F32)],
        compiler_params=params(),
        cost_estimate=cost(2 * total * width * 3 * width, 10e6),
        name="input_backward",
    )(dqkv, qkv_weight, xs, dh, row(ln1_gain))
    dx_rows, dx_specials = settle(send_back(outs[:4], groups), at, groups, part, ns)
    small1 = outs[4]

    def swap(v, bit):
        return lax.ppermute(v, "dp", [(s, s ^ bit) for s in range(replicas)])

    ring = ([(0, 1), (1, 0), (2, 3), (3, 2)], [(0, 3), (3, 0), (1, 2), (2, 1)])

    def total_of(sent, kept, x_first):
        v = kept + swap(sent, 1)
        v = v.reshape(2, 2, -1, v.shape[1])
        if x_first:
            v = v[:, 0] + swap(v[:, 1], 2)
            v = v[0] + swap(v[1], 4)
        else:
            v = v[0] + swap(v[1], 4)
            v = v[0] + swap(v[1], 2)
        for way in ring if x_first else ring[::-1]:
            v = v + lax.ppermute(v, "seq", way)
        return v.astype(F32)

    def natural(sent, kept):
        v = jnp.stack([kept, sent]).reshape(2, OWNERS // 2, -1, kept.shape[1])
        v = v.transpose(1, 0, 2, 3).reshape(-1, kept.shape[1])
        v = lax.psum_scatter(v, "dp", scatter_dimension=0, tiled=True)
        return lax.psum(v, "seq").astype(F32)

    def reduce(sent, kept, x_first):
        return total_of(sent, kept, x_first) if direct else natural(sent, kept)

    d_fc1 = reduce(w1s, w1k, True)
    d_fc2 = reduce(w2s, w2k, False)
    d_qk = reduce(cs, ck, True)
    d_vp = reduce(ds_, dk_, False)
    d_qkv = jnp.concatenate([d_qk, d_vp[:, :width]], axis=1)
    d_proj = d_vp[:, width:]

    flat = flat.reshape(3, width)
    vectors = jnp.concatenate([small1, flat[0:1], flat[2:3], small2, db1.reshape(-1, width)], axis=0)
    vectors = lax.psum(vectors, ("dp", "seq"))
    mine = lax.axis_index("dp")
    wide = vectors[8:].reshape(-1)

    def shard(v):
        size = v.shape[-1] // replicas
        return lax.dynamic_slice_in_dim(v, mine * size, size, axis=v.ndim - 1)

    s = shard(vectors[:8])
    return (
        out_rows, out_specials, dx_rows, dx_specials,
        s[0], s[1], d_qkv, s[2:4], d_proj, s[7], s[4], s[5], d_fc1, shard(wide), d_fc2, s[6],
    )


def solution(mesh):
    rows = P("dp", "seq", None)
    lead = P("dp", None, None)
    flat = P("dp")
    matrix = P("dp", None)
    return jax.shard_map(
        shards,
        mesh=mesh,
        in_specs=(rows, lead, matrix, *[P()] * 12, rows, lead),
        out_specs=(
            rows, lead, rows, lead, flat, flat, matrix, P(None, "dp"), matrix, flat, flat, flat,
            matrix, flat, matrix, flat,
        ),
        check_vma=False,
    )
```

```python
from functools import partial

import jax
import jax.numpy as jnp
from jax import lax
from jax.experimental import pallas as pl
from jax.experimental.pallas import tpu as pltpu
from jax.sharding import PartitionSpec as P

HEAD_DIM = 64
KEEP = 1.0 / 0.9
EPS = 1e-06
BF = jnp.bfloat16
F32 = jnp.float32
COLUMNS = 128
PACE = 0.3
OWNERS = 8
VMEM = 60 * 2**20

ERF_P = 0.425
ERF_C = (
    0.2396707695899643,
    0.2419609266760862,
    0.1999560009093125,
    0.2575598334337707,
    -0.1079240365384954,
    0.4126939875393689,
    -0.3161029975019298,
    0.07218539595215835,
)


def dot(a, b):
    return lax.dot_general(a, b, (((1,), (0,)), ((), ())), preferred_element_type=F32)


def dot_nt(a, b):
    return lax.dot_general(a, b, (((1,), (1,)), ((), ())), preferred_element_type=F32)


def dot_tn(a, b):
    return lax.dot_general(a, b, (((0,), (0,)), ((), ())), preferred_element_type=F32)


def gelu_both(u):
    t = 1.0 / (1.0 + (ERF_P * 0.5**0.5) * jnp.abs(u))
    poly = jnp.full_like(t, 0.5 * ERF_C[-1])
    for c in ERF_C[-2::-1]:
        poly = poly * t + 0.5 * c
    bell = jnp.exp(-0.5 * u * u)
    tail = poly * t * bell
    cdf = jnp.where(u >= 0, 1.0 - tail, tail)
    return u * cdf, cdf + u * (bell * 0.3989422804014327)


def normalize(x):
    center = x - jnp.mean(x, axis=-1, keepdims=True)
    inv = lax.rsqrt(jnp.mean(center * center, axis=-1, keepdims=True) + EPS)
    return center * inv, inv


def norm_back(up, hat, inv, gain):
    e = up * gain
    return inv * (
        e
        - jnp.mean(e, axis=-1, keepdims=True)
        - hat * jnp.mean(e * hat, axis=-1, keepdims=True)
    )


def both_heads(v, low):
    return jnp.concatenate([jnp.where(low, v, BF(0)), jnp.where(low, BF(0), v)], axis=0)


def colsum(v):
    return jnp.sum(v, axis=0, keepdims=True)


def place(b):
    return (b & 1) * (OWNERS // 2) + lax.shift_right_logical(b, 1)


def store_relative(ref, lead, value, d):
    n = value.shape[0] // OWNERS
    for b in range(OWNERS):
        spot = pl.multiple_of(place(b ^ d) * n, n)
        ref[lead, pl.ds(spot, n), :] = value[b * n : (b + 1) * n]


def forward_kernel(
    at, keep, x0, x1, x2, x3, sp, g1, b1, wq, bq, wp, bp, g2, b2,
    *refs, rows, heads, lo, images,
):
    xs, a1t, qkv, prob, ot, h, a2, a2t, buf = refs[-9:]
    i = lo + pl.program_id(0)
    d = at[1]
    part = x0.shape[1]
    ns = sp.shape[1]
    width = x0.shape[2]
    buf[...] = jnp.zeros_like(buf)
    buf[0:ns, :] = sp[0].astype(F32)
    for k, ref in enumerate((x0, x1, x2, x3)):
        buf[ns + k * part : ns + (k + 1) * part, :] = ref[0].astype(F32)
    x = buf[...]
    xs[0] = x.astype(BF)
    hat, _ = normalize(x)
    a1 = (hat * g1[...].astype(F32) + b1[...].astype(F32)).astype(BF)
    store_relative(a1t, 0, a1.astype(F32).T.astype(BF), d)
    both = (dot(a1, wq[...]) + bq[...]).astype(BF)
    qkv[0] = both
    padded = x.shape[0]
    low = lax.broadcasted_iota(jnp.int32, (padded, 2 * HEAD_DIM), 1) < HEAD_DIM
    seen = lax.broadcasted_iota(jnp.int32, (2 * padded, padded), 1) < rows
    outs = []
    for j in range(heads // 2):
        c = j * 2 * HEAD_DIM
        q = both[:, c : c + 2 * HEAD_DIM] * BF(HEAD_DIM**-0.5)
        k = both[:, width + c : width + c + 2 * HEAD_DIM]
        v = both[:, 2 * width + c : 2 * width + c + 2 * HEAD_DIM]
        s = jnp.where(seen, dot_nt(both_heads(q, low), k), -1e30)
        e = jnp.exp(s - jnp.max(s, axis=-1, keepdims=True))
        p = (e * (1.0 / jnp.sum(e, axis=-1, keepdims=True))).astype(BF)
        prob[0, j] = p
        pv = dot(p, v)
        outs.append(jnp.where(low, pv[:padded], pv[padded:]))
    o32 = jnp.concatenate(outs, axis=1)
    store_relative(ot, 0, o32.T.astype(BF), d)
    y = dot(o32.astype(BF), wp[...]) + bp[...].astype(F32)
    m1 = keep[at[0] * images + i, 0].astype(F32) * KEEP
    hh = x + m1 * y
    h[0] = hh
    hat2, _ = normalize(hh)
    n2 = hat2 * g2[...].astype(F32) + b2[...].astype(F32)
    a2[0] = n2.astype(BF)
    store_relative(a2t, 0, n2.T.astype(BF), d)


def feed_kernel(
    at, keep, h, a2, w1, b1, w2, b2, act, slope, o0, o1, o2, o3, z, *, images, part, ns
):
    t = pl.program_id(0)
    padded = h.shape[1]
    wa = w1[...]
    wb = w2[...]
    bias = b1[...].astype(F32)
    for i in range(images):
        r = slice(i * padded, (i + 1) * padded)
        g, dg = gelu_both(dot(a2[i], wa) + bias)
        g = g.astype(BF)
        act[i] = g
        slope[i] = dg.astype(BF)
        more = dot(g, wb)

        @pl.when(t == 0)
        def _(r=r, more=more):
            z[r, :] = more

        @pl.when(t > 0)
        def _(r=r, more=more):
            z[r, :] += more

    @pl.when(t == pl.num_programs(0) - 1)
    def _():
        for i in range(images):
            m2 = keep[at[0] * images + i, 1].astype(F32) * KEEP
            r = slice(i * padded, (i + 1) * padded)
            z[r, :] = h[i] + m2 * (z[r, :] + b2[...].astype(F32))
            for k, ref in enumerate((o0, o1, o2, o3)):
                lo = i * padded + ns + k * part
                ref[i] = jnp.concatenate(
                    [z[lo : lo + part, :], z[i * padded : i * padded + ns, :]], axis=0
                ).astype(BF)


def feed_back_kernel(
    at, keep, g0, g1, g2, g3, sg, h, a2t, act, slope, w1, w2, gain,
    dh, dy, w2s, w2k, w1s, w1k, db1, small,
    dout, dz, da2, *, images,
):
    t = pl.program_id(0)
    part = g0.shape[1]
    ns = sg.shape[1]
    padded = h.shape[1]

    @pl.when(t == 0)
    def _():
        for i in range(images):
            m2 = keep[at[0] * images + i, 1].astype(F32) * KEEP
            r = i * padded
            dout[r : r + padded, :] = jnp.zeros((padded, dout.shape[1]), F32)
            dout[r : r + ns, :] = sg[i].astype(F32)
            for k, ref in enumerate((g0, g1, g2, g3)):
                lo = r + ns + k * part
                dout[lo : lo + part, :] = ref[i].astype(F32)
            dz[r : r + padded, :] = (dout[r : r + padded, :] * m2).astype(BF)
        da2[...] = jnp.zeros_like(da2)

    wa = w1[...]
    wb = w2[...]
    grad1 = None
    db = None
    for i in range(images):
        r = slice(i * padded, (i + 1) * padded)
        du = (slope[i].astype(F32) * dot_nt(dz[r, :], wb)).astype(BF)
        da2[r, :] += dot_nt(du, wa)
        g = dot(a2t[i], du)
        s = colsum(du.astype(F32))
        grad1 = g if grad1 is None else grad1 + g
        db = s if db is None else db + s
    db1[...] = db
    n = w1k.shape[2]
    for p in range(w1k.shape[0]):
        w1k[p, 0] = grad1[p * n : (p + 1) * n].astype(BF)
        w1s[p, 0] = grad1[grad1.shape[0] // 2 + p * n :][:n].astype(BF)
    grad2 = dot_tn(act[...].reshape(images * padded, -1), dz[...]).astype(BF)
    half = grad2.shape[0] // 2
    odd = at[1] & 1

    @pl.when(odd == 0)
    def _():
        w2k[...] = grad2[:half]
        w2s[...] = grad2[half:]

    @pl.when(odd == 1)
    def _():
        w2k[...] = grad2[half:]
        w2s[...] = grad2[:half]

    @pl.when(t == pl.num_programs(0) - 1)
    def _():
        gains = gain[...].astype(F32)
        sums = [jnp.zeros((1, dout.shape[1]), F32) for _ in range(4)]
        for i in range(images):
            m1 = keep[at[0] * images + i, 0].astype(F32) * KEEP
            r = slice(i * padded, (i + 1) * padded)
            hat, inv = normalize(h[i])
            up = da2[r, :]
            grad = dout[r, :] + norm_back(up, hat, inv, gains)
            dh[i] = grad
            low = (m1 * grad).astype(BF)
            dy[i] = low
            for j, v in enumerate((up * hat, up, dz[r, :].astype(F32), low.astype(F32))):
                sums[j] = sums[j] + colsum(v)
        small[...] = jnp.concatenate(sums, axis=0)


def heads_kernel(dy, prob, qkv, wp, wq, xs, dh, gain, *refs, heads, part, ns):
    dqkv, o0, o1, o2, o3, flat, small, buf = refs[-8:]
    i = pl.program_id(0)
    width = dy.shape[2]
    padded = dy.shape[1]
    low = lax.broadcasted_iota(jnp.int32, (padded, 2 * HEAD_DIM), 1) < HEAD_DIM
    do = dot_nt(dy[0], wp[...]).astype(BF)
    for j in range(heads // 2):
        c = j * 2 * HEAD_DIM
        q = qkv[0, :, c : c + 2 * HEAD_DIM]
        k = qkv[0, :, width + c : width + c + 2 * HEAD_DIM]
        v = qkv[0, :, 2 * width + c : 2 * width + c + 2 * HEAD_DIM]
        g = both_heads(do[:, c : c + 2 * HEAD_DIM], low)
        p = prob[0, j]
        p32 = p.astype(F32)
        w = p32 * dot_nt(g, v)
        ds = (w - p32 * jnp.sum(w, axis=-1, keepdims=True)).astype(BF)
        dq = dot(ds, k)
        dq = jnp.where(low, dq[:padded], dq[padded:]) * HEAD_DIM**-0.5
        dk = dot_tn(ds, both_heads(q, low)) * HEAD_DIM**-0.5
        dqkv[0, :, c : c + 2 * HEAD_DIM] = dq.astype(BF)
        dqkv[0, :, width + c : width + c + 2 * HEAD_DIM] = dk.astype(BF)
        dqkv[0, :, 2 * width + c : 2 * width + c + 2 * HEAD_DIM] = dot_tn(p, g).astype(BF)
    grads = dqkv[0]
    tops = colsum(grads.astype(F32))
    up = dot_nt(grads, wq[...])
    hat, inv = normalize(xs[0].astype(F32))
    buf[...] = dh[0] + norm_back(up, hat, inv, gain[...].astype(F32))
    for k, ref in enumerate((o0, o1, o2, o3)):
        lo = ns + k * part
        ref[0] = jnp.concatenate([buf[lo : lo + part, :], buf[0:ns, :]], axis=0).astype(BF)
    sums = jnp.concatenate([colsum(up * hat), colsum(up)], axis=0)

    @pl.when(i == 0)
    def _():
        flat[...] = tops
        small[...] = sums

    @pl.when(i > 0)
    def _():
        flat[...] += tops
        small[...] += sums


def weights_kernel(
    at, dqkv, dy, a1k, a1s, ok, os_, flat_a, flat_b, small_a, small_b, small2, db1,
    cs, ck, ds_, dk_, cols,
):
    t = pl.program_id(0)
    images, _, width = dy.shape

    @pl.when(t == 0)
    def _():
        n = width // OWNERS
        per = db1.shape[1] // width
        flat = flat_a[...] + flat_b[...]
        eight = jnp.concatenate(
            [small_a[...] + small_b[...], flat[:, :width], flat[:, 2 * width :], small2[...]], axis=0
        ).T
        long = jnp.broadcast_to(db1[...], (8, db1.shape[1])).T
        cols[...] = jnp.zeros_like(cols)
        for b in range(OWNERS):
            rows = pl.ds(pl.multiple_of(place(b ^ at[1]) * n, n), n)
            cols[rows, 0:8] = eight[b * n : (b + 1) * n]
            for j in range(per):
                lo = (b * per + j) * n
                cols[rows, 8 + j : 9 + j] = long[lo : lo + n, 0:1]

    block = cs.shape[0]
    for side, (a1, o, c_ref, d_ref) in enumerate(((a1s, os_, cs, ds_), (a1k, ok, ck, dk_))):
        g = dot(a1[0], dqkv[0])
        p = dot(o[0], dy[0])
        for i in range(1, images):
            g = g + dot(a1[i], dqkv[i])
            p = p + dot(o[i], dy[i])
        c_ref[:, : 2 * width] = g[:, : 2 * width].astype(BF)
        c_ref[:, 2 * width :] = jnp.zeros((block, COLUMNS), BF)
        d_ref[:, :width] = g[:, 2 * width :].astype(BF)
        d_ref[:, width : 2 * width] = p.astype(BF)
        lo = pl.multiple_of((1 - side) * (width // 2) + t * block, block)
        d_ref[:, 2 * width :] = cols[pl.ds(lo, block), :].astype(BF)


def gather_kernel(at, c0, c1, c2, c3, rows, specials):
    k = pl.program_id(0)
    part = rows.shape[1]
    for j, ref in enumerate((c0, c1, c2, c3)):

        @pl.when(k == j)
        def _(ref=ref):
            rows[...] = ref[:, :part, :]
            specials[...] = ref[:, part:, :]


def sum_kernel(*refs, terms, pick):
    if pick:
        at, *refs = refs
        even = (at[0] & 1) == 0
    ins, outs = refs[: sum(terms)], refs[sum(terms) :]
    values = []
    for count in terms:
        mine, ins = ins[:count], ins[count:]
        total = mine[0][...].astype(F32)
        for ref in mine[1:]:
            total = total + ref[...].astype(F32)
        values.append(total)
    if pick:
        values = [jnp.where(even, *values), jnp.where(even, *values[::-1])]
    for ref, v in zip(outs, values):
        ref[...] = v.astype(BF)


def sums(jobs, at=None):
    specs, arrays, out_specs, out_shapes = [], [], [], []
    for job in jobs:
        for v, lead in job:
            tail = v.shape[len(lead) + 1 :]
            block = tuple(v.shape[i] if j is None else None for i, j in enumerate(lead))
            place_ = tuple(j or 0 for j in lead)
            specs.append(
                pl.BlockSpec((*block, None, *tail), lambda m, p=place_: (*p, m, 0, 0))
            )
            arrays.append(v)
        keep = tuple(b for b in block if b is not None)
        out_shapes.append(struct(*keep, v.shape[len(lead)], *tail))
        out_specs.append(
            pl.BlockSpec((*keep, None, *tail), lambda m, z=len(keep): (*(0,) * z, m, 0, 0))
        )
    if at is not None:
        specs.insert(0, pl.BlockSpec(memory_space=pltpu.SMEM))
        arrays.insert(0, at)
    return pl.pallas_call(
        partial(sum_kernel, terms=[len(job) for job in jobs], pick=at is not None),
        grid=(out_shapes[0].shape[-3],),
        in_specs=specs,
        out_specs=out_specs,
        out_shape=out_shapes,
        compiler_params=params(24),
        cost_estimate=cost(2),
        name="sums",
    )(*arrays)


def finish_feed_kernel(at, mine, other, fc1, fc2):
    even = (at[0] & 1) == 0
    n = fc1.shape[0]
    width = fc2.shape[1]
    for m in range(mine.shape[0]):
        p, q = mine[m].astype(F32), other[m].astype(F32)
        fc1[:, m * width : (m + 1) * width] = jnp.where(even, p, q)
        fc2[m * n : (m + 1) * n, :] = jnp.where(even, q, p)


def finish_kernel(at, mine, other, qkv, proj, *rest):
    vectors, long = rest[:-1], rest[-1]
    width = proj.shape[1]
    even = (at[0] & 1) == 0
    p, q = mine[...].astype(F32), other[...].astype(F32)
    c, d = jnp.where(even, p, q), jnp.where(even, q, p)
    qkv[:, : 2 * width] = c[:, : 2 * width]
    qkv[:, 2 * width :] = d[:, :width]
    proj[...] = d[:, width : 2 * width]
    n = c.shape[0]
    flat = d[:, 2 * width :].T
    row = 0
    for ref in vectors:
        ref[...] = flat[row : row + ref.shape[0]]
        row += ref.shape[0]
    for j in range(long.shape[1] // n):
        long[:, j * n : (j + 1) * n] = flat[row + j : row + j + 1]


def whole(shape):
    return pl.BlockSpec(shape, lambda *_: (0,) * len(shape))


def params(mib=60):
    return pltpu.CompilerParams(
        dimension_semantics=("arbitrary",), vmem_limit_bytes=mib * 2**20
    )


def cost(us):
    return pl.CostEstimate(flops=int(us * 1e9 * PACE), bytes_accessed=1, transcendentals=0)


ANY = pl.BlockSpec(memory_space=pl.ANY)


def struct(*shape, dtype=BF):
    return jax.ShapeDtypeStruct(shape, dtype)


def after(v, *others):
    return lax.optimization_barrier((v, *others))[0]


def together(*vs):
    return lax.optimization_barrier(vs)


def swap(v, bit):
    return lax.ppermute(v, "dp", [(s, s ^ bit) for s in range(lax.axis_size("dp"))])


def send_around(x, groups, lo, count):
    me = lax.axis_index("seq")
    n = x.shape[0] // groups
    got = []
    for k in range(1, groups):
        block = lax.dynamic_slice_in_dim(x, n * ((me + k) % groups) + lo, count)
        got.append(lax.ppermute(block, "seq", [(s, (s + k) % groups) for s in range(groups)]))
    return got


def send_back(chunks, groups):
    return [chunks[0]] + [
        lax.ppermute(c, "seq", [(s, (s - k) % groups) for s in range(groups)])
        for k, c in enumerate(chunks)
        if k
    ]


def settle(chunks, at, groups, part, ns):
    n, _, width = chunks[0].shape
    return pl.pallas_call(
        gather_kernel,
        grid_spec=pltpu.PrefetchScalarGridSpec(
            num_scalar_prefetch=1,
            grid=(groups,),
            in_specs=[whole(c.shape) for c in chunks],
            out_specs=[
                pl.BlockSpec((n, part, width), lambda k, at: ((at[0] + k) % groups, 0, 0)),
                pl.BlockSpec((n, ns, width), lambda k, at: ((at[0] + k) % groups, 0, 0)),
            ],
        ),
        out_shape=[struct(n * groups, part, width), struct(n * groups, ns, width)],
        compiler_params=params(16),
        cost_estimate=cost(2),
        name="settle",
    )(at, *chunks)


def shards(
    patches, specials, keep_mask, ln1_gain, ln1_bias, qkv_weight, qv_bias, proj_weight, proj_bias,
    ln2_gain, ln2_bias, fc1_weight, fc1_bias, fc2_weight, fc2_bias, grad_patches, grad_specials,
):
    images, part, width = patches.shape
    ns = specials.shape[1]
    groups = lax.axis_size("seq")
    replicas = lax.axis_size("dp")
    hidden = fc1_weight.shape[1]
    heads = width // HEAD_DIM
    n = images // groups
    rows = ns + groups * part
    padded = -(-rows // 16) * 16
    steps = OWNERS // 2
    chunk = hidden // steps
    half = width // 2
    direct = replicas == OWNERS
    me = lax.axis_index("seq")
    d = lax.axis_index("dp") if direct else jnp.int32(0)
    at = jnp.stack([me, d]).astype(jnp.int32)

    def row(v):
        return v.reshape(1, -1)

    def per_image(lo, *shape):
        return pl.BlockSpec((1, *shape), lambda i, *_: (lo + i,) + (0,) * len(shape))

    got = together(*send_around(patches, groups, 0, n))
    zero = jnp.zeros((width,), F32)
    qkv_bias = row(jnp.concatenate([qv_bias[0].astype(F32), zero, qv_bias[1].astype(F32)]))

    shapes = [
        ((padded, width), BF), ((width, padded), BF), ((padded, 3 * width), BF),
        ((heads // 2, 2 * padded, padded), BF), ((width, padded), BF),
        ((padded, width), F32), ((padded, width), BF), ((width, padded), BF),
    ]

    def forward(got, lo, count, before=()):
        own = pl.BlockSpec((1, part, width), lambda i, at, keep: (at[0] * n + lo + i, 0, 0))
        ins = 15
        return pl.pallas_call(
            partial(forward_kernel, rows=rows, heads=heads, lo=lo, images=n),
            grid_spec=pltpu.PrefetchScalarGridSpec(
                num_scalar_prefetch=2,
                grid=(count,),
                in_specs=[
                    own, *[per_image(0, part, width)] * 3,
                    pl.BlockSpec((1, ns, width), lambda i, at, keep: (at[0] * n + lo + i, 0, 0)),
                    whole((1, width)), whole((1, width)),
                    whole(qkv_weight.shape), whole((1, 3 * width)),
                    whole(proj_weight.shape), *[whole((1, width))] * 3,
                    *[ANY] * len(before),
                ],
                out_specs=[per_image(lo, *shape) for shape, _ in shapes],
                scratch_shapes=[pltpu.VMEM((padded, width), F32)],
            ),
            out_shape=[struct(n, *shape, dtype=dtype) for shape, dtype in shapes],
            input_output_aliases={ins + j: j for j in range(len(before))},
            compiler_params=params(60),
            cost_estimate=cost(5 * count),
            name="attention_forward",
        )(
            at, keep_mask, patches, *got, specials, row(ln1_gain), row(ln1_bias), qkv_weight, qkv_bias,
            proj_weight, row(proj_bias), row(ln2_gain), row(ln2_bias), *before,
        )

    got_grad = send_around(after(grad_patches, *got), groups, 0, n)
    xs, a1t, qkv, prob, ot, h, a2, a2t = forward(got, 0, n)

    total = n * padded
    act, slope, *out_chunks = pl.pallas_call(
        partial(feed_kernel, images=n, part=part, ns=ns),
        grid_spec=pltpu.PrefetchScalarGridSpec(
            num_scalar_prefetch=2,
            grid=(steps,),
            in_specs=[
                whole(h.shape), whole(a2.shape),
                pl.BlockSpec((width, chunk), lambda t, *_: (0, t)),
                pl.BlockSpec((1, chunk), lambda t, *_: (0, t)),
                pl.BlockSpec((chunk, width), lambda t, *_: (t, 0)),
                whole((1, width)),
            ],
            out_specs=[
                *[pl.BlockSpec((n, padded, chunk), lambda t, *_: (0, 0, t))] * 2,
                *[whole((n, part + ns, width))] * 4,
            ],
            scratch_shapes=[pltpu.VMEM((total, width), F32)],
        ),
        out_shape=[*[struct(n, padded, hidden)] * 2, *[struct(n, part + ns, width)] * 4],
        compiler_params=params(60),
        cost_estimate=cost(20),
        name="feed_forward",
    )(
        at, keep_mask, h, a2, fc1_weight, row(fc1_bias), fc2_weight, row(fc2_bias)
    )
    act, slope, *got_grad = together(act, slope, *got_grad)
    back_out = send_back(out_chunks, groups)

    def owner(t, at):
        return t ^ lax.shift_right_logical(at[1], 1)

    dh, dy, w2s, w2k, w1s, w1k, db1, small2 = pl.pallas_call(
        partial(feed_back_kernel, images=n),
        grid_spec=pltpu.PrefetchScalarGridSpec(
            num_scalar_prefetch=2,
            grid=(steps,),
            in_specs=[
                pl.BlockSpec((n, part, width), lambda t, at, keep: (at[0], 0, 0)),
                *[whole((n, part, width))] * 3,
                pl.BlockSpec((n, ns, width), lambda t, at, keep: (at[0], 0, 0)),
                whole(h.shape), whole(a2t.shape),
                *[pl.BlockSpec((n, padded, chunk), lambda t, at, keep: (0, 0, owner(t, at)))] * 2,
                pl.BlockSpec((width, chunk), lambda t, at, keep: (0, owner(t, at))),
                pl.BlockSpec((chunk, width), lambda t, at, keep: (owner(t, at), 0)),
                whole((1, width)),
            ],
            out_specs=[
                whole((n, padded, width)), whole((n, padded, width)),
                *[pl.BlockSpec((chunk // 2, width), lambda t, *_: (t, 0))] * 2,
                *[pl.BlockSpec((steps, 1, width // OWNERS, chunk), lambda t, at, keep: (0, owner(t, at), 0, 0))] * 2,
                pl.BlockSpec((1, chunk), lambda t, at, keep: (0, owner(t, at))),
                whole((4, width)),
            ],
            scratch_shapes=[
                pltpu.VMEM((total, width), F32), pltpu.VMEM((total, width), BF),
                pltpu.VMEM((total, width), F32),
            ],
        ),
        out_shape=[
            struct(n, padded, width, dtype=F32), struct(n, padded, width),
            *[struct(hidden // 2, width)] * 2, *[struct(steps, steps, width // OWNERS, chunk)] * 2,
            struct(1, hidden, dtype=F32), struct(4, width, dtype=F32),
        ],
        compiler_params=params(60),
        cost_estimate=cost(25),
        name="feed_backward",
    )(
        at, keep_mask, grad_patches, *got_grad, grad_specials, h, a2t, act, slope, fc1_weight,
        fc2_weight, row(ln2_gain),
    )

    dy, w1s, w2s, *back_out = together(dy, w1s, w2s, *back_out)

    def backward(dy, lo, count, before=()):
        ins = 8
        return pl.pallas_call(
            partial(heads_kernel, heads=heads, part=part, ns=ns),
            grid=(count,),
            in_specs=[
                per_image(lo, padded, width), per_image(lo, heads // 2, 2 * padded, padded),
                per_image(lo, padded, 3 * width), whole(proj_weight.shape), whole(qkv_weight.shape),
                per_image(lo, padded, width), per_image(lo, padded, width), whole((1, width)),
                *[ANY] * len(before),
            ],
            out_specs=[
                per_image(lo, padded, 3 * width), *[per_image(lo, part + ns, width)] * 4,
                whole((1, 3 * width)), whole((2, width)),
            ],
            out_shape=[
                struct(n, padded, 3 * width), *[struct(n, part + ns, width)] * 4,
                struct(1, 3 * width, dtype=F32), struct(2, width, dtype=F32),
            ],
            scratch_shapes=[pltpu.VMEM((padded, width), F32)],
            input_output_aliases={ins + j: j for j in range(len(before))},
            compiler_params=params(60),
            cost_estimate=cost(7 * count),
            name="attention_backward",
        )(dy, prob, qkv, proj_weight, qkv_weight, xs, dh, row(ln1_gain), *before)

    n1 = width // OWNERS
    x_half, y_half = (None, 1), (1, None)
    if direct:
        ra, rb = swap(w1s, 1), swap(w2s, 1)
    *made, flat_a, small_a = backward(dy, 0, 1)
    if direct:
        ra, rb, dy, *made = together(ra, rb, dy, *made)
        wa, wb, ra, rb = (v.reshape(2, 2, steps, n1, chunk) for v in (w1k, w2k, ra, rb))
        as_, bs = sums([[(wa, x_half), (ra, x_half)], [(wb, y_half), (rb, y_half)]])
        dy, as_, bs = together(dy, as_, bs)
        qa, qb = swap(as_, 2), swap(bs, 4)
    dqkv, *back_dx, flat_b, small_b = backward(dy, 1, n - 1, made)
    back_dx = send_back(back_dx, groups)

    rows_k = pl.BlockSpec((n, half // 2, padded), lambda t, at: (0, t, 0))
    rows_s = pl.BlockSpec((n, half // 2, padded), lambda t, at: (0, 2 + t, 0))
    wide = 2 * width + COLUMNS
    cs, ck, ds_, dk_ = pl.pallas_call(
        weights_kernel,
        grid_spec=pltpu.PrefetchScalarGridSpec(
            num_scalar_prefetch=1,
            grid=(2,),
            in_specs=[
                whole(dqkv.shape), whole(dy.shape), rows_k, rows_s, rows_k, rows_s,
                *[whole((1, 3 * width))] * 2, *[whole((2, width))] * 2, whole((4, width)),
                whole((1, hidden)),
            ],
            out_specs=[pl.BlockSpec((half // 2, wide), lambda t, at: (t, 0))] * 4,
            scratch_shapes=[pltpu.VMEM((width, COLUMNS), F32)],
        ),
        out_shape=[struct(half, wide)] * 4,
        compiler_params=params(60),
        cost_estimate=cost(6),
        name="attention_weights",
    )(at, dqkv, dy, a1t, a1t, ot, ot, flat_a, flat_b, small_a, small_b, small2, db1)

    if not direct:
        out_rows, out_specials = settle(back_out, at, groups, part, ns)
        dx_rows, dx_specials = settle(back_dx, at, groups, part, ns)
        return (
            out_rows, out_specials, dx_rows, dx_specials,
            *natural_sums(
                w1s, w1k, w2s, w2k, cs, ck, ds_, dk_, flat_a + flat_b, small_a + small_b, small2, db1
            ),
        )

    def near(v):
        return lax.ppermute(v, "seq", [(s, s ^ 1) for s in range(groups)])

    def far(v):
        return lax.ppermute(v, "seq", [(s, s ^ 2) for s in range(groups)])

    qa, qb, cs, ds_ = together(qa, qb, cs, ds_)
    as_, bs = sums(
        [[(wa, (1, 0)), (ra, (1, 0)), (qa, (1,))], [(wb, (0, 1)), (rb, (0, 1)), (qb, (1,))]]
    )
    as_, bs, cs, ds_, back_dx[1], back_dx[3] = together(as_, bs, cs, ds_, back_dx[1], back_dx[3])
    ta, tb = swap(as_, 4), swap(bs, 2)
    rc, rd = swap(cs, 1), swap(ds_, 1)
    rc, rd, ck, dk_ = together(rc, rd, ck, dk_)
    wc, wd, rc, rd = (v.reshape(2, 2, 2, n1 // 2, -1) for v in (ck, dk_, rc, rd))
    cs, ds_ = sums([[(wc, x_half), (rc, x_half)], [(wd, y_half), (rd, y_half)]])
    ta, tb, cs, ds_ = together(ta, tb, cs, ds_)
    qc, qd = swap(cs, 2), swap(ds_, 4)
    e1, es = sums(
        [
            [(wa, (0, 0)), (ra, (0, 0)), (qa, (0,)), (ta, ())],
            [(wb, (0, 0)), (rb, (0, 0)), (qb, (0,)), (tb, ())],
        ],
        at,
    )
    re = near(es)
    back_out = together(*back_out, e1)[:groups]
    out_rows, out_specials = settle(back_out, at, groups, part, ns)
    re, out_rows, *back_dx = together(re, out_rows, *back_dx)
    e1 = e1 + re
    e1, qc, qd = together(e1, qc, qd)
    re = far(e1)
    cs, ds_ = sums(
        [[(wc, (1, 0)), (rc, (1, 0)), (qc, (1,))], [(wd, (0, 1)), (rd, (0, 1)), (qd, (1,))]]
    )
    tc, td = swap(cs, 4), swap(ds_, 2)
    tc, td = together(tc, td)
    f1, fs = sums(
        [
            [(wc, (0, 0)), (rc, (0, 0)), (qc, (0,)), (tc, ())],
            [(wd, (0, 0)), (rd, (0, 0)), (qd, (0,)), (td, ())],
        ],
        at,
    )
    rf = near(fs)
    back_dx = together(*back_dx, f1)[:groups]
    dx_rows, dx_specials = settle(back_dx, at, groups, part, ns)
    rf, re, dx_rows = together(rf, re, dx_rows)
    f1 = f1 + rf
    rf = far(f1)
    e1 = e1 + re
    re = near(e1)
    re, f1 = together(re, f1)
    smem = pl.BlockSpec(memory_space=pltpu.SMEM)
    vmem = pl.BlockSpec(memory_space=pltpu.VMEM)
    d_fc1, d_fc2 = pl.pallas_call(
        finish_feed_kernel,
        in_specs=[smem, vmem, vmem],
        out_shape=[struct(n1, hidden, dtype=F32), struct(hidden // OWNERS, width, dtype=F32)],
        compiler_params=pltpu.CompilerParams(vmem_limit_bytes=24 * 2**20),
        cost_estimate=cost(2),
        name="finish_feed",
    )(at, e1, re)
    rf, d_fc1 = together(rf, d_fc1)
    f1 = f1 + rf
    rf = near(f1)
    done = pl.pallas_call(
        finish_kernel,
        in_specs=[smem, vmem, vmem],
        out_shape=[
            struct(n1, 3 * width, dtype=F32), struct(n1, width, dtype=F32),
            *[struct(1, n1, dtype=F32)] * 2, struct(2, n1, dtype=F32),
            *[struct(1, n1, dtype=F32)] * 4, struct(1, hidden // OWNERS, dtype=F32),
        ],
        compiler_params=pltpu.CompilerParams(vmem_limit_bytes=24 * 2**20),
        cost_estimate=cost(2),
        name="finish",
    )(at, f1.reshape(n1, -1), rf.reshape(n1, -1))
    d_qkv, d_proj, gain1, bias1, d_qv, gain2, bias2, d_fc2b, d_projb, d_fc1b = done

    def one(v):
        return v.reshape(-1)

    return (
        out_rows, out_specials, dx_rows, dx_specials,
        one(gain1), one(bias1), d_qkv, d_qv, d_proj, one(d_projb), one(gain2), one(bias2),
        d_fc1, one(d_fc1b), d_fc2, one(d_fc2b),
    )


def natural_sums(w1s, w1k, w2s, w2k, cs, ck, ds_, dk_, flat, small1, small2, db1):
    width = small1.shape[1]
    replicas = lax.axis_size("dp")

    def natural(sent, kept):
        if kept.ndim == 4:
            kept, sent = (v.transpose(0, 2, 1, 3).reshape(width // 2, -1) for v in (kept, sent))
        v = jnp.stack([kept, sent]).reshape(2, OWNERS // 2, -1, kept.shape[1])
        v = v.transpose(1, 0, 2, 3).reshape(-1, kept.shape[1])
        v = lax.psum_scatter(v, "dp", scatter_dimension=0, tiled=True)
        return lax.psum(v, "seq").astype(F32)

    d_fc1, d_fc2 = natural(w1s, w1k), natural(w2s, w2k)
    d_qk, d_vp = natural(cs, ck), natural(ds_, dk_)
    d_qkv = jnp.concatenate([d_qk[:, : 2 * width], d_vp[:, :width]], axis=1)
    d_proj = d_vp[:, width : 2 * width]
    flat = flat.reshape(3, width)
    vectors = jnp.concatenate([small1, flat[0:1], flat[2:3], small2, db1.reshape(-1, width)], axis=0)
    vectors = lax.psum(vectors, ("dp", "seq"))
    mine = lax.axis_index("dp")

    def shard(v):
        size = v.shape[-1] // replicas
        return lax.dynamic_slice_in_dim(v, mine * size, size, axis=v.ndim - 1)

    s = shard(vectors[:8])
    d_fc1b = shard(vectors[8:].reshape(-1))
    return s[0], s[1], d_qkv, s[2:4], d_proj, s[7], s[4], s[5], d_fc1, d_fc1b, d_fc2, s[6]


def solution(mesh):
    rows = P("dp", "seq", None)
    lead = P("dp", None, None)
    flat = P("dp")
    matrix = P("dp", None)
    return jax.shard_map(
        shards,
        mesh=mesh,
        in_specs=(rows, lead, matrix, *[P()] * 12, rows, lead),
        out_specs=(
            rows, lead, rows, lead, flat, flat, matrix, P(None, "dp"), matrix, flat, flat, flat,
            matrix, flat, matrix, flat,
        ),
        check_vma=False,
    )
```

```python
from functools import partial

import jax
import jax.numpy as jnp
from jax import lax
from jax.experimental import pallas as pl
from jax.experimental.pallas import tpu as pltpu
from jax.sharding import PartitionSpec as P

HEAD_DIM = 64
KEEP = 1.0 / 0.9
EPS = 1e-06
BF = jnp.bfloat16
F32 = jnp.float32
COLUMNS = 128
PACE = 0.3
OWNERS = 8
VMEM = 60 * 2**20

def dot(a, b):
    return lax.dot_general(a, b, (((1,), (0,)), ((), ())), preferred_element_type=F32)


def dot_nt(a, b):
    return lax.dot_general(a, b, (((1,), (1,)), ((), ())), preferred_element_type=F32)


def dot_tn(a, b):
    return lax.dot_general(a, b, (((0,), (0,)), ((), ())), preferred_element_type=F32)


def gelu_both(u):
    cdf = 0.5 + 0.5 * lax.erf(u * 0.5**0.5)
    return u * cdf, cdf + u * (jnp.exp(-0.5 * u * u) * 0.3989422804014327)


def normalize(x):
    center = x - jnp.mean(x, axis=-1, keepdims=True)
    inv = lax.rsqrt(jnp.mean(center * center, axis=-1, keepdims=True) + EPS)
    return center * inv, inv


def norm_back(up, hat, inv, gain):
    e = up * gain
    return inv * (
        e
        - jnp.mean(e, axis=-1, keepdims=True)
        - hat * jnp.mean(e * hat, axis=-1, keepdims=True)
    )


def both_heads(v, low):
    return jnp.concatenate([jnp.where(low, v, BF(0)), jnp.where(low, BF(0), v)], axis=0)


def colsum(v):
    return jnp.sum(v, axis=0, keepdims=True)


def place(b):
    return (b & 1) * (OWNERS // 2) + lax.shift_right_logical(b, 1)


def store_relative(ref, lead, value, d):
    n = value.shape[0] // OWNERS
    for b in range(OWNERS):
        spot = pl.multiple_of(place(b ^ d) * n, n)
        ref[lead, pl.ds(spot, n), :] = value[b * n : (b + 1) * n]


def forward_kernel(
    at, keep, x0, x1, x2, x3, sp, g1, b1, wq, bq, wp, bp, g2, b2,
    xs, a1t, qkv, prob, ot, h, a2, a2t, buf, *, rows, heads,
):
    i = pl.program_id(0)
    d = at[1]
    part = x0.shape[1]
    ns = sp.shape[1]
    width = x0.shape[2]
    buf[...] = jnp.zeros_like(buf)
    buf[0:ns, :] = sp[0].astype(F32)
    came = [ref[0].astype(F32) for ref in (x0, x1, x2, x3)]
    for s in range(len(came)):
        k = (at[0] - s) & 3
        near, far = (jnp.where((k & 1) == 0, came[j], came[j + 1]) for j in (0, 2))
        buf[ns + s * part : ns + (s + 1) * part, :] = jnp.where(k < 2, near, far)
    x = buf[...]
    xs[0] = x.astype(BF)
    hat, _ = normalize(x)
    a1 = (hat * g1[...].astype(F32) + b1[...].astype(F32)).astype(BF)
    store_relative(a1t, 0, a1.T, d)
    both = (dot(a1, wq[...]) + bq[...]).astype(BF)
    qkv[0] = both
    padded = x.shape[0]
    low = lax.broadcasted_iota(jnp.int32, (padded, 2 * HEAD_DIM), 1) < HEAD_DIM
    seen = lax.broadcasted_iota(jnp.int32, (2 * padded, padded), 1) < rows
    outs = []
    for j in range(heads // 2):
        c = j * 2 * HEAD_DIM
        q = both[:, c : c + 2 * HEAD_DIM] * BF(HEAD_DIM**-0.5)
        k = both[:, width + c : width + c + 2 * HEAD_DIM]
        v = both[:, 2 * width + c : 2 * width + c + 2 * HEAD_DIM]
        s = jnp.where(seen, dot_nt(both_heads(q, low), k), -1e30)
        e = jnp.exp(s - jnp.max(s, axis=-1, keepdims=True))
        p = (e * (1.0 / jnp.sum(e, axis=-1, keepdims=True))).astype(BF)
        prob[0, j] = p
        pv = dot(p, v)
        outs.append(jnp.where(low, pv[:padded], pv[padded:]))
    o32 = jnp.concatenate(outs, axis=1)
    o = o32.astype(BF)
    store_relative(ot, 0, o.T, d)
    y = dot(o, wp[...]) + bp[...].astype(F32)
    m1 = keep[at[0] * pl.num_programs(0) + i, 0].astype(F32) * KEEP
    hh = x + m1 * y
    h[0] = hh
    hat2, _ = normalize(hh)
    n2 = (hat2 * g2[...].astype(F32) + b2[...].astype(F32)).astype(BF)
    a2[0] = n2
    store_relative(a2t, 0, n2.T, d)


def feed_kernel(
    at, keep, g0, g1, g2, g3, sg, h, a2, a2t, w1, b1, w2, b2, gain,
    out, dh, dy, w2s, w2k, w1s, w1k, db1, small,
    dout, dz, z, da2, acts, dus, across, *, images,
):
    t = pl.program_id(0)
    part = g0.shape[1]
    ns = sg.shape[1]
    padded = h.shape[1]

    @pl.when(t == 0)
    def _():
        for i in range(images):
            m2 = keep[at[0] * images + i, 1].astype(F32) * KEEP
            r = i * padded
            dout[r : r + padded, :] = jnp.zeros((padded, dout.shape[1]), F32)
            dout[r : r + ns, :] = sg[i].astype(F32)
            for k, ref in enumerate((g0, g1, g2, g3)):
                lo = r + ns + k * part
                dout[lo : lo + part, :] = ref[i].astype(F32)
            dz[r : r + padded, :] = (dout[r : r + padded, :] * m2).astype(BF)
            across[:, r : r + padded] = a2t[i]
        z[...] = jnp.zeros_like(z)
        da2[...] = jnp.zeros_like(da2)

    wa = w1[...]
    wb = w2[...]
    bias = b1[...].astype(F32)
    db = None
    for i in range(images):
        r = slice(i * padded, (i + 1) * padded)
        g, slope = gelu_both(dot(a2[i], wa) + bias)
        acts[r, :] = g.astype(BF)
        du = (slope * dot_nt(dz[r, :], wb)).astype(BF)
        dus[r, :] = du
        s = colsum(du.astype(F32))
        db = s if db is None else db + s
    db1[...] = db
    z[...] += dot(acts[...], wb)
    da2[...] += dot_nt(dus[...], wa)
    half = across.shape[0] // 2
    w1k[...] = dot(across[:half, :], dus[...]).astype(BF).reshape(w1k.shape)
    w1s[...] = dot(across[half:, :], dus[...]).astype(BF).reshape(w1s.shape)
    half = acts.shape[1] // 2
    for side, ref in enumerate((w2k, w2s)):
        lo = pl.multiple_of(((at[1] & 1) ^ side) * half, half)
        ref[...] = dot_tn(acts[:, pl.ds(lo, half)], dz[...]).astype(BF)

    @pl.when(t == pl.num_programs(0) - 1)
    def _():
        gains = gain[...].astype(F32)
        sums = [jnp.zeros((1, dout.shape[1]), F32) for _ in range(4)]
        for i in range(images):
            m1 = keep[at[0] * images + i, 0].astype(F32) * KEEP
            m2 = keep[at[0] * images + i, 1].astype(F32) * KEEP
            r = slice(i * padded, (i + 1) * padded)
            x = h[i]
            z[r, :] = x + m2 * (z[r, :] + b2[...].astype(F32))
            for k in range(out.shape[0] // images):
                lo = i * padded + ns + k * part
                out[k * images + i] = jnp.concatenate(
                    [z[lo : lo + part, :], z[i * padded : i * padded + ns, :]], axis=0
                ).astype(BF)
            hat, inv = normalize(x)
            up = da2[r, :]
            grad = dout[r, :] + norm_back(up, hat, inv, gains)
            dh[i] = grad
            low = (m1 * grad).astype(BF)
            dy[i] = low
            for j, v in enumerate((up * hat, up, dz[r, :].astype(F32), low.astype(F32))):
                sums[j] = sums[j] + colsum(v)
        small[...] = jnp.concatenate(sums, axis=0)


def heads_kernel(
    at, dy, prob, qkv, wp_any, wq_any, xs, dh, gain, a1t_any, ot_any, small2, db1,
    out, small, flat, cs, ck, ds_, dk_,
    buf, dqkv, dys, wp, wq, a1t, ot, a1, o, cols, sems, *, images, heads, part, ns,
):
    i = pl.program_id(0)
    width = dy.shape[2]
    padded = dy.shape[1]
    fetches = [
        pltpu.make_async_copy(src, dst, sems.at[j])
        for j, (src, dst) in enumerate(((wp_any, wp), (wq_any, wq), (a1t_any, a1t), (ot_any, ot)))
    ]

    @pl.when(i == 0)
    def _():
        for fetch in fetches:
            fetch.start()
        fetches[0].wait()

    @pl.when(i < images)
    def _():
        low = lax.broadcasted_iota(jnp.int32, (padded, 2 * HEAD_DIM), 1) < HEAD_DIM
        mine = pl.ds(pl.multiple_of(i * padded, padded), padded)
        dys[mine, :] = dy[0]
        do = dot_nt(dy[0], wp[...]).astype(BF)
        for j in range(heads // 2):
            c = j * 2 * HEAD_DIM
            q = qkv[0, :, c : c + 2 * HEAD_DIM]
            k = qkv[0, :, width + c : width + c + 2 * HEAD_DIM]
            v = qkv[0, :, 2 * width + c : 2 * width + c + 2 * HEAD_DIM]
            g = both_heads(do[:, c : c + 2 * HEAD_DIM], low)
            p = prob[0, j]
            p32 = p.astype(F32)
            w = p32 * dot_nt(g, v)
            ds = (w - p32 * jnp.sum(w, axis=-1, keepdims=True)).astype(BF)
            dq = dot(ds, k)
            dq = jnp.where(low, dq[:padded], dq[padded:]) * HEAD_DIM**-0.5
            dk = dot_tn(ds, both_heads(q, low)) * HEAD_DIM**-0.5
            dqkv[mine, c : c + 2 * HEAD_DIM] = dq.astype(BF)
            dqkv[mine, width + c : width + c + 2 * HEAD_DIM] = dk.astype(BF)
            dqkv[mine, 2 * width + c : 2 * width + c + 2 * HEAD_DIM] = dot_tn(p, g).astype(BF)

        @pl.when(i == 0)
        def _():
            fetches[1].wait()

        grads = dqkv[mine, :]
        tops = colsum(grads.astype(F32))
        up = dot_nt(grads, wq[...])
        hat, inv = normalize(xs[0].astype(F32))
        buf[...] = dh[0] + norm_back(up, hat, inv, gain[...].astype(F32))
        for k in range(out.shape[0] // images):
            lo = ns + k * part
            out[k * images + i] = jnp.concatenate(
                [buf[lo : lo + part, :], buf[0:ns, :]], axis=0
            ).astype(BF)
        sums = jnp.concatenate([colsum(up * hat), colsum(up)], axis=0)

        @pl.when(i == 0)
        def _():
            flat[...] = tops
            small[...] = sums

        @pl.when(i > 0)
        def _():
            flat[...] += tops
            small[...] += sums

    @pl.when(i == images)
    def _():
        n = width // OWNERS
        per = db1.shape[1] // width
        eight = jnp.concatenate(
            [small[...], flat[:, :width], flat[:, 2 * width :], small2[...]], axis=0
        ).T
        long = jnp.broadcast_to(db1[...], (8, db1.shape[1])).T
        cols[...] = jnp.zeros_like(cols)
        for b in range(OWNERS):
            rows = pl.ds(pl.multiple_of(place(b ^ at[1]) * n, n), n)
            cols[rows, 0:8] = eight[b * n : (b + 1) * n]
            for j in range(per):
                lo = (b * per + j) * n
                cols[rows, 8 + j : 9 + j] = long[lo : lo + n, 0:1]
        fetches[2].wait()
        fetches[3].wait()

    half = cs.shape[0]
    for step, lo, c_ref, d_ref in ((images, half, cs, ds_), (images + 1, 0, ck, dk_)):

        @pl.when(i == step)
        def _(lo=lo, c_ref=c_ref, d_ref=d_ref):
            for n in range(images):
                lanes = slice(n * padded, (n + 1) * padded)
                a1[:, lanes] = a1t[n, lo : lo + half, :]
                o[:, lanes] = ot[n, lo : lo + half, :]
            c_ref[:, : 2 * width] = dot(a1[...], dqkv[:, : 2 * width]).astype(BF)
            c_ref[:, 2 * width :] = jnp.zeros((half, COLUMNS), BF)
            d_ref[:, :width] = dot(a1[...], dqkv[:, 2 * width :]).astype(BF)
            d_ref[:, width : 2 * width] = dot(o[...], dys[...]).astype(BF)
            d_ref[:, 2 * width :] = cols[lo : lo + half, :].astype(BF)


def settle_kernel(both, rows, specials):
    part = rows.shape[1]
    rows[...] = both[:, :part, :]
    specials[...] = both[:, part:, :]


def sum_kernel(*refs, jobs, pick):
    if pick:
        at, *refs = refs
        even = (at[0] & 1) == 0
    terms = [lead for job in jobs for lead in job]
    count = len(terms)
    arrays, outs, bufs, sems = refs[:count], refs[count : -count - 1], refs[-count - 1 : -1], refs[-1]
    fetches = [
        pltpu.make_async_copy(array.at[lead], buf, sems.at[k])
        for k, (array, lead, buf) in enumerate(zip(arrays, terms, bufs))
    ]
    for fetch in fetches:
        fetch.start()
    for fetch in fetches:
        fetch.wait()
    values = []
    for job in jobs:
        total = None
        for ref in bufs[: len(job)]:
            v = ref[...].astype(F32)
            total = v if total is None else total + v
        bufs = bufs[len(job) :]
        values.append(total)
    if pick:
        values = [jnp.where(even, *values), jnp.where(even, *values[::-1])]
    pieces = len(outs) // len(values)
    for k, ref in enumerate(outs):
        v, n = values[k // pieces], ref.shape[0]
        lo = k % pieces * n if pieces > 1 else 0
        ref[...] = (v if pieces == 1 else v[lo : lo + n]).astype(BF).reshape(ref.shape)


def sums(jobs, at=None, mib=60, pieces=1):
    arrays, bufs, out_shapes, leads = [], [], [], []
    for job in jobs:
        leads.append([])
        for v, lead in job:
            index = tuple(slice(None) if j is None else j for j in lead)
            kept = tuple(v.shape[k] for k, j in enumerate(lead) if j is None) + v.shape[len(lead) :]
            leads[-1].append(index)
            arrays.append(v)
            bufs.append(pltpu.VMEM(kept, BF))
        out_shapes += [struct(kept[0] // pieces, *kept[1:])] * pieces
    specs = [ANY] * len(arrays)
    if at is not None:
        specs.insert(0, pl.BlockSpec(memory_space=pltpu.SMEM))
        arrays.insert(0, at)
    return pl.pallas_call(
        partial(sum_kernel, jobs=leads, pick=at is not None),
        in_specs=specs,
        out_shape=out_shapes,
        scratch_shapes=[*bufs, pltpu.SemaphoreType.DMA((len(bufs),))],
        compiler_params=pltpu.CompilerParams(vmem_limit_bytes=mib * 2**20),
        cost_estimate=cost(2),
        name="sums",
    )(*arrays)


def finish_feed_kernel(at, mine_a, other_a, mine_b, other_b, fc1, fc2):
    even = (at[0] & 1) == 0
    n = fc1.shape[0]
    width = fc2.shape[1]
    half = mine_a.shape[0]
    for m in range(2 * half):
        mine, other = (mine_a, other_a) if m < half else (mine_b, other_b)
        p, q = mine[m % half].astype(F32), other[m % half].astype(F32)
        fc1[:, m * width : (m + 1) * width] = jnp.where(even, p, q)
        fc2[m * n : (m + 1) * n, :] = jnp.where(even, q, p)


def finish_kernel(at, mine, other, qkv, proj, *rest):
    vectors, long = rest[:-1], rest[-1]
    width = proj.shape[1]
    even = (at[0] & 1) == 0
    p, q = mine[...].astype(F32), other[...].astype(F32)
    c, d = jnp.where(even, p, q), jnp.where(even, q, p)
    qkv[:, : 2 * width] = c[:, : 2 * width]
    qkv[:, 2 * width :] = d[:, :width]
    proj[...] = d[:, width : 2 * width]
    n = c.shape[0]
    flat = d[:, 2 * width :].T
    row = 0
    for ref in vectors:
        ref[...] = flat[row : row + ref.shape[0]]
        row += ref.shape[0]
    for j in range(long.shape[1] // n):
        long[:, j * n : (j + 1) * n] = flat[row + j : row + j + 1]


def whole(shape, mode=None):
    return pl.BlockSpec(shape, lambda *_: (0,) * len(shape), pipeline_mode=mode)


def params(mib=60):
    return pltpu.CompilerParams(
        dimension_semantics=("arbitrary",), vmem_limit_bytes=mib * 2**20
    )


def cost(us):
    return pl.CostEstimate(flops=int(us * 1e9 * PACE), bytes_accessed=1, transcendentals=0)


ANY = pl.BlockSpec(memory_space=pl.ANY)


def struct(*shape, dtype=BF):
    return jax.ShapeDtypeStruct(shape, dtype)


def after(v, *others):
    return lax.optimization_barrier((v, *others))[0]


def together(*vs):
    return lax.optimization_barrier(vs)


def swap(v, bit):
    return lax.ppermute(v, "dp", [(s, s ^ bit) for s in range(lax.axis_size("dp"))])


def exchange(x):
    return lax.all_to_all(x, "seq", split_axis=0, concat_axis=0, tiled=True)


def settle(both, ns):
    images, rows, width = both.shape
    n = images // 4
    return pl.pallas_call(
        settle_kernel,
        grid=(images // n,),
        in_specs=[pl.BlockSpec((n, rows, width), lambda i: (i, 0, 0))],
        out_specs=[
            pl.BlockSpec((n, rows - ns, width), lambda i: (i, 0, 0)),
            pl.BlockSpec((n, ns, width), lambda i: (i, 0, 0)),
        ],
        out_shape=[struct(images, rows - ns, width), struct(images, ns, width)],
        compiler_params=params(60),
        cost_estimate=cost(2),
        name="settle",
    )(both)


def shards(
    patches, specials, keep_mask, ln1_gain, ln1_bias, qkv_weight, qv_bias, proj_weight, proj_bias,
    ln2_gain, ln2_bias, fc1_weight, fc1_bias, fc2_weight, fc2_bias, grad_patches, grad_specials,
):
    images, part, width = patches.shape
    ns = specials.shape[1]
    groups = lax.axis_size("seq")
    replicas = lax.axis_size("dp")
    hidden = fc1_weight.shape[1]
    heads = width // HEAD_DIM
    n = images // groups
    rows = ns + groups * part
    padded = -(-rows // 16) * 16
    steps = OWNERS // 2
    chunk = hidden // steps
    half = width // 2
    direct = replicas == OWNERS
    me = lax.axis_index("seq")
    d = lax.axis_index("dp") if direct else jnp.int32(0)
    at = jnp.stack([me, d]).astype(jnp.int32)

    def per_image(lo, *shape):
        return pl.BlockSpec((1, *shape), lambda i, *_: (lo + i,) + (0,) * len(shape))

    moved = []
    for k in range(1, groups):
        block = lax.dynamic_slice_in_dim(patches, n * ((me + k) % groups), n)
        moved.append(lax.ppermute(block, "seq", [(s, (s + k) % groups) for s in range(groups)]))
    moved = together(*moved)
    grads = exchange(after(grad_patches, *moved))
    vectors = (
        fc1_bias, ln1_gain, ln1_bias, qv_bias[0], jnp.zeros_like(proj_bias), qv_bias[1], proj_bias,
        ln2_gain, ln2_bias, fc2_bias,
    )
    vectors = jnp.concatenate([v.astype(F32) for v in vectors]).reshape(1, -1)
    first = hidden // width

    def vector(k, wide=1):
        return pl.BlockSpec((1, wide * width), lambda *_: (0, (first + k) // wide))

    shapes = [
        ((padded, width), BF), ((width, padded), BF), ((padded, 3 * width), BF),
        ((heads // 2, 2 * padded, padded), BF), ((width, padded), BF),
        ((padded, width), F32), ((padded, width), BF), ((width, padded), BF),
    ]

    xs, a1t, qkv, prob, ot, h, a2, a2t = pl.pallas_call(
        partial(forward_kernel, rows=rows, heads=heads),
        grid_spec=pltpu.PrefetchScalarGridSpec(
            num_scalar_prefetch=2,
            grid=(n,),
            in_specs=[
                pl.BlockSpec((1, part, width), lambda i, at, keep: (at[0] * n + i, 0, 0)),
                *[per_image(0, part, width)] * (groups - 1),
                pl.BlockSpec((1, ns, width), lambda i, at, keep: (at[0] * n + i, 0, 0)),
                vector(0), vector(1), whole(qkv_weight.shape), vector(2, 3),
                whole(proj_weight.shape), vector(5), vector(6), vector(7),
            ],
            out_specs=[per_image(0, *shape) for shape, _ in shapes],
            scratch_shapes=[pltpu.VMEM((padded, width), F32)],
        ),
        out_shape=[struct(n, *shape, dtype=dtype) for shape, dtype in shapes],
        compiler_params=params(60),
        cost_estimate=cost(15),
        name="attention_forward",
    )(
        at, keep_mask, patches, *moved, specials, vectors, vectors, qkv_weight, vectors, proj_weight,
        vectors, vectors, vectors,
    )

    total = n * padded
    h, grads = together(h, grads)

    def owner(t, at):
        return t ^ lax.shift_right_logical(at[1], 1)

    once = pl.Buffered(1)
    out_rows, dh, dy, w2s, w2k, w1s, w1k, db1, small2 = pl.pallas_call(
        partial(feed_kernel, images=n),
        grid_spec=pltpu.PrefetchScalarGridSpec(
            num_scalar_prefetch=2,
            grid=(steps,),
            in_specs=[
                *[
                    pl.BlockSpec((n, part, width), lambda t, at, keep, k=k: (k, 0, 0), pipeline_mode=once)
                    for k in range(groups)
                ],
                pl.BlockSpec((n, ns, width), lambda t, at, keep: (at[0], 0, 0)),
                whole(h.shape, once), whole(a2.shape, once), whole(a2t.shape, once),
                pl.BlockSpec((width, chunk), lambda t, at, keep: (0, owner(t, at))),
                pl.BlockSpec((1, chunk), lambda t, at, keep: (0, owner(t, at))),
                pl.BlockSpec((chunk, width), lambda t, at, keep: (owner(t, at), 0)),
                vector(8), vector(6),
            ],
            out_specs=[
                whole((images, part + ns, width)),
                whole((n, padded, width)), whole((n, padded, width)),
                *[pl.BlockSpec((chunk // 2, width), lambda t, *_: (t, 0))] * 2,
                *[pl.BlockSpec((steps, 1, width // OWNERS, chunk), lambda t, at, keep: (0, owner(t, at), 0, 0))] * 2,
                pl.BlockSpec((1, chunk), lambda t, at, keep: (0, owner(t, at))),
                whole((4, width)),
            ],
            scratch_shapes=[
                pltpu.VMEM((total, width), F32), pltpu.VMEM((total, width), BF),
                pltpu.VMEM((total, width), F32), pltpu.VMEM((total, width), F32),
                pltpu.VMEM((total, chunk), BF), pltpu.VMEM((total, chunk), BF),
                pltpu.VMEM((width, total), BF),
            ],
        ),
        out_shape=[
            struct(images, part + ns, width),
            struct(n, padded, width, dtype=F32), struct(n, padded, width),
            *[struct(hidden // 2, width)] * 2, *[struct(steps, steps, width // OWNERS, chunk)] * 2,
            struct(1, hidden, dtype=F32), struct(4, width, dtype=F32),
        ],
        compiler_params=params(60),
        cost_estimate=cost(30),
        name="feed_forward",
    )(
        at, keep_mask, *[grads] * groups, grad_specials, h, a2, a2t, fc1_weight, vectors,
        fc2_weight, vectors, vectors,
    )

    n1 = width // OWNERS
    x_half, y_half = (None, 1), (1, None)
    if direct:
        ra, rb = swap(w1s, 1), swap(w2s, 1)
        ra, rb = together(ra, rb)
        wa, wb, ra, rb = (v.reshape(2, 2, steps, n1, chunk) for v in (w1k, w2k, ra, rb))
        as_, bs = sums([[(wa, x_half), (ra, x_half)], [(wb, y_half), (rb, y_half)]], mib=60)
        dy, as_, bs = together(dy, as_, bs)
        qa, qb = swap(as_, 2), swap(bs, 4)
    out_rows = exchange(out_rows)

    def per_image_last(*shape):
        return pl.BlockSpec(
            (1, *shape), lambda i, *_: (jnp.minimum(i, n - 1),) + (0,) * len(shape)
        )

    wide = 2 * width + COLUMNS
    dx_rows, small1, flat, cs, ck, ds_, dk_ = pl.pallas_call(
        partial(heads_kernel, images=n, heads=heads, part=part, ns=ns),
        grid_spec=pltpu.PrefetchScalarGridSpec(
            num_scalar_prefetch=1,
            grid=(n + 2,),
            in_specs=[
                per_image_last(padded, width), per_image_last(heads // 2, 2 * padded, padded),
                per_image_last(padded, 3 * width), ANY, ANY, per_image_last(padded, width),
                per_image_last(padded, width), vector(0), ANY, ANY, whole((4, width)),
                whole((1, hidden)),
            ],
            out_specs=[
                whole((images, part + ns, width)), whole((2, width)), whole((1, 3 * width)),
                *[whole((half, wide))] * 4,
            ],
            scratch_shapes=[
                pltpu.VMEM((padded, width), F32), pltpu.VMEM((total, 3 * width), BF),
                pltpu.VMEM((total, width), BF), pltpu.VMEM(proj_weight.shape, BF),
                pltpu.VMEM(qkv_weight.shape, BF), pltpu.VMEM(a1t.shape, BF), pltpu.VMEM(ot.shape, BF),
                pltpu.VMEM((half, total), BF), pltpu.VMEM((half, total), BF),
                pltpu.VMEM((width, COLUMNS), F32), pltpu.SemaphoreType.DMA((4,)),
            ],
        ),
        out_shape=[
            struct(images, part + ns, width), struct(2, width, dtype=F32),
            struct(1, 3 * width, dtype=F32), *[struct(half, wide)] * 4,
        ],
        compiler_params=params(60),
        cost_estimate=cost(22),
        name="attention_backward",
    )(at, dy, prob, qkv, proj_weight, qkv_weight, xs, dh, vectors, a1t, ot, small2, db1)

    cs, ds_, out_rows = together(cs, ds_, out_rows)
    dx_rows = exchange(dx_rows)

    if not direct:
        out_rows, out_specials = settle(out_rows, ns)
        dx_rows, dx_specials = settle(dx_rows, ns)
        return (
            out_rows, out_specials, dx_rows, dx_specials,
            *natural_sums(
                w1s, w1k, w2s, w2k, cs, ck, ds_, dk_, flat, small1, small2, db1
            ),
        )

    def near(v):
        return lax.ppermute(v, "seq", [(s, s ^ 1) for s in range(groups)])

    def far(v):
        return lax.ppermute(v, "seq", [(s, s ^ 2) for s in range(groups)])

    qa, qb, cs, ds_ = together(qa, qb, cs, ds_)
    as_, bs = sums(
        [[(wa, (1, 0)), (ra, (1, 0)), (qa, (1,))], [(wb, (0, 1)), (rb, (0, 1)), (qb, (1,))]]
    )
    as_, bs, cs, ds_ = together(as_, bs, cs, ds_)
    ta, tb = swap(as_, 4), swap(bs, 2)
    rc, rd = swap(cs, 1), swap(ds_, 1)
    rc, rd, ck, dk_ = together(rc, rd, ck, dk_)
    wc, wd, rc, rd = (v.reshape(2, 2, 2, n1 // 2, -1) for v in (ck, dk_, rc, rd))
    cs, ds_ = sums([[(wc, x_half), (rc, x_half)], [(wd, y_half), (rd, y_half)]])
    qc, qd = swap(cs, 2), swap(ds_, 4)
    out_rows, out_specials = settle(after(out_rows, cs), ns)
    ta, tb, cs, out_rows = together(ta, tb, cs, out_rows)
    e, es = sums(
        [
            [(wa, (0, 0)), (ra, (0, 0)), (qa, (0,)), (ta, ())],
            [(wb, (0, 0)), (rb, (0, 0)), (qb, (0,)), (tb, ())],
        ],
        at,
    )
    re = near(es)
    qc, qd, e = together(qc, qd, e)
    cs, ds_ = sums(
        [[(wc, (1, 0)), (rc, (1, 0)), (qc, (1,))], [(wd, (0, 1)), (rd, (0, 1)), (qd, (1,))]]
    )
    cs, ds_, re, dx_rows = together(cs, ds_, re, dx_rows)
    tc, td = swap(cs, 4), swap(ds_, 2)
    e = e + re
    e, g = e[: steps // 2], e[steps // 2 :]
    re, rg = far(e), far(g)
    e, g, tc, td = together(e, g, tc, td)
    f1, fs = sums(
        [
            [(wc, (0, 0)), (rc, (0, 0)), (qc, (0,)), (tc, ())],
            [(wd, (0, 0)), (rd, (0, 0)), (qd, (0,)), (td, ())],
        ],
        at,
    )
    rf = near(fs)
    f1, re, e = together(f1, re, e)
    e = e + re
    re = near(e)
    dx_rows, dx_specials = settle(after(dx_rows, e), ns)
    rf, dx_rows = together(rf, dx_rows)
    f1 = f1 + rf
    rf = far(f1)
    f1, rg, g = together(f1, rg, g)
    g = g + rg
    rg = near(g)
    rf, g = together(rf, g)
    f1 = f1 + rf
    rf = near(f1)
    re, rg, f1 = together(re, rg, f1)
    smem = pl.BlockSpec(memory_space=pltpu.SMEM)
    vmem = pl.BlockSpec(memory_space=pltpu.VMEM)
    d_fc1, d_fc2 = pl.pallas_call(
        finish_feed_kernel,
        in_specs=[smem, *[vmem] * 4],
        out_shape=[struct(n1, hidden, dtype=F32), struct(hidden // OWNERS, width, dtype=F32)],
        compiler_params=pltpu.CompilerParams(vmem_limit_bytes=60 * 2**20),
        cost_estimate=cost(2),
        name="finish_feed",
    )(at, e, re, g, rg)
    rf, d_fc1 = together(rf, d_fc1)
    done = pl.pallas_call(
        finish_kernel,
        in_specs=[smem, vmem, vmem],
        out_shape=[
            struct(n1, 3 * width, dtype=F32), struct(n1, width, dtype=F32),
            *[struct(1, n1, dtype=F32)] * 2, struct(2, n1, dtype=F32),
            *[struct(1, n1, dtype=F32)] * 4, struct(1, hidden // OWNERS, dtype=F32),
        ],
        compiler_params=pltpu.CompilerParams(vmem_limit_bytes=60 * 2**20),
        cost_estimate=cost(2),
        name="finish",
    )(at, f1.reshape(n1, -1), rf.reshape(n1, -1))
    d_qkv, d_proj, gain1, bias1, d_qv, gain2, bias2, d_fc2b, d_projb, d_fc1b = done

    def one(v):
        return v.reshape(-1)

    return (
        out_rows, out_specials, dx_rows, dx_specials,
        one(gain1), one(bias1), d_qkv, d_qv, d_proj, one(d_projb), one(gain2), one(bias2),
        d_fc1, one(d_fc1b), d_fc2, one(d_fc2b),
    )


def natural_sums(w1s, w1k, w2s, w2k, cs, ck, ds_, dk_, flat, small1, small2, db1):
    width = small1.shape[1]
    replicas = lax.axis_size("dp")

    def natural(sent, kept):
        if kept.ndim == 4:
            kept, sent = (v.transpose(0, 2, 1, 3).reshape(width // 2, -1) for v in (kept, sent))
        v = jnp.stack([kept, sent]).reshape(2, OWNERS // 2, -1, kept.shape[1])
        v = v.transpose(1, 0, 2, 3).reshape(-1, kept.shape[1])
        v = lax.psum_scatter(v, "dp", scatter_dimension=0, tiled=True)
        return lax.psum(v, "seq").astype(F32)

    d_fc1, d_fc2 = natural(w1s, w1k), natural(w2s, w2k)
    d_qk, d_vp = natural(cs, ck), natural(ds_, dk_)
    d_qkv = jnp.concatenate([d_qk[:, : 2 * width], d_vp[:, :width]], axis=1)
    d_proj = d_vp[:, width : 2 * width]
    flat = flat.reshape(3, width)
    vectors = jnp.concatenate([small1, flat[0:1], flat[2:3], small2, db1.reshape(-1, width)], axis=0)
    vectors = lax.psum(vectors, ("dp", "seq"))
    mine = lax.axis_index("dp")

    def shard(v):
        size = v.shape[-1] // replicas
        return lax.dynamic_slice_in_dim(v, mine * size, size, axis=v.ndim - 1)

    s = shard(vectors[:8])
    d_fc1b = shard(vectors[8:].reshape(-1))
    return s[0], s[1], d_qkv, s[2:4], d_proj, s[7], s[4], s[5], d_fc1, d_fc1b, d_fc2, s[6]


def solution(mesh):
    rows = P("dp", "seq", None)
    lead = P("dp", None, None)
    flat = P("dp")
    matrix = P("dp", None)
    return jax.shard_map(
        shards,
        mesh=mesh,
        in_specs=(rows, lead, matrix, *[P()] * 12, rows, lead),
        out_specs=(
            rows, lead, rows, lead, flat, flat, matrix, P(None, "dp"), matrix, flat, flat, flat,
            matrix, flat, matrix, flat,
        ),
        check_vma=False,
    )
```

```python
from functools import partial

import jax
import jax.numpy as jnp
from jax import lax
from jax.experimental import pallas as pl
from jax.experimental.pallas import tpu as pltpu
from jax.sharding import PartitionSpec as P

HEAD_DIM = 64
KEEP = 1.0 / 0.9
EPS = 1e-06
BF = jnp.bfloat16
F32 = jnp.float32
COLUMNS = 128
PACE = 0.3
OWNERS = 8
VMEM = 60 * 2**20

def dot(a, b):
    return lax.dot_general(a, b, (((1,), (0,)), ((), ())), preferred_element_type=F32)


def dot_nt(a, b):
    return lax.dot_general(a, b, (((1,), (1,)), ((), ())), preferred_element_type=F32)


def dot_tn(a, b):
    return lax.dot_general(a, b, (((0,), (0,)), ((), ())), preferred_element_type=F32)


def gelu_both(u):
    cdf = 0.5 + 0.5 * lax.erf(u * 0.5**0.5)
    return u * cdf, cdf + u * (jnp.exp(-0.5 * u * u) * 0.3989422804014327)


def normalize(x):
    center = x - jnp.mean(x, axis=-1, keepdims=True)
    inv = lax.rsqrt(jnp.mean(center * center, axis=-1, keepdims=True) + EPS)
    return center * inv, inv


def norm_back(up, hat, inv, gain):
    e = up * gain
    return inv * (
        e
        - jnp.mean(e, axis=-1, keepdims=True)
        - hat * jnp.mean(e * hat, axis=-1, keepdims=True)
    )


def both_heads(v, low):
    return jnp.concatenate([jnp.where(low, v, BF(0)), jnp.where(low, BF(0), v)], axis=0)


def colsum(v):
    return jnp.sum(v, axis=0, keepdims=True)


def place(b):
    return (b & 1) * (OWNERS // 2) + lax.shift_right_logical(b, 1)


def store_relative(ref, lead, value, d):
    n = value.shape[0] // OWNERS
    for b in range(OWNERS):
        spot = pl.multiple_of(place(b ^ d) * n, n)
        ref[lead, pl.ds(spot, n), :] = value[b * n : (b + 1) * n]


def unpacked(tall, i, images, part):
    base = part // 16 * 16
    rest = part - base
    last = tall[images * base :, :].astype(F32)
    row = last[:rest]
    for j in range(1, images):
        row = jnp.where(i == j, last[j * rest : (j + 1) * rest], row)
    most = tall[pl.ds(pl.multiple_of(i * base, base), base), :].astype(F32)
    return jnp.concatenate([most, row], axis=0)


def forward_kernel(
    at, keep, x0, x1, x2, x3, sp, g1, b1, wq, bq, wp, bp, g2, b2,
    xs, a1t, qkv, prob, ot, h, a2, a2t, buf, *, rows, heads,
):
    i = pl.program_id(0)
    d = at[1]
    part = x0.shape[1]
    ns = sp.shape[1]
    width = x0.shape[2]
    buf[...] = jnp.zeros_like(buf)
    buf[0:ns, :] = sp[0].astype(F32)
    came = [x0[0].astype(F32)]
    came += [unpacked(ref, i, x1.shape[0] // part, part) for ref in (x1, x2, x3)]
    for s in range(len(came)):
        k = (at[0] - s) & 3
        near, far = (jnp.where((k & 1) == 0, came[j], came[j + 1]) for j in (0, 2))
        buf[ns + s * part : ns + (s + 1) * part, :] = jnp.where(k < 2, near, far)
    x = buf[...]
    xs[0] = x.astype(BF)
    hat, _ = normalize(x)
    a1 = (hat * g1[...].astype(F32) + b1[...].astype(F32)).astype(BF)
    store_relative(a1t, 0, a1.T, d)
    both = (dot(a1, wq[...]) + bq[...]).astype(BF)
    qkv[0] = both
    padded = x.shape[0]
    low = lax.broadcasted_iota(jnp.int32, (padded, 2 * HEAD_DIM), 1) < HEAD_DIM
    seen = lax.broadcasted_iota(jnp.int32, (2 * padded, padded), 1) < rows
    outs = []
    for j in range(heads // 2):
        c = j * 2 * HEAD_DIM
        q = both[:, c : c + 2 * HEAD_DIM] * BF(HEAD_DIM**-0.5)
        k = both[:, width + c : width + c + 2 * HEAD_DIM]
        v = both[:, 2 * width + c : 2 * width + c + 2 * HEAD_DIM]
        s = jnp.where(seen, dot_nt(both_heads(q, low), k), -1e30)
        e = jnp.exp(s - jnp.max(s, axis=-1, keepdims=True))
        p = (e * (1.0 / jnp.sum(e, axis=-1, keepdims=True))).astype(BF)
        prob[0, j] = p
        pv = dot(p, v)
        outs.append(jnp.where(low, pv[:padded], pv[padded:]))
    o32 = jnp.concatenate(outs, axis=1)
    o = o32.astype(BF)
    store_relative(ot, 0, o.T, d)
    y = dot(o, wp[...]) + bp[...].astype(F32)
    m1 = keep[at[0] * pl.num_programs(0) + i, 0].astype(F32) * KEEP
    hh = x + m1 * y
    h[0] = hh
    hat2, _ = normalize(hh)
    n2 = (hat2 * g2[...].astype(F32) + b2[...].astype(F32)).astype(BF)
    a2[0] = n2
    store_relative(a2t, 0, n2.T, d)


def feed_kernel(
    at, keep, g0, g1, g2, g3, sg, h, a2, a2t, w1, b1, w2, b2, gain,
    out, dh, dy, w2s, w2k, w1s, w1k, db1, small,
    dout, dz, z, da2, acts, dus, across, *, images,
):
    t = pl.program_id(0)
    part = g0.shape[1] // images
    ns = sg.shape[1]
    padded = h.shape[1]

    @pl.when(t == 0)
    def _():
        for i in range(images):
            m2 = keep[at[0] * images + i, 1].astype(F32) * KEEP
            r = i * padded
            dout[r : r + padded, :] = jnp.zeros((padded, dout.shape[1]), F32)
            dout[r : r + ns, :] = sg[i].astype(F32)
            for k, ref in enumerate((g0, g1, g2, g3)):
                lo = r + ns + k * part
                dout[lo : lo + part, :] = unpacked(ref.at[0], i, images, part)
            dz[r : r + padded, :] = (dout[r : r + padded, :] * m2).astype(BF)
            across[:, r : r + padded] = a2t[i]
        z[...] = jnp.zeros_like(z)
        da2[...] = jnp.zeros_like(da2)

    wa = w1[...]
    wb = w2[...]
    bias = b1[...].astype(F32)
    db = None
    for i in range(images):
        r = slice(i * padded, (i + 1) * padded)
        g, slope = gelu_both(dot(a2[i], wa) + bias)
        acts[r, :] = g.astype(BF)
        du = (slope * dot_nt(dz[r, :], wb)).astype(BF)
        dus[r, :] = du
        s = colsum(du.astype(F32))
        db = s if db is None else db + s
    db1[...] = db
    z[...] += dot(acts[...], wb)
    da2[...] += dot_nt(dus[...], wa)
    half = across.shape[0] // 2
    w1k[...] = dot(across[:half, :], dus[...]).astype(BF).reshape(w1k.shape)
    w1s[...] = dot(across[half:, :], dus[...]).astype(BF).reshape(w1s.shape)
    half = acts.shape[1] // 2
    for side, ref in enumerate((w2k, w2s)):
        lo = pl.multiple_of(((at[1] & 1) ^ side) * half, half)
        ref[...] = dot_tn(acts[:, pl.ds(lo, half)], dz[...]).astype(BF)

    @pl.when(t == pl.num_programs(0) - 1)
    def _():
        gains = gain[...].astype(F32)
        sums = [jnp.zeros((1, dout.shape[1]), F32) for _ in range(4)]
        for i in range(images):
            m1 = keep[at[0] * images + i, 0].astype(F32) * KEEP
            m2 = keep[at[0] * images + i, 1].astype(F32) * KEEP
            r = slice(i * padded, (i + 1) * padded)
            x = h[i]
            z[r, :] = x + m2 * (z[r, :] + b2[...].astype(F32))
            for k in range(out.shape[0] // images):
                lo = i * padded + ns + k * part
                out[k * images + i] = jnp.concatenate(
                    [z[lo : lo + part, :], z[i * padded : i * padded + ns, :]], axis=0
                ).astype(BF)
            hat, inv = normalize(x)
            up = da2[r, :]
            grad = dout[r, :] + norm_back(up, hat, inv, gains)
            dh[i] = grad
            low = (m1 * grad).astype(BF)
            dy[i] = low
            for j, v in enumerate((up * hat, up, dz[r, :].astype(F32), low.astype(F32))):
                sums[j] = sums[j] + colsum(v)
        small[...] = jnp.concatenate(sums, axis=0)


def heads_kernel(
    at, dy, prob, qkv, wp_any, wq_any, xs, dh, gain, a1t_any, ot_any, small2, db1,
    out, small, flat, cs, ck, ds_, dk_,
    buf, dqkv, dys, wp, wq, a1t, ot, a1, o, cols, sems, *, images, heads, part, ns,
):
    i = pl.program_id(0)
    width = dy.shape[2]
    padded = dy.shape[1]
    fetches = [
        pltpu.make_async_copy(src, dst, sems.at[j])
        for j, (src, dst) in enumerate(((wp_any, wp), (wq_any, wq), (a1t_any, a1t), (ot_any, ot)))
    ]

    @pl.when(i == 0)
    def _():
        for fetch in fetches:
            fetch.start()
        fetches[0].wait()

    @pl.when(i < images)
    def _():
        low = lax.broadcasted_iota(jnp.int32, (padded, 2 * HEAD_DIM), 1) < HEAD_DIM
        mine = pl.ds(pl.multiple_of(i * padded, padded), padded)
        dys[mine, :] = dy[0]
        do = dot_nt(dy[0], wp[...]).astype(BF)
        for j in range(heads // 2):
            c = j * 2 * HEAD_DIM
            q = qkv[0, :, c : c + 2 * HEAD_DIM]
            k = qkv[0, :, width + c : width + c + 2 * HEAD_DIM]
            v = qkv[0, :, 2 * width + c : 2 * width + c + 2 * HEAD_DIM]
            g = both_heads(do[:, c : c + 2 * HEAD_DIM], low)
            p = prob[0, j]
            p32 = p.astype(F32)
            w = p32 * dot_nt(g, v)
            ds = (w - p32 * jnp.sum(w, axis=-1, keepdims=True)).astype(BF)
            dq = dot(ds, k)
            dq = jnp.where(low, dq[:padded], dq[padded:]) * HEAD_DIM**-0.5
            dk = dot_tn(ds, both_heads(q, low)) * HEAD_DIM**-0.5
            dqkv[mine, c : c + 2 * HEAD_DIM] = dq.astype(BF)
            dqkv[mine, width + c : width + c + 2 * HEAD_DIM] = dk.astype(BF)
            dqkv[mine, 2 * width + c : 2 * width + c + 2 * HEAD_DIM] = dot_tn(p, g).astype(BF)

        @pl.when(i == 0)
        def _():
            fetches[1].wait()

        grads = dqkv[mine, :]
        tops = colsum(grads.astype(F32))
        up = dot_nt(grads, wq[...])
        hat, inv = normalize(xs[0].astype(F32))
        buf[...] = dh[0] + norm_back(up, hat, inv, gain[...].astype(F32))
        for k in range(out.shape[0] // images):
            lo = ns + k * part
            out[k * images + i] = jnp.concatenate(
                [buf[lo : lo + part, :], buf[0:ns, :]], axis=0
            ).astype(BF)
        sums = jnp.concatenate([colsum(up * hat), colsum(up)], axis=0)

        @pl.when(i == 0)
        def _():
            flat[...] = tops
            small[...] = sums

        @pl.when(i > 0)
        def _():
            flat[...] += tops
            small[...] += sums

    @pl.when(i == images)
    def _():
        n = width // OWNERS
        per = db1.shape[1] // width
        eight = jnp.concatenate(
            [small[...], flat[:, :width], flat[:, 2 * width :], small2[...]], axis=0
        ).T
        long = jnp.broadcast_to(db1[...], (8, db1.shape[1])).T
        cols[...] = jnp.zeros_like(cols)
        for b in range(OWNERS):
            rows = pl.ds(pl.multiple_of(place(b ^ at[1]) * n, n), n)
            cols[rows, 0:8] = eight[b * n : (b + 1) * n]
            for j in range(per):
                lo = (b * per + j) * n
                cols[rows, 8 + j : 9 + j] = long[lo : lo + n, 0:1]
        fetches[2].wait()
        fetches[3].wait()

    half = cs.shape[0]
    for step, lo, c_ref, d_ref in ((images, half, cs, ds_), (images + 1, 0, ck, dk_)):

        @pl.when(i == step)
        def _(lo=lo, c_ref=c_ref, d_ref=d_ref):
            for n in range(images):
                lanes = slice(n * padded, (n + 1) * padded)
                a1[:, lanes] = a1t[n, lo : lo + half, :]
                o[:, lanes] = ot[n, lo : lo + half, :]
            c_ref[:, : 2 * width] = dot(a1[...], dqkv[:, : 2 * width]).astype(BF)
            c_ref[:, 2 * width :] = jnp.zeros((half, COLUMNS), BF)
            d_ref[:, :width] = dot(a1[...], dqkv[:, 2 * width :]).astype(BF)
            d_ref[:, width : 2 * width] = dot(o[...], dys[...]).astype(BF)
            d_ref[:, 2 * width :] = cols[lo : lo + half, :].astype(BF)


def settle_kernel(both, rows, specials):
    part = rows.shape[1]
    rows[...] = both[:, :part, :]
    specials[...] = both[:, part:, :]


def sum_kernel(*refs, jobs, pick):
    if pick:
        at, *refs = refs
        even = (at[0] & 1) == 0
    terms = [lead for job in jobs for lead in job]
    count = len(terms)
    arrays, outs, bufs, sems = refs[:count], refs[count : -count - 1], refs[-count - 1 : -1], refs[-1]
    fetches = [
        pltpu.make_async_copy(array.at[lead], buf, sems.at[k])
        for k, (array, lead, buf) in enumerate(zip(arrays, terms, bufs))
    ]
    for fetch in fetches:
        fetch.start()
    for fetch in fetches:
        fetch.wait()
    values = []
    for job in jobs:
        total = None
        for ref in bufs[: len(job)]:
            v = ref[...].astype(F32)
            total = v if total is None else total + v
        bufs = bufs[len(job) :]
        values.append(total)
    if pick:
        values = [jnp.where(even, *values), jnp.where(even, *values[::-1])]
    pieces = len(outs) // len(values)
    for k, ref in enumerate(outs):
        v, n = values[k // pieces], ref.shape[0]
        lo = k % pieces * n if pieces > 1 else 0
        ref[...] = (v if pieces == 1 else v[lo : lo + n]).astype(BF).reshape(ref.shape)


def sums(jobs, at=None, mib=60, pieces=1):
    arrays, bufs, out_shapes, leads = [], [], [], []
    for job in jobs:
        leads.append([])
        for v, lead in job:
            index = tuple(slice(None) if j is None else j for j in lead)
            kept = tuple(v.shape[k] for k, j in enumerate(lead) if j is None) + v.shape[len(lead) :]
            leads[-1].append(index)
            arrays.append(v)
            bufs.append(pltpu.VMEM(kept, BF))
        out_shapes += [struct(kept[0] // pieces, *kept[1:])] * pieces
    specs = [ANY] * len(arrays)
    if at is not None:
        specs.insert(0, pl.BlockSpec(memory_space=pltpu.SMEM))
        arrays.insert(0, at)
    return pl.pallas_call(
        partial(sum_kernel, jobs=leads, pick=at is not None),
        in_specs=specs,
        out_shape=out_shapes,
        scratch_shapes=[*bufs, pltpu.SemaphoreType.DMA((len(bufs),))],
        compiler_params=pltpu.CompilerParams(vmem_limit_bytes=mib * 2**20),
        cost_estimate=cost(2),
        name="sums",
    )(*arrays)


def finish_feed_kernel(at, mine_a, other_a, mine_b, other_b, fc1, fc2):
    even = (at[0] & 1) == 0
    n = fc1.shape[0]
    width = fc2.shape[1]
    half = mine_a.shape[0]
    for m in range(2 * half):
        mine, other = (mine_a, other_a) if m < half else (mine_b, other_b)
        p, q = mine[m % half].astype(F32), other[m % half].astype(F32)
        fc1[:, m * width : (m + 1) * width] = jnp.where(even, p, q)
        fc2[m * n : (m + 1) * n, :] = jnp.where(even, q, p)


def finish_kernel(at, mine, other, qkv, proj, *rest):
    vectors, long = rest[:-1], rest[-1]
    width = proj.shape[1]
    even = (at[0] & 1) == 0
    p, q = mine[...].astype(F32), other[...].astype(F32)
    c, d = jnp.where(even, p, q), jnp.where(even, q, p)
    qkv[:, : 2 * width] = c[:, : 2 * width]
    qkv[:, 2 * width :] = d[:, :width]
    proj[...] = d[:, width : 2 * width]
    n = c.shape[0]
    flat = d[:, 2 * width :].T
    row = 0
    for ref in vectors:
        ref[...] = flat[row : row + ref.shape[0]]
        row += ref.shape[0]
    parts = [flat[row + j : row + j + 1] for j in range(long.shape[0] // n)]
    long[...] = jnp.concatenate(parts, axis=1).reshape(long.shape)


def whole(shape, mode=None):
    return pl.BlockSpec(shape, lambda *_: (0,) * len(shape), pipeline_mode=mode)


def params(mib=60):
    return pltpu.CompilerParams(
        dimension_semantics=("arbitrary",), vmem_limit_bytes=mib * 2**20
    )


def cost(us):
    return pl.CostEstimate(flops=int(us * 1e9 * PACE), bytes_accessed=1, transcendentals=0)


ANY = pl.BlockSpec(memory_space=pl.ANY)


def struct(*shape, dtype=BF):
    return jax.ShapeDtypeStruct(shape, dtype)


def after(v, *others):
    return lax.optimization_barrier((v, *others))[0]


def together(*vs):
    return lax.optimization_barrier(vs)


def swap(v, bit):
    return lax.ppermute(v, "dp", [(s, s ^ bit) for s in range(lax.axis_size("dp"))])


def pack(x, blocks):
    images, part, width = x.shape
    x = x.reshape(blocks, images // blocks, part, width)
    base = part // 16 * 16
    return jnp.concatenate(
        [x[:, :, :base].reshape(blocks, -1, width), x[:, :, base:].reshape(blocks, -1, width)], axis=1
    )


def exchange(x):
    return lax.all_to_all(x, "seq", split_axis=0, concat_axis=0, tiled=True)


def settle(both, ns):
    images, rows, width = both.shape
    n = images // 4
    return pl.pallas_call(
        settle_kernel,
        grid=(images // n,),
        in_specs=[pl.BlockSpec((n, rows, width), lambda i: (i, 0, 0))],
        out_specs=[
            pl.BlockSpec((n, rows - ns, width), lambda i: (i, 0, 0)),
            pl.BlockSpec((n, ns, width), lambda i: (i, 0, 0)),
        ],
        out_shape=[struct(images, rows - ns, width), struct(images, ns, width)],
        compiler_params=params(60),
        cost_estimate=cost(2),
        name="settle",
    )(both)


def shards(
    patches, specials, keep_mask, ln1_gain, ln1_bias, qkv_weight, qv_bias, proj_weight, proj_bias,
    ln2_gain, ln2_bias, fc1_weight, fc1_bias, fc2_weight, fc2_bias, grad_patches, grad_specials,
):
    images, part, width = patches.shape
    ns = specials.shape[1]
    groups = lax.axis_size("seq")
    replicas = lax.axis_size("dp")
    hidden = fc1_weight.shape[1]
    heads = width // HEAD_DIM
    n = images // groups
    rows = ns + groups * part
    padded = -(-rows // 16) * 16
    steps = OWNERS // 2
    chunk = hidden // steps
    half = width // 2
    direct = replicas == OWNERS
    me = lax.axis_index("seq")
    d = lax.axis_index("dp") if direct else jnp.int32(0)
    at = jnp.stack([me, d]).astype(jnp.int32)

    def per_image(lo, *shape):
        return pl.BlockSpec((1, *shape), lambda i, *_: (lo + i,) + (0,) * len(shape))

    moved = []
    for k in range(1, groups):
        block = pack(lax.dynamic_slice_in_dim(patches, n * ((me + k) % groups), n), 1)[0]
        moved.append(lax.ppermute(block, "seq", [(s, (s + k) % groups) for s in range(groups)]))
    moved = together(*moved)
    grads = exchange(after(pack(grad_patches, groups), *moved))
    vectors = (
        fc1_bias, ln1_gain, ln1_bias, qv_bias[0], jnp.zeros_like(proj_bias), qv_bias[1], proj_bias,
        ln2_gain, ln2_bias, fc2_bias,
    )
    vectors = jnp.concatenate([v.astype(F32) for v in vectors]).reshape(1, -1)
    first = hidden // width

    def vector(k, wide=1):
        return pl.BlockSpec((1, wide * width), lambda *_: (0, (first + k) // wide))

    shapes = [
        ((padded, width), BF), ((width, padded), BF), ((padded, 3 * width), BF),
        ((heads // 2, 2 * padded, padded), BF), ((width, padded), BF),
        ((padded, width), F32), ((padded, width), BF), ((width, padded), BF),
    ]

    xs, a1t, qkv, prob, ot, h, a2, a2t = pl.pallas_call(
        partial(forward_kernel, rows=rows, heads=heads),
        grid_spec=pltpu.PrefetchScalarGridSpec(
            num_scalar_prefetch=2,
            grid=(n,),
            in_specs=[
                pl.BlockSpec((1, part, width), lambda i, at, keep: (at[0] * n + i, 0, 0)),
                *[whole((n * part, width))] * (groups - 1),
                pl.BlockSpec((1, ns, width), lambda i, at, keep: (at[0] * n + i, 0, 0)),
                vector(0), vector(1), whole(qkv_weight.shape), vector(2, 3),
                whole(proj_weight.shape), vector(5), vector(6), vector(7),
            ],
            out_specs=[per_image(0, *shape) for shape, _ in shapes],
            scratch_shapes=[pltpu.VMEM((padded, width), F32)],
        ),
        out_shape=[struct(n, *shape, dtype=dtype) for shape, dtype in shapes],
        compiler_params=params(60),
        cost_estimate=cost(15),
        name="attention_forward",
    )(
        at, keep_mask, patches, *moved, specials, vectors, vectors, qkv_weight, vectors, proj_weight,
        vectors, vectors, vectors,
    )

    total = n * padded
    h, grads = together(h, grads)

    def owner(t, at):
        return t ^ lax.shift_right_logical(at[1], 1)

    once = pl.Buffered(1)
    out_rows, dh, dy, w2s, w2k, w1s, w1k, db1, small2 = pl.pallas_call(
        partial(feed_kernel, images=n),
        grid_spec=pltpu.PrefetchScalarGridSpec(
            num_scalar_prefetch=2,
            grid=(steps,),
            in_specs=[
                *[
                    pl.BlockSpec((1, n * part, width), lambda t, at, keep, k=k: (k, 0, 0), pipeline_mode=once)
                    for k in range(groups)
                ],
                pl.BlockSpec((n, ns, width), lambda t, at, keep: (at[0], 0, 0)),
                whole(h.shape, once), whole(a2.shape, once), whole(a2t.shape, once),
                pl.BlockSpec((width, chunk), lambda t, at, keep: (0, owner(t, at))),
                pl.BlockSpec((1, chunk), lambda t, at, keep: (0, owner(t, at))),
                pl.BlockSpec((chunk, width), lambda t, at, keep: (owner(t, at), 0)),
                vector(8), vector(6),
            ],
            out_specs=[
                whole((images, part + ns, width)),
                whole((n, padded, width)), whole((n, padded, width)),
                *[pl.BlockSpec((chunk // 2, width), lambda t, *_: (t, 0))] * 2,
                *[pl.BlockSpec((steps, 1, width // OWNERS, chunk), lambda t, at, keep: (0, owner(t, at), 0, 0))] * 2,
                pl.BlockSpec((1, chunk), lambda t, at, keep: (0, owner(t, at))),
                whole((4, width)),
            ],
            scratch_shapes=[
                pltpu.VMEM((total, width), F32), pltpu.VMEM((total, width), BF),
                pltpu.VMEM((total, width), F32), pltpu.VMEM((total, width), F32),
                pltpu.VMEM((total, chunk), BF), pltpu.VMEM((total, chunk), BF),
                pltpu.VMEM((width, total), BF),
            ],
        ),
        out_shape=[
            struct(images, part + ns, width),
            struct(n, padded, width, dtype=F32), struct(n, padded, width),
            *[struct(hidden // 2, width)] * 2, *[struct(steps, steps, width // OWNERS, chunk)] * 2,
            struct(1, hidden, dtype=F32), struct(4, width, dtype=F32),
        ],
        compiler_params=params(60),
        cost_estimate=cost(30),
        name="feed_forward",
    )(
        at, keep_mask, *[grads] * groups, grad_specials, h, a2, a2t, fc1_weight, vectors,
        fc2_weight, vectors, vectors,
    )

    n1 = width // OWNERS
    x_half, y_half = (None, 1), (1, None)
    if direct:
        ra, rb = swap(w1s, 1), swap(w2s, 1)
        ra, rb = together(ra, rb)
        wa, wb, ra, rb = (v.reshape(2, 2, steps, n1, chunk) for v in (w1k, w2k, ra, rb))
        as_, bs = sums([[(wa, x_half), (ra, x_half)], [(wb, y_half), (rb, y_half)]], mib=60)
        dy, as_, bs = together(dy, as_, bs)
        qa, qb = swap(as_, 2), swap(bs, 4)
    out_rows = exchange(out_rows)

    def per_image_last(*shape):
        return pl.BlockSpec(
            (1, *shape), lambda i, *_: (jnp.minimum(i, n - 1),) + (0,) * len(shape)
        )

    wide = 2 * width + COLUMNS
    dx_rows, small1, flat, cs, ck, ds_, dk_ = pl.pallas_call(
        partial(heads_kernel, images=n, heads=heads, part=part, ns=ns),
        grid_spec=pltpu.PrefetchScalarGridSpec(
            num_scalar_prefetch=1,
            grid=(n + 2,),
            in_specs=[
                per_image_last(padded, width), per_image_last(heads // 2, 2 * padded, padded),
                per_image_last(padded, 3 * width), ANY, ANY, per_image_last(padded, width),
                per_image_last(padded, width), vector(0), ANY, ANY, whole((4, width)),
                whole((1, hidden)),
            ],
            out_specs=[
                whole((images, part + ns, width)), whole((2, width)), whole((1, 3 * width)),
                *[whole((half, wide))] * 4,
            ],
            scratch_shapes=[
                pltpu.VMEM((padded, width), F32), pltpu.VMEM((total, 3 * width), BF),
                pltpu.VMEM((total, width), BF), pltpu.VMEM(proj_weight.shape, BF),
                pltpu.VMEM(qkv_weight.shape, BF), pltpu.VMEM(a1t.shape, BF), pltpu.VMEM(ot.shape, BF),
                pltpu.VMEM((half, total), BF), pltpu.VMEM((half, total), BF),
                pltpu.VMEM((width, COLUMNS), F32), pltpu.SemaphoreType.DMA((4,)),
            ],
        ),
        out_shape=[
            struct(images, part + ns, width), struct(2, width, dtype=F32),
            struct(1, 3 * width, dtype=F32), *[struct(half, wide)] * 4,
        ],
        compiler_params=params(60),
        cost_estimate=cost(22),
        name="attention_backward",
    )(at, dy, prob, qkv, proj_weight, qkv_weight, xs, dh, vectors, a1t, ot, small2, db1)

    cs, ds_, out_rows = together(cs, ds_, out_rows)
    dx_rows = exchange(dx_rows)

    if not direct:
        out_rows, out_specials = settle(out_rows, ns)
        dx_rows, dx_specials = settle(dx_rows, ns)
        return (
            out_rows, out_specials, dx_rows, dx_specials,
            *natural_sums(
                w1s, w1k, w2s, w2k, cs, ck, ds_, dk_, flat, small1, small2, db1
            ),
        )

    def near(v):
        return lax.ppermute(v, "seq", [(s, s ^ 1) for s in range(groups)])

    def far(v):
        return lax.ppermute(v, "seq", [(s, s ^ 2) for s in range(groups)])

    qa, qb, cs, ds_ = together(qa, qb, cs, ds_)
    as_, bs = sums(
        [[(wa, (1, 0)), (ra, (1, 0)), (qa, (1,))], [(wb, (0, 1)), (rb, (0, 1)), (qb, (1,))]]
    )
    as_, bs, cs, ds_ = together(as_, bs, cs, ds_)
    ta, tb = swap(as_, 4), swap(bs, 2)
    rc, rd = swap(cs, 1), swap(ds_, 1)
    rc, rd, ck, dk_ = together(rc, rd, ck, dk_)
    wc, wd, rc, rd = (v.reshape(2, 2, 2, n1 // 2, -1) for v in (ck, dk_, rc, rd))
    cs, ds_ = sums([[(wc, x_half), (rc, x_half)], [(wd, y_half), (rd, y_half)]])
    qc, qd = swap(cs, 2), swap(ds_, 4)
    out_rows, out_specials = settle(after(out_rows, cs), ns)
    ta, tb, cs, out_rows = together(ta, tb, cs, out_rows)
    e, es = sums(
        [
            [(wa, (0, 0)), (ra, (0, 0)), (qa, (0,)), (ta, ())],
            [(wb, (0, 0)), (rb, (0, 0)), (qb, (0,)), (tb, ())],
        ],
        at,
    )
    re = near(es)
    qc, qd, e = together(qc, qd, e)
    cs, ds_ = sums(
        [[(wc, (1, 0)), (rc, (1, 0)), (qc, (1,))], [(wd, (0, 1)), (rd, (0, 1)), (qd, (1,))]]
    )
    cs, ds_, re = together(cs, ds_, re)
    tc, td = swap(cs, 4), swap(ds_, 2)
    e = e + re
    e, g = e[: steps // 2], e[steps // 2 :]
    re, rg = far(e), far(g)
    e, g, tc, td = together(e, g, tc, td)
    f1, fs = sums(
        [
            [(wc, (0, 0)), (rc, (0, 0)), (qc, (0,)), (tc, ())],
            [(wd, (0, 0)), (rd, (0, 0)), (qd, (0,)), (td, ())],
        ],
        at,
    )
    rf = near(fs)
    f1, re, e = together(f1, re, e)
    e = e + re
    re = near(e)
    dx_rows, dx_specials = settle(after(dx_rows, e), ns)
    rf, dx_rows = together(rf, dx_rows)
    f1 = f1 + rf
    rf = far(f1)
    f1, rg, g = together(f1, rg, g)
    g = g + rg
    rg = near(g)
    rf, g = together(rf, g)
    f1 = f1 + rf
    rf = near(f1)
    re, rg, f1 = together(re, rg, f1)
    smem = pl.BlockSpec(memory_space=pltpu.SMEM)
    vmem = pl.BlockSpec(memory_space=pltpu.VMEM)
    d_fc1, d_fc2 = pl.pallas_call(
        finish_feed_kernel,
        in_specs=[smem, *[vmem] * 4],
        out_shape=[struct(n1, hidden, dtype=F32), struct(hidden // OWNERS, width, dtype=F32)],
        compiler_params=pltpu.CompilerParams(vmem_limit_bytes=60 * 2**20),
        cost_estimate=cost(2),
        name="finish_feed",
    )(at, e, re, g, rg)
    rf, d_fc1 = together(rf, d_fc1)
    done = pl.pallas_call(
        finish_kernel,
        in_specs=[smem, vmem, vmem],
        out_shape=[
            struct(n1, 3 * width, dtype=F32), struct(n1, width, dtype=F32),
            *[struct(1, n1, dtype=F32)] * 2, struct(2, n1, dtype=F32),
            *[struct(1, n1, dtype=F32)] * 4, struct(hidden // OWNERS, dtype=F32),
        ],
        compiler_params=pltpu.CompilerParams(vmem_limit_bytes=60 * 2**20),
        cost_estimate=cost(2),
        name="finish",
    )(at, f1.reshape(n1, -1), rf.reshape(n1, -1))
    d_qkv, d_proj, gain1, bias1, d_qv, gain2, bias2, d_fc2b, d_projb, d_fc1b = done

    def one(v):
        return v.reshape(-1)

    return (
        out_rows, out_specials, dx_rows, dx_specials,
        one(gain1), one(bias1), d_qkv, d_qv, d_proj, one(d_projb), one(gain2), one(bias2),
        d_fc1, one(d_fc1b), d_fc2, one(d_fc2b),
    )


def natural_sums(w1s, w1k, w2s, w2k, cs, ck, ds_, dk_, flat, small1, small2, db1):
    width = small1.shape[1]
    replicas = lax.axis_size("dp")

    def natural(sent, kept):
        if kept.ndim == 4:
            kept, sent = (v.transpose(0, 2, 1, 3).reshape(width // 2, -1) for v in (kept, sent))
        v = jnp.stack([kept, sent]).reshape(2, OWNERS // 2, -1, kept.shape[1])
        v = v.transpose(1, 0, 2, 3).reshape(-1, kept.shape[1])
        v = lax.psum_scatter(v, "dp", scatter_dimension=0, tiled=True)
        return lax.psum(v, "seq").astype(F32)

    d_fc1, d_fc2 = natural(w1s, w1k), natural(w2s, w2k)
    d_qk, d_vp = natural(cs, ck), natural(ds_, dk_)
    d_qkv = jnp.concatenate([d_qk[:, : 2 * width], d_vp[:, :width]], axis=1)
    d_proj = d_vp[:, width : 2 * width]
    flat = flat.reshape(3, width)
    vectors = jnp.concatenate([small1, flat[0:1], flat[2:3], small2, db1.reshape(-1, width)], axis=0)
    vectors = lax.psum(vectors, ("dp", "seq"))
    mine = lax.axis_index("dp")

    def shard(v):
        size = v.shape[-1] // replicas
        return lax.dynamic_slice_in_dim(v, mine * size, size, axis=v.ndim - 1)

    s = shard(vectors[:8])
    d_fc1b = shard(vectors[8:].reshape(-1))
    return s[0], s[1], d_qkv, s[2:4], d_proj, s[7], s[4], s[5], d_fc1, d_fc1b, d_fc2, s[6]


def solution(mesh):
    rows = P("dp", "seq", None)
    lead = P("dp", None, None)
    flat = P("dp")
    matrix = P("dp", None)
    return jax.shard_map(
        shards,
        mesh=mesh,
        in_specs=(rows, lead, matrix, *[P()] * 12, rows, lead),
        out_specs=(
            rows, lead, rows, lead, flat, flat, matrix, P(None, "dp"), matrix, flat, flat, flat,
            matrix, flat, matrix, flat,
        ),
        check_vma=False,
    )
```

```python
from functools import partial

import jax
import jax.numpy as jnp
from jax import lax
from jax.experimental import pallas as pl
from jax.experimental.pallas import tpu as pltpu
from jax.sharding import PartitionSpec as P

HEAD_DIM = 64
KEEP = 1.0 / 0.9
EPS = 1e-06
BF = jnp.bfloat16
F32 = jnp.float32
COLUMNS = 128
PACE = 0.3
OWNERS = 8
VMEM = 60 * 2**20

def dot(a, b):
    return lax.dot_general(a, b, (((1,), (0,)), ((), ())), preferred_element_type=F32)


def dot_nt(a, b):
    return lax.dot_general(a, b, (((1,), (1,)), ((), ())), preferred_element_type=F32)


def dot_tn(a, b):
    return lax.dot_general(a, b, (((0,), (0,)), ((), ())), preferred_element_type=F32)


def gelu_both(u):
    cdf = 0.5 + 0.5 * lax.erf(u * 0.5**0.5)
    return u * cdf, cdf + u * (jnp.exp(-0.5 * u * u) * 0.3989422804014327)


def normalize(x):
    center = x - jnp.mean(x, axis=-1, keepdims=True)
    inv = lax.rsqrt(jnp.mean(center * center, axis=-1, keepdims=True) + EPS)
    return center * inv, inv


def norm_back(up, hat, inv, gain):
    e = up * gain
    return inv * (
        e
        - jnp.mean(e, axis=-1, keepdims=True)
        - hat * jnp.mean(e * hat, axis=-1, keepdims=True)
    )


def both_heads(v, low):
    return jnp.concatenate([jnp.where(low, v, BF(0)), jnp.where(low, BF(0), v)], axis=0)


def colsum(v):
    return jnp.sum(v, axis=0, keepdims=True)


def place(b):
    return (b & 1) * (OWNERS // 2) + lax.shift_right_logical(b, 1)


def store_relative(ref, lead, value, d):
    n = value.shape[0] // OWNERS
    for b in range(OWNERS):
        spot = pl.multiple_of(place(b ^ d) * n, n)
        ref[lead, pl.ds(spot, n), :] = value[b * n : (b + 1) * n]


def unpacked(tall, i, images, part):
    base = part // 16 * 16
    rest = part - base
    last = tall[images * base :, :].astype(F32)
    row = last[:rest]
    for j in range(1, images):
        row = jnp.where(i == j, last[j * rest : (j + 1) * rest], row)
    most = tall[pl.ds(pl.multiple_of(i * base, base), base), :].astype(F32)
    return jnp.concatenate([most, row], axis=0)


def forward_kernel(
    at, keep, x0, x1, x2, x3, sp, g1, b1, wq, bq, wp, bp, g2, b2,
    xs, a1t, qkv, prob, ot, h, a2, a2t, buf, *, rows, heads,
):
    i = pl.program_id(0)
    d = at[1]
    part = x0.shape[1]
    ns = sp.shape[1]
    width = x0.shape[2]
    buf[...] = jnp.zeros_like(buf)
    buf[0:ns, :] = sp[0].astype(F32)
    came = [x0[0].astype(F32)]
    came += [unpacked(ref, i, x1.shape[0] // part, part) for ref in (x1, x2, x3)]
    for s in range(len(came)):
        k = (at[0] - s) & 3
        near, far = (jnp.where((k & 1) == 0, came[j], came[j + 1]) for j in (0, 2))
        buf[ns + s * part : ns + (s + 1) * part, :] = jnp.where(k < 2, near, far)
    x = buf[...]
    xs[0] = x.astype(BF)
    hat, _ = normalize(x)
    a1 = (hat * g1[...].astype(F32) + b1[...].astype(F32)).astype(BF)
    store_relative(a1t, 0, a1.T, d)
    both = (dot(a1, wq[...]) + bq[...]).astype(BF)
    qkv[0] = both
    padded = x.shape[0]
    low = lax.broadcasted_iota(jnp.int32, (padded, 2 * HEAD_DIM), 1) < HEAD_DIM
    seen = lax.broadcasted_iota(jnp.int32, (2 * padded, padded), 1) < rows
    outs = []
    for j in range(heads // 2):
        c = j * 2 * HEAD_DIM
        q = both[:, c : c + 2 * HEAD_DIM] * BF(HEAD_DIM**-0.5)
        k = both[:, width + c : width + c + 2 * HEAD_DIM]
        v = both[:, 2 * width + c : 2 * width + c + 2 * HEAD_DIM]
        s = jnp.where(seen, dot_nt(both_heads(q, low), k), -1e30)
        e = jnp.exp(s - jnp.max(s, axis=-1, keepdims=True))
        p = (e * (1.0 / jnp.sum(e, axis=-1, keepdims=True))).astype(BF)
        prob[0, j] = p
        pv = dot(p, v)
        outs.append(jnp.where(low, pv[:padded], pv[padded:]))
    o32 = jnp.concatenate(outs, axis=1)
    o = o32.astype(BF)
    store_relative(ot, 0, o.T, d)
    y = dot(o, wp[...]) + bp[...].astype(F32)
    m1 = keep[at[0] * pl.num_programs(0) + i, 0].astype(F32) * KEEP
    hh = x + m1 * y
    h[0] = hh
    hat2, _ = normalize(hh)
    n2 = (hat2 * g2[...].astype(F32) + b2[...].astype(F32)).astype(BF)
    a2[0] = n2
    store_relative(a2t, 0, n2.T, d)


def feed_kernel(
    at, keep, g0, g1, g2, g3, sg, h, a2, a2t, w1, b1, w2, b2, gain,
    out, dh, dy, w2s, w2k, w1s, w1k, db1, small,
    dout, dz, z, da2, acts, dus, across, *, images,
):
    t = pl.program_id(0)
    part = g0.shape[1] // images
    ns = sg.shape[1]
    padded = h.shape[1]

    @pl.when(t == 0)
    def _():
        for i in range(images):
            m2 = keep[at[0] * images + i, 1].astype(F32) * KEEP
            r = i * padded
            dout[r : r + padded, :] = jnp.zeros((padded, dout.shape[1]), F32)
            dout[r : r + ns, :] = sg[i].astype(F32)
            for k, ref in enumerate((g0, g1, g2, g3)):
                lo = r + ns + k * part
                dout[lo : lo + part, :] = unpacked(ref.at[0], i, images, part)
            dz[r : r + padded, :] = (dout[r : r + padded, :] * m2).astype(BF)
            across[:, r : r + padded] = a2t[i]
        z[...] = jnp.zeros_like(z)
        da2[...] = jnp.zeros_like(da2)

    wa = w1[...]
    wb = w2[...]
    bias = b1[...].astype(F32)
    db = None
    for i in range(images):
        r = slice(i * padded, (i + 1) * padded)
        g, slope = gelu_both(dot(a2[i], wa) + bias)
        acts[r, :] = g.astype(BF)
        du = (slope * dot_nt(dz[r, :], wb)).astype(BF)
        dus[r, :] = du
        s = colsum(du.astype(F32))
        db = s if db is None else db + s
    db1[...] = db
    z[...] += dot(acts[...], wb)
    da2[...] += dot_nt(dus[...], wa)
    half = across.shape[0] // 2
    w1k[...] = dot(across[:half, :], dus[...]).astype(BF).reshape(w1k.shape)
    w1s[...] = dot(across[half:, :], dus[...]).astype(BF).reshape(w1s.shape)
    half = acts.shape[1] // 2
    for side, ref in enumerate((w2k, w2s)):
        lo = pl.multiple_of(((at[1] & 1) ^ side) * half, half)
        ref[...] = dot_tn(acts[:, pl.ds(lo, half)], dz[...]).astype(BF)

    @pl.when(t == pl.num_programs(0) - 1)
    def _():
        gains = gain[...].astype(F32)
        sums = [jnp.zeros((1, dout.shape[1]), F32) for _ in range(4)]
        for i in range(images):
            m1 = keep[at[0] * images + i, 0].astype(F32) * KEEP
            m2 = keep[at[0] * images + i, 1].astype(F32) * KEEP
            r = slice(i * padded, (i + 1) * padded)
            x = h[i]
            z[r, :] = x + m2 * (z[r, :] + b2[...].astype(F32))
            for k in range(out.shape[0] // images):
                lo = i * padded + ns + k * part
                out[k * images + i] = jnp.concatenate(
                    [z[lo : lo + part, :], z[i * padded : i * padded + ns, :]], axis=0
                ).astype(BF)
            hat, inv = normalize(x)
            up = da2[r, :]
            grad = dout[r, :] + norm_back(up, hat, inv, gains)
            dh[i] = grad
            low = (m1 * grad).astype(BF)
            dy[i] = low
            for j, v in enumerate((up * hat, up, dz[r, :].astype(F32), low.astype(F32))):
                sums[j] = sums[j] + colsum(v)
        small[...] = jnp.concatenate(sums, axis=0)


def heads_kernel(
    at, dy, prob, qkv, wp_any, wq_any, xs, dh, gain, a1t_any, ot_any, small2, db1,
    out, small, flat, cs, ck, ds_, dk_,
    buf, dqkv, dys, wp, wq, a1t, ot, a1, o, cols, sems, *, images, heads, part, ns,
):
    i = pl.program_id(0)
    width = dy.shape[2]
    padded = dy.shape[1]
    fetches = [
        pltpu.make_async_copy(src, dst, sems.at[j])
        for j, (src, dst) in enumerate(((wp_any, wp), (wq_any, wq), (a1t_any, a1t), (ot_any, ot)))
    ]

    @pl.when(i == 0)
    def _():
        for fetch in fetches:
            fetch.start()
        fetches[0].wait()

    @pl.when(i < images)
    def _():
        low = lax.broadcasted_iota(jnp.int32, (padded, 2 * HEAD_DIM), 1) < HEAD_DIM
        mine = pl.ds(pl.multiple_of(i * padded, padded), padded)
        dys[mine, :] = dy[0]
        do = dot_nt(dy[0], wp[...]).astype(BF)
        for j in range(heads // 2):
            c = j * 2 * HEAD_DIM
            q = qkv[0, :, c : c + 2 * HEAD_DIM]
            k = qkv[0, :, width + c : width + c + 2 * HEAD_DIM]
            v = qkv[0, :, 2 * width + c : 2 * width + c + 2 * HEAD_DIM]
            g = both_heads(do[:, c : c + 2 * HEAD_DIM], low)
            p = prob[0, j]
            p32 = p.astype(F32)
            w = p32 * dot_nt(g, v)
            ds = (w - p32 * jnp.sum(w, axis=-1, keepdims=True)).astype(BF)
            dq = dot(ds, k)
            dq = jnp.where(low, dq[:padded], dq[padded:]) * HEAD_DIM**-0.5
            dk = dot_tn(ds, both_heads(q, low)) * HEAD_DIM**-0.5
            dqkv[mine, c : c + 2 * HEAD_DIM] = dq.astype(BF)
            dqkv[mine, width + c : width + c + 2 * HEAD_DIM] = dk.astype(BF)
            dqkv[mine, 2 * width + c : 2 * width + c + 2 * HEAD_DIM] = dot_tn(p, g).astype(BF)

        @pl.when(i == 0)
        def _():
            fetches[1].wait()

        grads = dqkv[mine, :]
        tops = colsum(grads.astype(F32))
        up = dot_nt(grads, wq[...])
        hat, inv = normalize(xs[0].astype(F32))
        buf[...] = dh[0] + norm_back(up, hat, inv, gain[...].astype(F32))
        for k in range(out.shape[0] // images):
            lo = ns + k * part
            out[k * images + i] = jnp.concatenate(
                [buf[lo : lo + part, :], buf[0:ns, :]], axis=0
            ).astype(BF)
        sums = jnp.concatenate([colsum(up * hat), colsum(up)], axis=0)

        @pl.when(i == 0)
        def _():
            flat[...] = tops
            small[...] = sums

        @pl.when(i > 0)
        def _():
            flat[...] += tops
            small[...] += sums

    @pl.when(i == images)
    def _():
        n = width // OWNERS
        per = db1.shape[1] // width
        eight = jnp.concatenate(
            [small[...], flat[:, :width], flat[:, 2 * width :], small2[...]], axis=0
        ).T
        long = jnp.broadcast_to(db1[...], (8, db1.shape[1])).T
        cols[...] = jnp.zeros_like(cols)
        for b in range(OWNERS):
            rows = pl.ds(pl.multiple_of(place(b ^ at[1]) * n, n), n)
            cols[rows, 0:8] = eight[b * n : (b + 1) * n]
            for j in range(per):
                lo = (b * per + j) * n
                cols[rows, 8 + j : 9 + j] = long[lo : lo + n, 0:1]
        fetches[2].wait()
        fetches[3].wait()

    half = cs.shape[0]
    for step, lo, c_ref, d_ref in ((images, half, cs, ds_), (images + 1, 0, ck, dk_)):

        @pl.when(i == step)
        def _(lo=lo, c_ref=c_ref, d_ref=d_ref):
            for n in range(images):
                lanes = slice(n * padded, (n + 1) * padded)
                a1[:, lanes] = a1t[n, lo : lo + half, :]
                o[:, lanes] = ot[n, lo : lo + half, :]
            c_ref[:, : 2 * width] = dot(a1[...], dqkv[:, : 2 * width]).astype(BF)
            c_ref[:, 2 * width :] = jnp.zeros((half, COLUMNS), BF)
            d_ref[:, :width] = dot(a1[...], dqkv[:, 2 * width :]).astype(BF)
            d_ref[:, width : 2 * width] = dot(o[...], dys[...]).astype(BF)
            d_ref[:, 2 * width :] = cols[lo : lo + half, :].astype(BF)


def settle_kernel(both, rows, specials):
    part = rows.shape[1]
    rows[...] = both[:, :part, :]
    specials[...] = both[:, part:, :]


def sum_kernel(*refs, jobs, pick):
    if pick:
        at, *refs = refs
        even = (at[0] & 1) == 0
    terms = [lead for job in jobs for lead in job]
    count = len(terms)
    arrays, outs, bufs, sems = refs[:count], refs[count : -count - 1], refs[-count - 1 : -1], refs[-1]
    fetches = [
        pltpu.make_async_copy(array.at[lead], buf, sems.at[k])
        for k, (array, lead, buf) in enumerate(zip(arrays, terms, bufs))
    ]
    for fetch in fetches:
        fetch.start()
    for fetch in fetches:
        fetch.wait()
    values = []
    for job in jobs:
        total = None
        for ref in bufs[: len(job)]:
            v = ref[...].astype(F32)
            total = v if total is None else total + v
        bufs = bufs[len(job) :]
        values.append(total)
    if pick:
        values = [jnp.where(even, *values), jnp.where(even, *values[::-1])]
    for ref, v in zip(outs, values):
        ref[...] = v.astype(BF)


def sums(jobs, at=None, mib=63):
    arrays, bufs, out_shapes, leads = [], [], [], []
    for job in jobs:
        leads.append([])
        for v, lead in job:
            index = tuple(slice(None) if j is None else j for j in lead)
            kept = tuple(v.shape[k] for k, j in enumerate(lead) if j is None) + v.shape[len(lead) :]
            leads[-1].append(index)
            arrays.append(v)
            bufs.append(pltpu.VMEM(kept, BF))
        out_shapes.append(struct(*kept))
    specs = [ANY] * len(arrays)
    if at is not None:
        specs.insert(0, pl.BlockSpec(memory_space=pltpu.SMEM))
        arrays.insert(0, at)
    return pl.pallas_call(
        partial(sum_kernel, jobs=leads, pick=at is not None),
        in_specs=specs,
        out_shape=out_shapes,
        scratch_shapes=[*bufs, pltpu.SemaphoreType.DMA((len(bufs),))],
        compiler_params=pltpu.CompilerParams(vmem_limit_bytes=mib * 2**20),
        cost_estimate=cost(2),
        name="sums",
    )(*arrays)


def finish_feed_kernel(at, mine, other, *refs):
    fc1, fc2 = refs[-2:]
    even = (at[0] & 1) == 0
    n = fc1.shape[0]
    width = fc2.shape[1]
    for m in range(mine.shape[0]):
        p, q = mine[m].astype(F32), other[m].astype(F32)
        fc1[:, m * width : (m + 1) * width] = jnp.where(even, p, q)
        fc2[m * n : (m + 1) * n, :] = jnp.where(even, q, p)


def finish_kernel(at, mine, other, qkv, proj, *rest):
    vectors, long = rest[:-1], rest[-1]
    width = proj.shape[1]
    even = (at[0] & 1) == 0
    p, q = mine[...].astype(F32), other[...].astype(F32)
    c, d = jnp.where(even, p, q), jnp.where(even, q, p)
    qkv[:, : 2 * width] = c[:, : 2 * width]
    qkv[:, 2 * width :] = d[:, :width]
    proj[...] = d[:, width : 2 * width]
    n = c.shape[0]
    flat = d[:, 2 * width :].T
    row = 0
    for ref in vectors:
        ref[...] = flat[row : row + ref.shape[0]]
        row += ref.shape[0]
    parts = [flat[row + j : row + j + 1] for j in range(long.shape[0] // n)]
    long[...] = jnp.concatenate(parts, axis=1).reshape(long.shape)


def whole(shape, mode=None):
    return pl.BlockSpec(shape, lambda *_: (0,) * len(shape), pipeline_mode=mode)


def params(mib=63):
    return pltpu.CompilerParams(
        dimension_semantics=("arbitrary",), vmem_limit_bytes=mib * 2**20
    )


def cost(us):
    return pl.CostEstimate(flops=int(us * 1e9 * PACE), bytes_accessed=1, transcendentals=0)


ANY = pl.BlockSpec(memory_space=pl.ANY)


def struct(*shape, dtype=BF):
    return jax.ShapeDtypeStruct(shape, dtype)


def after(v, *others):
    return lax.optimization_barrier((v, *others))[0]


def together(*vs):
    return lax.optimization_barrier(vs)


def swap(v, bit):
    return lax.ppermute(v, "dp", [(s, s ^ bit) for s in range(lax.axis_size("dp"))])


def pack(x, blocks):
    images, part, width = x.shape
    x = x.reshape(blocks, images // blocks, part, width)
    base = part // 16 * 16
    return jnp.concatenate(
        [x[:, :, :base].reshape(blocks, -1, width), x[:, :, base:].reshape(blocks, -1, width)], axis=1
    )


def exchange(x):
    return lax.all_to_all(x, "seq", split_axis=0, concat_axis=0, tiled=True)


def settle(both, ns):
    images, rows, width = both.shape
    n = images // 4
    return pl.pallas_call(
        settle_kernel,
        grid=(images // n,),
        in_specs=[pl.BlockSpec((n, rows, width), lambda i: (i, 0, 0))],
        out_specs=[
            pl.BlockSpec((n, rows - ns, width), lambda i: (i, 0, 0)),
            pl.BlockSpec((n, ns, width), lambda i: (i, 0, 0)),
        ],
        out_shape=[struct(images, rows - ns, width), struct(images, ns, width)],
        compiler_params=params(60),
        cost_estimate=cost(2),
        name="settle",
    )(both)


def shards(
    patches, specials, keep_mask, ln1_gain, ln1_bias, qkv_weight, qv_bias, proj_weight, proj_bias,
    ln2_gain, ln2_bias, fc1_weight, fc1_bias, fc2_weight, fc2_bias, grad_patches, grad_specials,
):
    images, part, width = patches.shape
    ns = specials.shape[1]
    groups = lax.axis_size("seq")
    replicas = lax.axis_size("dp")
    hidden = fc1_weight.shape[1]
    heads = width // HEAD_DIM
    n = images // groups
    rows = ns + groups * part
    padded = -(-rows // 16) * 16
    steps = OWNERS // 2
    chunk = hidden // steps
    half = width // 2
    direct = replicas == OWNERS
    me = lax.axis_index("seq")
    d = lax.axis_index("dp") if direct else jnp.int32(0)
    at = jnp.stack([me, d]).astype(jnp.int32)

    def per_image(lo, *shape):
        return pl.BlockSpec((1, *shape), lambda i, *_: (lo + i,) + (0,) * len(shape))

    moved = []
    for k in range(1, groups):
        block = pack(lax.dynamic_slice_in_dim(patches, n * ((me + k) % groups), n), 1)[0]
        moved.append(lax.ppermute(block, "seq", [(s, (s + k) % groups) for s in range(groups)]))
    moved = together(*moved)
    grads = exchange(after(pack(grad_patches, groups), *moved))
    vectors = (
        fc1_bias, ln1_gain, ln1_bias, qv_bias[0], jnp.zeros_like(proj_bias), qv_bias[1], proj_bias,
        ln2_gain, ln2_bias, fc2_bias,
    )
    vectors = jnp.concatenate([v.astype(F32) for v in vectors]).reshape(1, -1)
    first = hidden // width

    def vector(k, wide=1):
        return pl.BlockSpec((1, wide * width), lambda *_: (0, (first + k) // wide))

    shapes = [
        ((padded, width), BF), ((width, padded), BF), ((padded, 3 * width), BF),
        ((heads // 2, 2 * padded, padded), BF), ((width, padded), BF),
        ((padded, width), F32), ((padded, width), BF), ((width, padded), BF),
    ]

    xs, a1t, qkv, prob, ot, h, a2, a2t = pl.pallas_call(
        partial(forward_kernel, rows=rows, heads=heads),
        grid_spec=pltpu.PrefetchScalarGridSpec(
            num_scalar_prefetch=2,
            grid=(n,),
            in_specs=[
                pl.BlockSpec((1, part, width), lambda i, at, keep: (at[0] * n + i, 0, 0)),
                *[whole((n * part, width))] * (groups - 1),
                pl.BlockSpec((1, ns, width), lambda i, at, keep: (at[0] * n + i, 0, 0)),
                vector(0), vector(1), whole(qkv_weight.shape), vector(2, 3),
                whole(proj_weight.shape), vector(5), vector(6), vector(7),
            ],
            out_specs=[per_image(0, *shape) for shape, _ in shapes],
            scratch_shapes=[pltpu.VMEM((padded, width), F32)],
        ),
        out_shape=[struct(n, *shape, dtype=dtype) for shape, dtype in shapes],
        compiler_params=params(63),
        cost_estimate=cost(15),
        name="attention_forward",
    )(
        at, keep_mask, patches, *moved, specials, vectors, vectors, qkv_weight, vectors, proj_weight,
        vectors, vectors, vectors,
    )

    total = n * padded
    h, grads = together(h, grads)

    def owner(t, at):
        return t ^ lax.shift_right_logical(at[1], 1)

    once = pl.Buffered(1)
    out_rows, dh, dy, w2s, w2k, w1s, w1k, db1, small2 = pl.pallas_call(
        partial(feed_kernel, images=n),
        grid_spec=pltpu.PrefetchScalarGridSpec(
            num_scalar_prefetch=2,
            grid=(steps,),
            in_specs=[
                *[
                    pl.BlockSpec((1, n * part, width), lambda t, at, keep, k=k: (k, 0, 0), pipeline_mode=once)
                    for k in range(groups)
                ],
                pl.BlockSpec((n, ns, width), lambda t, at, keep: (at[0], 0, 0)),
                whole(h.shape, once), whole(a2.shape, once), whole(a2t.shape, once),
                pl.BlockSpec((width, chunk), lambda t, at, keep: (0, owner(t, at))),
                pl.BlockSpec((1, chunk), lambda t, at, keep: (0, owner(t, at))),
                pl.BlockSpec((chunk, width), lambda t, at, keep: (owner(t, at), 0)),
                vector(8), vector(6),
            ],
            out_specs=[
                whole((images, part + ns, width)),
                whole((n, padded, width)), whole((n, padded, width)),
                *[pl.BlockSpec((chunk // 2, width), lambda t, *_: (t, 0))] * 2,
                *[pl.BlockSpec((steps, 1, width // OWNERS, chunk), lambda t, at, keep: (0, owner(t, at), 0, 0))] * 2,
                pl.BlockSpec((1, chunk), lambda t, at, keep: (0, owner(t, at))),
                whole((4, width)),
            ],
            scratch_shapes=[
                pltpu.VMEM((total, width), F32), pltpu.VMEM((total, width), BF),
                pltpu.VMEM((total, width), F32), pltpu.VMEM((total, width), F32),
                pltpu.VMEM((total, chunk), BF), pltpu.VMEM((total, chunk), BF),
                pltpu.VMEM((width, total), BF),
            ],
        ),
        out_shape=[
            struct(images, part + ns, width),
            struct(n, padded, width, dtype=F32), struct(n, padded, width),
            *[struct(hidden // 2, width)] * 2, *[struct(steps, steps, width // OWNERS, chunk)] * 2,
            struct(1, hidden, dtype=F32), struct(4, width, dtype=F32),
        ],
        compiler_params=params(63),
        cost_estimate=cost(30),
        name="feed_forward",
    )(
        at, keep_mask, *[grads] * groups, grad_specials, h, a2, a2t, fc1_weight, vectors,
        fc2_weight, vectors, vectors,
    )

    n1 = width // OWNERS
    x_half, y_half = (None, 1), (1, None)
    if direct:
        ra, rb = swap(w1s, 1), swap(w2s, 1)
        ra, rb = together(ra, rb)
        wa, wb, ra, rb = (v.reshape(2, 2, steps, n1, chunk) for v in (w1k, w2k, ra, rb))
        as_, bs = sums([[(wa, x_half), (ra, x_half)], [(wb, y_half), (rb, y_half)]], mib=63)
        dy, as_, bs = together(dy, as_, bs)
        qa, qb = swap(as_, 2), swap(bs, 4)
    out_rows = exchange(out_rows)

    def per_image_last(*shape):
        return pl.BlockSpec(
            (1, *shape), lambda i, *_: (jnp.minimum(i, n - 1),) + (0,) * len(shape)
        )

    wide = 2 * width + COLUMNS
    dx_rows, small1, flat, cs, ck, ds_, dk_ = pl.pallas_call(
        partial(heads_kernel, images=n, heads=heads, part=part, ns=ns),
        grid_spec=pltpu.PrefetchScalarGridSpec(
            num_scalar_prefetch=1,
            grid=(n + 2,),
            in_specs=[
                per_image_last(padded, width), per_image_last(heads // 2, 2 * padded, padded),
                per_image_last(padded, 3 * width), ANY, ANY, per_image_last(padded, width),
                per_image_last(padded, width), vector(0), ANY, ANY, whole((4, width)),
                whole((1, hidden)),
            ],
            out_specs=[
                whole((images, part + ns, width)), whole((2, width)), whole((1, 3 * width)),
                *[whole((half, wide))] * 4,
            ],
            scratch_shapes=[
                pltpu.VMEM((padded, width), F32), pltpu.VMEM((total, 3 * width), BF),
                pltpu.VMEM((total, width), BF), pltpu.VMEM(proj_weight.shape, BF),
                pltpu.VMEM(qkv_weight.shape, BF), pltpu.VMEM(a1t.shape, BF), pltpu.VMEM(ot.shape, BF),
                pltpu.VMEM((half, total), BF), pltpu.VMEM((half, total), BF),
                pltpu.VMEM((width, COLUMNS), F32), pltpu.SemaphoreType.DMA((4,)),
            ],
        ),
        out_shape=[
            struct(images, part + ns, width), struct(2, width, dtype=F32),
            struct(1, 3 * width, dtype=F32), *[struct(half, wide)] * 4,
        ],
        compiler_params=params(63),
        cost_estimate=cost(22),
        name="attention_backward",
    )(at, dy, prob, qkv, proj_weight, qkv_weight, xs, dh, vectors, a1t, ot, small2, db1)

    cs, ds_, out_rows = together(cs, ds_, out_rows)
    dx_rows = exchange(dx_rows)

    if not direct:
        out_rows, out_specials = settle(out_rows, ns)
        dx_rows, dx_specials = settle(dx_rows, ns)
        return (
            out_rows, out_specials, dx_rows, dx_specials,
            *natural_sums(
                w1s, w1k, w2s, w2k, cs, ck, ds_, dk_, flat, small1, small2, db1
            ),
        )

    def near(v):
        return lax.ppermute(v, "seq", [(s, s ^ 1) for s in range(groups)])

    def far(v):
        return lax.ppermute(v, "seq", [(s, s ^ 2) for s in range(groups)])

    qa, qb, cs, ds_ = together(qa, qb, cs, ds_)
    as_, bs = sums(
        [[(wa, (1, 0)), (ra, (1, 0)), (qa, (1,))], [(wb, (0, 1)), (rb, (0, 1)), (qb, (1,))]]
    )
    as_, bs, cs, ds_ = together(as_, bs, cs, ds_)
    ta, tb = swap(as_, 4), swap(bs, 2)
    rc, rd = swap(cs, 1), swap(ds_, 1)
    rc, rd, ck, dk_ = together(rc, rd, ck, dk_)
    wc, wd, rc, rd = (v.reshape(2, 2, 2, n1 // 2, -1) for v in (ck, dk_, rc, rd))
    cs, ds_ = sums([[(wc, x_half), (rc, x_half)], [(wd, y_half), (rd, y_half)]])
    qc, qd = swap(cs, 2), swap(ds_, 4)
    ta, tb, cs = together(ta, tb, cs)
    e, es = sums(
        [
            [(wa, (0, 0)), (ra, (0, 0)), (qa, (0,)), (ta, ())],
            [(wb, (0, 0)), (rb, (0, 0)), (qb, (0,)), (tb, ())],
        ],
        at,
    )
    re = near(es)
    out_rows, out_specials = settle(after(out_rows, e), ns)
    qc, qd, e, out_rows = together(qc, qd, e, out_rows)
    cs, ds_ = sums(
        [[(wc, (1, 0)), (rc, (1, 0)), (qc, (1,))], [(wd, (0, 1)), (rd, (0, 1)), (qd, (1,))]],
        mib=60,
    )
    cs, ds_, re = together(cs, ds_, re)
    tc, td = swap(cs, 4), swap(ds_, 2)
    e = e + re
    e, g = e[: steps // 2], e[steps // 2 :]
    re, rg = far(e), far(g)
    e, g, tc, td = together(e, g, tc, td)
    f1, fs = sums(
        [
            [(wc, (0, 0)), (rc, (0, 0)), (qc, (0,)), (tc, ())],
            [(wd, (0, 0)), (rd, (0, 0)), (qd, (0,)), (td, ())],
        ],
        at,
        mib=60,
    )
    rf = near(fs)
    f1, re, e = together(f1, re, e)
    e = e + re
    re = near(e)
    dx_rows, dx_specials = settle(after(dx_rows, e), ns)
    rf, dx_rows = together(rf, dx_rows)
    f1 = f1 + rf
    rf = far(f1)
    f1, rg, g = together(f1, rg, g)
    g = g + rg
    rg = near(g)
    rf, g = together(rf, g)
    f1 = f1 + rf
    rf = near(f1)
    re, f1 = together(re, f1)
    smem = pl.BlockSpec(memory_space=pltpu.SMEM)
    vmem = pl.BlockSpec(memory_space=pltpu.VMEM)

    def finish_feed(k, mine, other, *before):
        return pl.pallas_call(
            finish_feed_kernel,
            grid=(1,),
            in_specs=[smem, whole(mine.shape), whole(other.shape), *[ANY] * len(before)],
            out_specs=[
                pl.BlockSpec((n1, hidden // 2), lambda i: (0, k)),
                pl.BlockSpec((hidden // OWNERS // 2, width), lambda i: (k, 0)),
            ],
            out_shape=[struct(n1, hidden, dtype=F32), struct(hidden // OWNERS, width, dtype=F32)],
            input_output_aliases={3 + j: j for j in range(len(before))},
            compiler_params=params(60),
            cost_estimate=cost(2),
            name="finish_feed",
        )(at, mine, other, *before)

    d_fc1, d_fc2 = finish_feed(0, e, re)
    rg, d_fc1, d_fc2 = together(rg, d_fc1, d_fc2)
    d_fc1, d_fc2 = finish_feed(1, g, rg, d_fc1, d_fc2)
    rf, d_fc1 = together(rf, d_fc1)
    done = pl.pallas_call(
        finish_kernel,
        in_specs=[smem, vmem, vmem],
        out_shape=[
            struct(n1, 3 * width, dtype=F32), struct(n1, width, dtype=F32),
            *[struct(1, n1, dtype=F32)] * 2, struct(2, n1, dtype=F32),
            *[struct(1, n1, dtype=F32)] * 4, struct(hidden // OWNERS, dtype=F32),
        ],
        compiler_params=pltpu.CompilerParams(vmem_limit_bytes=60 * 2**20),
        cost_estimate=cost(2),
        name="finish",
    )(at, f1.reshape(n1, -1), rf.reshape(n1, -1))
    d_qkv, d_proj, gain1, bias1, d_qv, gain2, bias2, d_fc2b, d_projb, d_fc1b = done

    def one(v):
        return v.reshape(-1)

    return (
        out_rows, out_specials, dx_rows, dx_specials,
        one(gain1), one(bias1), d_qkv, d_qv, d_proj, one(d_projb), one(gain2), one(bias2),
        d_fc1, one(d_fc1b), d_fc2, one(d_fc2b),
    )


def natural_sums(w1s, w1k, w2s, w2k, cs, ck, ds_, dk_, flat, small1, small2, db1):
    width = small1.shape[1]
    replicas = lax.axis_size("dp")

    def natural(sent, kept):
        if kept.ndim == 4:
            kept, sent = (v.transpose(0, 2, 1, 3).reshape(width // 2, -1) for v in (kept, sent))
        v = jnp.stack([kept, sent]).reshape(2, OWNERS // 2, -1, kept.shape[1])
        v = v.transpose(1, 0, 2, 3).reshape(-1, kept.shape[1])
        v = lax.psum_scatter(v, "dp", scatter_dimension=0, tiled=True)
        return lax.psum(v, "seq").astype(F32)

    d_fc1, d_fc2 = natural(w1s, w1k), natural(w2s, w2k)
    d_qk, d_vp = natural(cs, ck), natural(ds_, dk_)
    d_qkv = jnp.concatenate([d_qk[:, : 2 * width], d_vp[:, :width]], axis=1)
    d_proj = d_vp[:, width : 2 * width]
    flat = flat.reshape(3, width)
    vectors = jnp.concatenate([small1, flat[0:1], flat[2:3], small2, db1.reshape(-1, width)], axis=0)
    vectors = lax.psum(vectors, ("dp", "seq"))
    mine = lax.axis_index("dp")

    def shard(v):
        size = v.shape[-1] // replicas
        return lax.dynamic_slice_in_dim(v, mine * size, size, axis=v.ndim - 1)

    s = shard(vectors[:8])
    d_fc1b = shard(vectors[8:].reshape(-1))
    return s[0], s[1], d_qkv, s[2:4], d_proj, s[7], s[4], s[5], d_fc1, d_fc1b, d_fc2, s[6]


def solution(mesh):
    rows = P("dp", "seq", None)
    lead = P("dp", None, None)
    flat = P("dp")
    matrix = P("dp", None)
    return jax.shard_map(
        shards,
        mesh=mesh,
        in_specs=(rows, lead, matrix, *[P()] * 12, rows, lead),
        out_specs=(
            rows, lead, rows, lead, flat, flat, matrix, P(None, "dp"), matrix, flat, flat, flat,
            matrix, flat, matrix, flat,
        ),
        check_vma=False,
    )
```

```python
from functools import partial

import jax
import jax.numpy as jnp
from jax import lax
from jax.experimental import pallas as pl
from jax.experimental.pallas import tpu as pltpu
from jax.sharding import PartitionSpec as P

HEAD_DIM = 64
KEEP = 1.0 / 0.9
EPS = 1e-06
BF = jnp.bfloat16
F32 = jnp.float32
COLUMNS = 128
PACE = 0.3
OWNERS = 8
VMEM = 60 * 2**20

def dot(a, b):
    return lax.dot_general(a, b, (((1,), (0,)), ((), ())), preferred_element_type=F32)


def dot_nt(a, b):
    return lax.dot_general(a, b, (((1,), (1,)), ((), ())), preferred_element_type=F32)


def dot_tn(a, b):
    return lax.dot_general(a, b, (((0,), (0,)), ((), ())), preferred_element_type=F32)


def gelu_both(u):
    cdf = 0.5 + 0.5 * lax.erf(u * 0.5**0.5)
    return u * cdf, cdf + u * (jnp.exp(-0.5 * u * u) * 0.3989422804014327)


def normalize(x):
    center = x - jnp.mean(x, axis=-1, keepdims=True)
    inv = lax.rsqrt(jnp.mean(center * center, axis=-1, keepdims=True) + EPS)
    return center * inv, inv


def norm_back(up, hat, inv, gain):
    e = up * gain
    return inv * (
        e
        - jnp.mean(e, axis=-1, keepdims=True)
        - hat * jnp.mean(e * hat, axis=-1, keepdims=True)
    )


def both_heads(v, low):
    return jnp.concatenate([jnp.where(low, v, BF(0)), jnp.where(low, BF(0), v)], axis=0)


def colsum(v):
    return jnp.sum(v, axis=0, keepdims=True)


def place(b):
    return (b & 1) * (OWNERS // 2) + lax.shift_right_logical(b, 1)


def store_relative(ref, lead, value, d):
    n = value.shape[0] // OWNERS
    for b in range(OWNERS):
        spot = pl.multiple_of(place(b ^ d) * n, n)
        ref[lead, pl.ds(spot, n), :] = value[b * n : (b + 1) * n]


def unpacked(tall, i, images, part):
    base = part // 16 * 16
    rest = part - base
    last = tall[images * base :, :].astype(F32)
    row = last[:rest]
    for j in range(1, images):
        row = jnp.where(i == j, last[j * rest : (j + 1) * rest], row)
    most = tall[pl.ds(pl.multiple_of(i * base, base), base), :].astype(F32)
    return jnp.concatenate([most, row], axis=0)


def forward_kernel(
    at, keep, x0, x1, x2, x3, sp, g1, b1, wq, bq, wp, bp, g2, b2,
    xs, a1t, qkv, prob, ot, h, a2, a2t, buf, *, rows, heads,
):
    i = pl.program_id(0)
    d = at[1]
    part = x0.shape[1]
    ns = sp.shape[1]
    width = x0.shape[2]
    buf[...] = jnp.zeros_like(buf)
    buf[0:ns, :] = sp[0].astype(F32)
    came = [x0[0].astype(F32)]
    came += [unpacked(ref, i, x1.shape[0] // part, part) for ref in (x1, x2, x3)]
    for s in range(len(came)):
        k = (at[0] - s) & 3
        near, far = (jnp.where((k & 1) == 0, came[j], came[j + 1]) for j in (0, 2))
        buf[ns + s * part : ns + (s + 1) * part, :] = jnp.where(k < 2, near, far)
    x = buf[...]
    xs[0] = x.astype(BF)
    hat, _ = normalize(x)
    a1 = (hat * g1[...].astype(F32) + b1[...].astype(F32)).astype(BF)
    store_relative(a1t, 0, a1.T, d)
    both = (dot(a1, wq[...]) + bq[...]).astype(BF)
    qkv[0] = both
    padded = x.shape[0]
    low = lax.broadcasted_iota(jnp.int32, (padded, 2 * HEAD_DIM), 1) < HEAD_DIM
    seen = lax.broadcasted_iota(jnp.int32, (2 * padded, padded), 1) < rows
    outs = []
    for j in range(heads // 2):
        c = j * 2 * HEAD_DIM
        q = both[:, c : c + 2 * HEAD_DIM] * BF(HEAD_DIM**-0.5)
        k = both[:, width + c : width + c + 2 * HEAD_DIM]
        v = both[:, 2 * width + c : 2 * width + c + 2 * HEAD_DIM]
        s = jnp.where(seen, dot_nt(both_heads(q, low), k), -1e30)
        e = jnp.exp(s - jnp.max(s, axis=-1, keepdims=True))
        p = (e * (1.0 / jnp.sum(e, axis=-1, keepdims=True))).astype(BF)
        prob[0, j] = p
        pv = dot(p, v)
        outs.append(jnp.where(low, pv[:padded], pv[padded:]))
    o32 = jnp.concatenate(outs, axis=1)
    o = o32.astype(BF)
    store_relative(ot, 0, o.T, d)
    y = dot(o, wp[...]) + bp[...].astype(F32)
    m1 = keep[at[0] * pl.num_programs(0) + i, 0].astype(F32) * KEEP
    hh = x + m1 * y
    h[0] = hh
    hat2, _ = normalize(hh)
    n2 = (hat2 * g2[...].astype(F32) + b2[...].astype(F32)).astype(BF)
    a2[0] = n2
    store_relative(a2t, 0, n2.T, d)


def feed_kernel(
    at, keep, g0, g1, g2, g3, sg, h_any, a2, a2t_any, w1, b1, w2, b2, gain,
    out, dh, dy, w2s, w2k, w1s, w1k, db1, small,
    dout, dz, z, da2, acts, dus, across, h, a2t, sems, *, images,
):
    t = pl.program_id(0)
    fetch_h = pltpu.make_async_copy(h_any, h, sems.at[0])
    fetch_a2t = pltpu.make_async_copy(a2t_any, a2t, sems.at[1])
    part = g0.shape[1] // images
    ns = sg.shape[1]
    padded = h.shape[1]

    @pl.when(t == 0)
    def _():
        fetch_a2t.start()
        fetch_h.start()
        for i in range(images):
            m2 = keep[at[0] * images + i, 1].astype(F32) * KEEP
            r = i * padded
            dout[r : r + padded, :] = jnp.zeros((padded, dout.shape[1]), F32)
            dout[r : r + ns, :] = sg[i].astype(F32)
            for k, ref in enumerate((g0, g1, g2, g3)):
                lo = r + ns + k * part
                dout[lo : lo + part, :] = unpacked(ref.at[0], i, images, part)
            dz[r : r + padded, :] = (dout[r : r + padded, :] * m2).astype(BF)
        z[...] = jnp.zeros_like(z)
        da2[...] = jnp.zeros_like(da2)

    wa = w1[...]
    wb = w2[...]
    bias = b1[...].astype(F32)
    db = None
    for i in range(images):
        r = slice(i * padded, (i + 1) * padded)
        g, slope = gelu_both(dot(a2[i], wa) + bias)
        acts[r, :] = g.astype(BF)
        du = (slope * dot_nt(dz[r, :], wb)).astype(BF)
        dus[r, :] = du
        s = colsum(du.astype(F32))
        db = s if db is None else db + s
    db1[...] = db
    z[...] += dot(acts[...], wb)
    da2[...] += dot_nt(dus[...], wa)

    @pl.when(t == 0)
    def _():
        fetch_a2t.wait()
        for i in range(images):
            across[:, i * padded : (i + 1) * padded] = a2t[i]

    half = across.shape[0] // 2
    w1k[...] = dot(across[:half, :], dus[...]).astype(BF).reshape(w1k.shape)
    w1s[...] = dot(across[half:, :], dus[...]).astype(BF).reshape(w1s.shape)
    half = acts.shape[1] // 2
    for side, ref in enumerate((w2k, w2s)):
        lo = pl.multiple_of(((at[1] & 1) ^ side) * half, half)
        ref[...] = dot_tn(acts[:, pl.ds(lo, half)], dz[...]).astype(BF)

    @pl.when(t == pl.num_programs(0) - 1)
    def _():
        fetch_h.wait()
        gains = gain[...].astype(F32)
        sums = [jnp.zeros((1, dout.shape[1]), F32) for _ in range(4)]
        for i in range(images):
            m1 = keep[at[0] * images + i, 0].astype(F32) * KEEP
            m2 = keep[at[0] * images + i, 1].astype(F32) * KEEP
            r = slice(i * padded, (i + 1) * padded)
            x = h[i]
            z[r, :] = x + m2 * (z[r, :] + b2[...].astype(F32))
            for k in range(out.shape[0] // images):
                lo = i * padded + ns + k * part
                out[k * images + i] = jnp.concatenate(
                    [z[lo : lo + part, :], z[i * padded : i * padded + ns, :]], axis=0
                ).astype(BF)
            hat, inv = normalize(x)
            up = da2[r, :]
            grad = dout[r, :] + norm_back(up, hat, inv, gains)
            dh[i] = grad
            low = (m1 * grad).astype(BF)
            dy[i] = low
            for j, v in enumerate((up * hat, up, dz[r, :].astype(F32), low.astype(F32))):
                sums[j] = sums[j] + colsum(v)
        small[...] = jnp.concatenate(sums, axis=0)


def heads_kernel(
    at, dy, prob, qkv, wp_any, wq_any, xs, dh, gain, a1t_any, ot_any, small2, db1,
    out, small, flat, cs_any, ck, ds_any, dk_,
    buf, dqkv, dys, wp, wq, a1t, ot, a1, o, cols, cs, ds_, sems, *, images, heads, part, ns,
):
    i = pl.program_id(0)
    width = dy.shape[2]
    padded = dy.shape[1]
    fetches = [
        pltpu.make_async_copy(src, dst, sems.at[j])
        for j, (src, dst) in enumerate(((wp_any, wp), (wq_any, wq), (a1t_any, a1t), (ot_any, ot)))
    ]

    @pl.when(i == 0)
    def _():
        for fetch in fetches:
            fetch.start()
        fetches[0].wait()

    @pl.when(i < images)
    def _():
        low = lax.broadcasted_iota(jnp.int32, (padded, 2 * HEAD_DIM), 1) < HEAD_DIM
        mine = pl.ds(pl.multiple_of(i * padded, padded), padded)
        dys[mine, :] = dy[0]
        do = dot_nt(dy[0], wp[...]).astype(BF)
        for j in range(heads // 2):
            c = j * 2 * HEAD_DIM
            q = qkv[0, :, c : c + 2 * HEAD_DIM]
            k = qkv[0, :, width + c : width + c + 2 * HEAD_DIM]
            v = qkv[0, :, 2 * width + c : 2 * width + c + 2 * HEAD_DIM]
            g = both_heads(do[:, c : c + 2 * HEAD_DIM], low)
            p = prob[0, j]
            p32 = p.astype(F32)
            w = p32 * dot_nt(g, v)
            ds = (w - p32 * jnp.sum(w, axis=-1, keepdims=True)).astype(BF)
            dq = dot(ds, k)
            dq = jnp.where(low, dq[:padded], dq[padded:]) * HEAD_DIM**-0.5
            dk = dot_tn(ds, both_heads(q, low)) * HEAD_DIM**-0.5
            dqkv[mine, c : c + 2 * HEAD_DIM] = dq.astype(BF)
            dqkv[mine, width + c : width + c + 2 * HEAD_DIM] = dk.astype(BF)
            dqkv[mine, 2 * width + c : 2 * width + c + 2 * HEAD_DIM] = dot_tn(p, g).astype(BF)

        @pl.when(i == 0)
        def _():
            fetches[1].wait()

        grads = dqkv[mine, :]
        tops = colsum(grads.astype(F32))
        up = dot_nt(grads, wq[...])
        hat, inv = normalize(xs[0].astype(F32))
        buf[...] = dh[0] + norm_back(up, hat, inv, gain[...].astype(F32))
        for k in range(out.shape[0] // images):
            lo = ns + k * part
            out[k * images + i] = jnp.concatenate(
                [buf[lo : lo + part, :], buf[0:ns, :]], axis=0
            ).astype(BF)
        sums = jnp.concatenate([colsum(up * hat), colsum(up)], axis=0)

        @pl.when(i == 0)
        def _():
            flat[...] = tops
            small[...] = sums

        @pl.when(i > 0)
        def _():
            flat[...] += tops
            small[...] += sums

    @pl.when(i == images)
    def _():
        n = width // OWNERS
        per = db1.shape[1] // width
        eight = jnp.concatenate(
            [small[...], flat[:, :width], flat[:, 2 * width :], small2[...]], axis=0
        ).T
        long = jnp.broadcast_to(db1[...], (8, db1.shape[1])).T
        cols[...] = jnp.zeros_like(cols)
        for b in range(OWNERS):
            rows = pl.ds(pl.multiple_of(place(b ^ at[1]) * n, n), n)
            cols[rows, 0:8] = eight[b * n : (b + 1) * n]
            for j in range(per):
                lo = (b * per + j) * n
                cols[rows, 8 + j : 9 + j] = long[lo : lo + n, 0:1]
        fetches[2].wait()
        fetches[3].wait()

    send = [
        pltpu.make_async_copy(cs, cs_any, sems.at[4]),
        pltpu.make_async_copy(ds_, ds_any, sems.at[5]),
    ]
    half = cs.shape[0]
    for step, lo, c_ref, d_ref in ((images, half, cs, ds_), (images + 1, 0, ck, dk_)):

        @pl.when(i == step)
        def _(lo=lo, c_ref=c_ref, d_ref=d_ref):
            for n in range(images):
                lanes = slice(n * padded, (n + 1) * padded)
                a1[:, lanes] = a1t[n, lo : lo + half, :]
                o[:, lanes] = ot[n, lo : lo + half, :]
            c_ref[:, : 2 * width] = dot(a1[...], dqkv[:, : 2 * width]).astype(BF)
            c_ref[:, 2 * width :] = jnp.zeros((half, COLUMNS), BF)
            d_ref[:, :width] = dot(a1[...], dqkv[:, 2 * width :]).astype(BF)
            d_ref[:, width : 2 * width] = dot(o[...], dys[...]).astype(BF)
            d_ref[:, 2 * width :] = cols[lo : lo + half, :].astype(BF)
            for copy in send:
                copy.start() if lo else copy.wait()


def settle_kernel(both, rows, specials):
    part = rows.shape[1]
    rows[...] = both[:, :part, :]
    specials[...] = both[:, part:, :]


def sum_kernel(*refs, jobs, pick):
    if pick:
        at, *refs = refs
        even = (at[0] & 1) == 0
    terms = [lead for job in jobs for lead in job]
    count = len(terms)
    arrays, outs, bufs, sems = refs[:count], refs[count : -count - 1], refs[-count - 1 : -1], refs[-1]
    fetches = [
        pltpu.make_async_copy(array.at[lead], buf, sems.at[k])
        for k, (array, lead, buf) in enumerate(zip(arrays, terms, bufs))
    ]
    for fetch in fetches:
        fetch.start()
    for fetch in fetches:
        fetch.wait()
    values = []
    for job in jobs:
        total = None
        for ref in bufs[: len(job)]:
            v = ref[...].astype(F32)
            total = v if total is None else total + v
        bufs = bufs[len(job) :]
        values.append(total)
    if pick:
        values = [jnp.where(even, *values), jnp.where(even, *values[::-1])]
    for ref, v in zip(outs, values):
        ref[...] = v.astype(BF)


def sums(jobs, at=None, mib=63):
    arrays, bufs, out_shapes, leads = [], [], [], []
    for job in jobs:
        leads.append([])
        for v, lead in job:
            index = tuple(slice(None) if j is None else j for j in lead)
            kept = tuple(v.shape[k] for k, j in enumerate(lead) if j is None) + v.shape[len(lead) :]
            leads[-1].append(index)
            arrays.append(v)
            bufs.append(pltpu.VMEM(kept, BF))
        out_shapes.append(struct(*kept))
    specs = [ANY] * len(arrays)
    if at is not None:
        specs.insert(0, pl.BlockSpec(memory_space=pltpu.SMEM))
        arrays.insert(0, at)
    return pl.pallas_call(
        partial(sum_kernel, jobs=leads, pick=at is not None),
        in_specs=specs,
        out_shape=out_shapes,
        scratch_shapes=[*bufs, pltpu.SemaphoreType.DMA((len(bufs),))],
        compiler_params=pltpu.CompilerParams(vmem_limit_bytes=mib * 2**20),
        cost_estimate=cost(2),
        name="sums",
    )(*arrays)


def finish_feed_kernel(at, mine, other, *refs):
    fc1, fc2 = refs[-2:]
    even = (at[0] & 1) == 0
    n = fc1.shape[0]
    width = fc2.shape[1]
    for m in range(mine.shape[0]):
        p, q = mine[m].astype(F32), other[m].astype(F32)
        fc1[:, m * width : (m + 1) * width] = jnp.where(even, p, q)
        fc2[m * n : (m + 1) * n, :] = jnp.where(even, q, p)


def finish_kernel(at, mine, other, qkv, proj, *rest):
    vectors, long = rest[:-1], rest[-1]
    width = proj.shape[1]
    even = (at[0] & 1) == 0
    p, q = mine[...].astype(F32), other[...].astype(F32)
    c, d = jnp.where(even, p, q), jnp.where(even, q, p)
    qkv[:, : 2 * width] = c[:, : 2 * width]
    qkv[:, 2 * width :] = d[:, :width]
    proj[...] = d[:, width : 2 * width]
    n = c.shape[0]
    flat = d[:, 2 * width :].T
    row = 0
    for ref in vectors:
        ref[...] = flat[row : row + ref.shape[0]]
        row += ref.shape[0]
    parts = [flat[row + j : row + j + 1] for j in range(long.shape[0] // n)]
    long[...] = jnp.concatenate(parts, axis=1).reshape(long.shape)


def whole(shape, mode=None):
    return pl.BlockSpec(shape, lambda *_: (0,) * len(shape), pipeline_mode=mode)


def params(mib=63):
    return pltpu.CompilerParams(
        dimension_semantics=("arbitrary",), vmem_limit_bytes=mib * 2**20
    )


def cost(us):
    return pl.CostEstimate(flops=int(us * 1e9 * PACE), bytes_accessed=1, transcendentals=0)


ANY = pl.BlockSpec(memory_space=pl.ANY)


def struct(*shape, dtype=BF):
    return jax.ShapeDtypeStruct(shape, dtype)


def after(v, *others):
    return lax.optimization_barrier((v, *others))[0]


def together(*vs):
    return lax.optimization_barrier(vs)


def swap(v, bit):
    return lax.ppermute(v, "dp", [(s, s ^ bit) for s in range(lax.axis_size("dp"))])


def pack(x, blocks):
    images, part, width = x.shape
    x = x.reshape(blocks, images // blocks, part, width)
    base = part // 16 * 16
    return jnp.concatenate(
        [x[:, :, :base].reshape(blocks, -1, width), x[:, :, base:].reshape(blocks, -1, width)], axis=1
    )


def exchange(x):
    return lax.all_to_all(x, "seq", split_axis=0, concat_axis=0, tiled=True)


def settle(both, ns):
    images, rows, width = both.shape
    n = images // 4
    return pl.pallas_call(
        settle_kernel,
        grid=(images // n,),
        in_specs=[pl.BlockSpec((n, rows, width), lambda i: (i, 0, 0))],
        out_specs=[
            pl.BlockSpec((n, rows - ns, width), lambda i: (i, 0, 0)),
            pl.BlockSpec((n, ns, width), lambda i: (i, 0, 0)),
        ],
        out_shape=[struct(images, rows - ns, width), struct(images, ns, width)],
        compiler_params=params(60),
        cost_estimate=cost(2),
        name="settle",
    )(both)


def shards(
    patches, specials, keep_mask, ln1_gain, ln1_bias, qkv_weight, qv_bias, proj_weight, proj_bias,
    ln2_gain, ln2_bias, fc1_weight, fc1_bias, fc2_weight, fc2_bias, grad_patches, grad_specials,
):
    images, part, width = patches.shape
    ns = specials.shape[1]
    groups = lax.axis_size("seq")
    replicas = lax.axis_size("dp")
    hidden = fc1_weight.shape[1]
    heads = width // HEAD_DIM
    n = images // groups
    rows = ns + groups * part
    padded = -(-rows // 16) * 16
    steps = OWNERS // 2
    chunk = hidden // steps
    half = width // 2
    direct = replicas == OWNERS
    me = lax.axis_index("seq")
    d = lax.axis_index("dp") if direct else jnp.int32(0)
    at = jnp.stack([me, d]).astype(jnp.int32)

    def per_image(lo, *shape):
        return pl.BlockSpec((1, *shape), lambda i, *_: (lo + i,) + (0,) * len(shape))

    moved = []
    for k in range(1, groups):
        block = pack(lax.dynamic_slice_in_dim(patches, n * ((me + k) % groups), n), 1)[0]
        moved.append(lax.ppermute(block, "seq", [(s, (s + k) % groups) for s in range(groups)]))
    moved = together(*moved)
    grads = exchange(after(pack(grad_patches, groups), *moved))
    vectors = (
        fc1_bias, ln1_gain, ln1_bias, qv_bias[0], jnp.zeros_like(proj_bias), qv_bias[1], proj_bias,
        ln2_gain, ln2_bias, fc2_bias,
    )
    vectors = jnp.concatenate([v.astype(F32) for v in vectors]).reshape(1, -1)
    first = hidden // width

    def vector(k, wide=1):
        return pl.BlockSpec((1, wide * width), lambda *_: (0, (first + k) // wide))

    shapes = [
        ((padded, width), BF), ((width, padded), BF), ((padded, 3 * width), BF),
        ((heads // 2, 2 * padded, padded), BF), ((width, padded), BF),
        ((padded, width), F32), ((padded, width), BF), ((width, padded), BF),
    ]

    xs, a1t, qkv, prob, ot, h, a2, a2t = pl.pallas_call(
        partial(forward_kernel, rows=rows, heads=heads),
        grid_spec=pltpu.PrefetchScalarGridSpec(
            num_scalar_prefetch=2,
            grid=(n,),
            in_specs=[
                pl.BlockSpec((1, part, width), lambda i, at, keep: (at[0] * n + i, 0, 0)),
                *[whole((n * part, width))] * (groups - 1),
                pl.BlockSpec((1, ns, width), lambda i, at, keep: (at[0] * n + i, 0, 0)),
                vector(0), vector(1), whole(qkv_weight.shape), vector(2, 3),
                whole(proj_weight.shape), vector(5), vector(6), vector(7),
            ],
            out_specs=[per_image(0, *shape) for shape, _ in shapes],
            scratch_shapes=[pltpu.VMEM((padded, width), F32)],
        ),
        out_shape=[struct(n, *shape, dtype=dtype) for shape, dtype in shapes],
        compiler_params=params(63),
        cost_estimate=cost(15),
        name="attention_forward",
    )(
        at, keep_mask, patches, *moved, specials, vectors, vectors, qkv_weight, vectors, proj_weight,
        vectors, vectors, vectors,
    )

    total = n * padded
    h, grads = together(h, grads)

    def owner(t, at):
        return t ^ lax.shift_right_logical(at[1], 1)

    once = pl.Buffered(1)
    out_rows, dh, dy, w2s, w2k, w1s, w1k, db1, small2 = pl.pallas_call(
        partial(feed_kernel, images=n),
        grid_spec=pltpu.PrefetchScalarGridSpec(
            num_scalar_prefetch=2,
            grid=(steps,),
            in_specs=[
                *[
                    pl.BlockSpec((1, n * part, width), lambda t, at, keep, k=k: (k, 0, 0), pipeline_mode=once)
                    for k in range(groups)
                ],
                pl.BlockSpec((n, ns, width), lambda t, at, keep: (at[0], 0, 0)),
                ANY, whole(a2.shape, once), ANY,
                pl.BlockSpec((width, chunk), lambda t, at, keep: (0, owner(t, at))),
                pl.BlockSpec((1, chunk), lambda t, at, keep: (0, owner(t, at))),
                pl.BlockSpec((chunk, width), lambda t, at, keep: (owner(t, at), 0)),
                vector(8), vector(6),
            ],
            out_specs=[
                whole((images, part + ns, width)),
                whole((n, padded, width)), whole((n, padded, width)),
                *[pl.BlockSpec((chunk // 2, width), lambda t, *_: (t, 0))] * 2,
                *[pl.BlockSpec((steps, 1, width // OWNERS, chunk), lambda t, at, keep: (0, owner(t, at), 0, 0))] * 2,
                pl.BlockSpec((1, chunk), lambda t, at, keep: (0, owner(t, at))),
                whole((4, width)),
            ],
            scratch_shapes=[
                pltpu.VMEM((total, width), F32), pltpu.VMEM((total, width), BF),
                pltpu.VMEM((total, width), F32), pltpu.VMEM((total, width), F32),
                pltpu.VMEM((total, chunk), BF), pltpu.VMEM((total, chunk), BF),
                pltpu.VMEM((width, total), BF), pltpu.VMEM(h.shape, F32), pltpu.VMEM(a2t.shape, BF),
                pltpu.SemaphoreType.DMA((2,)),
            ],
        ),
        out_shape=[
            struct(images, part + ns, width),
            struct(n, padded, width, dtype=F32), struct(n, padded, width),
            *[struct(hidden // 2, width)] * 2, *[struct(steps, steps, width // OWNERS, chunk)] * 2,
            struct(1, hidden, dtype=F32), struct(4, width, dtype=F32),
        ],
        compiler_params=params(63),
        cost_estimate=cost(30),
        name="feed_forward",
    )(
        at, keep_mask, *[grads] * groups, grad_specials, h, a2, a2t, fc1_weight, vectors,
        fc2_weight, vectors, vectors,
    )

    n1 = width // OWNERS
    x_half, y_half = (None, 1), (1, None)
    if direct:
        ra, rb = swap(w1s, 1), swap(w2s, 1)
        ra, rb = together(ra, rb)
        wa, wb, ra, rb = (v.reshape(2, 2, steps, n1, chunk) for v in (w1k, w2k, ra, rb))
        as_, bs = sums([[(wa, x_half), (ra, x_half)], [(wb, y_half), (rb, y_half)]], mib=63)
        dy, as_, bs = together(dy, as_, bs)
        qa, qb = swap(as_, 2), swap(bs, 4)
    out_rows = exchange(out_rows)

    def per_image_last(*shape):
        return pl.BlockSpec(
            (1, *shape), lambda i, *_: (jnp.minimum(i, n - 1),) + (0,) * len(shape)
        )

    wide = 2 * width + COLUMNS
    dx_rows, small1, flat, cs, ck, ds_, dk_ = pl.pallas_call(
        partial(heads_kernel, images=n, heads=heads, part=part, ns=ns),
        grid_spec=pltpu.PrefetchScalarGridSpec(
            num_scalar_prefetch=1,
            grid=(n + 2,),
            in_specs=[
                per_image_last(padded, width), per_image_last(heads // 2, 2 * padded, padded),
                per_image_last(padded, 3 * width), ANY, ANY, per_image_last(padded, width),
                per_image_last(padded, width), vector(0), ANY, ANY, whole((4, width)),
                whole((1, hidden)),
            ],
            out_specs=[
                whole((images, part + ns, width)), whole((2, width)), whole((1, 3 * width)),
                ANY, whole((half, wide)), ANY, whole((half, wide)),
            ],
            scratch_shapes=[
                pltpu.VMEM((padded, width), F32), pltpu.VMEM((total, 3 * width), BF),
                pltpu.VMEM((total, width), BF), pltpu.VMEM(proj_weight.shape, BF),
                pltpu.VMEM(qkv_weight.shape, BF), pltpu.VMEM(a1t.shape, BF), pltpu.VMEM(ot.shape, BF),
                pltpu.VMEM((half, total), BF), pltpu.VMEM((half, total), BF),
                pltpu.VMEM((width, COLUMNS), F32), pltpu.VMEM((half, wide), BF),
                pltpu.VMEM((half, wide), BF), pltpu.SemaphoreType.DMA((6,)),
            ],
        ),
        out_shape=[
            struct(images, part + ns, width), struct(2, width, dtype=F32),
            struct(1, 3 * width, dtype=F32), *[struct(half, wide)] * 4,
        ],
        compiler_params=params(63),
        cost_estimate=cost(22),
        name="attention_backward",
    )(at, dy, prob, qkv, proj_weight, qkv_weight, xs, dh, vectors, a1t, ot, small2, db1)

    cs, ds_, out_rows = together(cs, ds_, out_rows)
    dx_rows = exchange(dx_rows)

    if not direct:
        out_rows, out_specials = settle(out_rows, ns)
        dx_rows, dx_specials = settle(dx_rows, ns)
        return (
            out_rows, out_specials, dx_rows, dx_specials,
            *natural_sums(
                w1s, w1k, w2s, w2k, cs, ck, ds_, dk_, flat, small1, small2, db1
            ),
        )

    def near(v):
        return lax.ppermute(v, "seq", [(s, s ^ 1) for s in range(groups)])

    def far(v):
        return lax.ppermute(v, "seq", [(s, s ^ 2) for s in range(groups)])

    qa, qb, cs, ds_ = together(qa, qb, cs, ds_)
    as_, bs = sums(
        [[(wa, (1, 0)), (ra, (1, 0)), (qa, (1,))], [(wb, (0, 1)), (rb, (0, 1)), (qb, (1,))]]
    )
    as_, bs, cs, ds_ = together(as_, bs, cs, ds_)
    ta, tb = swap(as_, 4), swap(bs, 2)
    rc, rd = swap(cs, 1), swap(ds_, 1)
    rc, rd, ck, dk_ = together(rc, rd, ck, dk_)
    wc, wd, rc, rd = (v.reshape(2, 2, 2, n1 // 2, -1) for v in (ck, dk_, rc, rd))
    cs, ds_ = sums([[(wc, x_half), (rc, x_half)], [(wd, y_half), (rd, y_half)]])
    qc, qd = swap(cs, 2), swap(ds_, 4)
    ta, tb, cs = together(ta, tb, cs)
    e, es = sums(
        [
            [(wa, (0, 0)), (ra, (0, 0)), (qa, (0,)), (ta, ())],
            [(wb, (0, 0)), (rb, (0, 0)), (qb, (0,)), (tb, ())],
        ],
        at,
    )
    re = near(es)
    out_rows, out_specials = settle(after(out_rows, e), ns)
    qc, qd, e, out_rows = together(qc, qd, e, out_rows)
    cs, ds_ = sums(
        [[(wc, (1, 0)), (rc, (1, 0)), (qc, (1,))], [(wd, (0, 1)), (rd, (0, 1)), (qd, (1,))]],
        mib=60,
    )
    cs, ds_, re = together(cs, ds_, re)
    tc, td = swap(cs, 4), swap(ds_, 2)
    e = e + re
    e, g = e[: steps // 2], e[steps // 2 :]
    re, rg = far(e), far(g)
    e, g, tc, td = together(e, g, tc, td)
    f1, fs = sums(
        [
            [(wc, (0, 0)), (rc, (0, 0)), (qc, (0,)), (tc, ())],
            [(wd, (0, 0)), (rd, (0, 0)), (qd, (0,)), (td, ())],
        ],
        at,
        mib=60,
    )
    rf = near(fs)
    f1, re, e = together(f1, re, e)
    e = e + re
    re = near(e)
    dx_rows, dx_specials = settle(after(dx_rows, e), ns)
    rf, dx_rows = together(rf, dx_rows)
    f1 = f1 + rf
    rf = far(f1)
    f1, rg, g = together(f1, rg, g)
    g = g + rg
    rg = near(g)
    rf, g = together(rf, g)
    f1 = f1 + rf
    rf = near(f1)
    re, f1 = together(re, f1)
    smem = pl.BlockSpec(memory_space=pltpu.SMEM)
    vmem = pl.BlockSpec(memory_space=pltpu.VMEM)

    def finish_feed(k, mine, other, *before):
        return pl.pallas_call(
            finish_feed_kernel,
            grid=(1,),
            in_specs=[smem, whole(mine.shape), whole(other.shape), *[ANY] * len(before)],
            out_specs=[
                pl.BlockSpec((n1, hidden // 2), lambda i: (0, k)),
                pl.BlockSpec((hidden // OWNERS // 2, width), lambda i: (k, 0)),
            ],
            out_shape=[struct(n1, hidden, dtype=F32), struct(hidden // OWNERS, width, dtype=F32)],
            input_output_aliases={3 + j: j for j in range(len(before))},
            compiler_params=params(60),
            cost_estimate=cost(2),
            name="finish_feed",
        )(at, mine, other, *before)

    d_fc1, d_fc2 = finish_feed(0, e, re)
    rg, d_fc1, d_fc2 = together(rg, d_fc1, d_fc2)
    d_fc1, d_fc2 = finish_feed(1, g, rg, d_fc1, d_fc2)
    rf, d_fc1 = together(rf, d_fc1)
    done = pl.pallas_call(
        finish_kernel,
        in_specs=[smem, vmem, vmem],
        out_shape=[
            struct(n1, 3 * width, dtype=F32), struct(n1, width, dtype=F32),
            *[struct(1, n1, dtype=F32)] * 2, struct(2, n1, dtype=F32),
            *[struct(1, n1, dtype=F32)] * 4, struct(hidden // OWNERS, dtype=F32),
        ],
        compiler_params=pltpu.CompilerParams(vmem_limit_bytes=60 * 2**20),
        cost_estimate=cost(2),
        name="finish",
    )(at, f1.reshape(n1, -1), rf.reshape(n1, -1))
    d_qkv, d_proj, gain1, bias1, d_qv, gain2, bias2, d_fc2b, d_projb, d_fc1b = done

    def one(v):
        return v.reshape(-1)

    return (
        out_rows, out_specials, dx_rows, dx_specials,
        one(gain1), one(bias1), d_qkv, d_qv, d_proj, one(d_projb), one(gain2), one(bias2),
        d_fc1, one(d_fc1b), d_fc2, one(d_fc2b),
    )


def natural_sums(w1s, w1k, w2s, w2k, cs, ck, ds_, dk_, flat, small1, small2, db1):
    width = small1.shape[1]
    replicas = lax.axis_size("dp")

    def natural(sent, kept):
        if kept.ndim == 4:
            kept, sent = (v.transpose(0, 2, 1, 3).reshape(width // 2, -1) for v in (kept, sent))
        v = jnp.stack([kept, sent]).reshape(2, OWNERS // 2, -1, kept.shape[1])
        v = v.transpose(1, 0, 2, 3).reshape(-1, kept.shape[1])
        v = lax.psum_scatter(v, "dp", scatter_dimension=0, tiled=True)
        return lax.psum(v, "seq").astype(F32)

    d_fc1, d_fc2 = natural(w1s, w1k), natural(w2s, w2k)
    d_qk, d_vp = natural(cs, ck), natural(ds_, dk_)
    d_qkv = jnp.concatenate([d_qk[:, : 2 * width], d_vp[:, :width]], axis=1)
    d_proj = d_vp[:, width : 2 * width]
    flat = flat.reshape(3, width)
    vectors = jnp.concatenate([small1, flat[0:1], flat[2:3], small2, db1.reshape(-1, width)], axis=0)
    vectors = lax.psum(vectors, ("dp", "seq"))
    mine = lax.axis_index("dp")

    def shard(v):
        size = v.shape[-1] // replicas
        return lax.dynamic_slice_in_dim(v, mine * size, size, axis=v.ndim - 1)

    s = shard(vectors[:8])
    d_fc1b = shard(vectors[8:].reshape(-1))
    return s[0], s[1], d_qkv, s[2:4], d_proj, s[7], s[4], s[5], d_fc1, d_fc1b, d_fc2, s[6]


def solution(mesh):
    rows = P("dp", "seq", None)
    lead = P("dp", None, None)
    flat = P("dp")
    matrix = P("dp", None)
    return jax.shard_map(
        shards,
        mesh=mesh,
        in_specs=(rows, lead, matrix, *[P()] * 12, rows, lead),
        out_specs=(
            rows, lead, rows, lead, flat, flat, matrix, P(None, "dp"), matrix, flat, flat, flat,
            matrix, flat, matrix, flat,
        ),
        check_vma=False,
    )
```

```python
from functools import partial

import jax
import jax.numpy as jnp
from jax import lax
from jax.experimental import pallas as pl
from jax.experimental.pallas import tpu as pltpu
from jax.sharding import PartitionSpec as P

HEAD_DIM = 64
KEEP = 1.0 / 0.9
EPS = 1e-06
BF = jnp.bfloat16
F32 = jnp.float32
COLUMNS = 128
PACE = 0.3
OWNERS = 8
VMEM = 60 * 2**20

def dot(a, b):
    return lax.dot_general(a, b, (((1,), (0,)), ((), ())), preferred_element_type=F32)


def dot_nt(a, b):
    return lax.dot_general(a, b, (((1,), (1,)), ((), ())), preferred_element_type=F32)


def dot_tn(a, b):
    return lax.dot_general(a, b, (((0,), (0,)), ((), ())), preferred_element_type=F32)


def gelu_both(u):
    cdf = 0.5 + 0.5 * lax.erf(u * 0.5**0.5)
    return u * cdf, cdf + u * (jnp.exp(-0.5 * u * u) * 0.3989422804014327)


def normalize(x):
    center = x - jnp.mean(x, axis=-1, keepdims=True)
    inv = lax.rsqrt(jnp.mean(center * center, axis=-1, keepdims=True) + EPS)
    return center * inv, inv


def norm_back(up, hat, inv, gain):
    e = up * gain
    return inv * (
        e
        - jnp.mean(e, axis=-1, keepdims=True)
        - hat * jnp.mean(e * hat, axis=-1, keepdims=True)
    )


def both_heads(v, low):
    return jnp.concatenate([jnp.where(low, v, BF(0)), jnp.where(low, BF(0), v)], axis=0)


def colsum(v):
    return jnp.sum(v, axis=0, keepdims=True)


def place(b):
    return (b & 1) * (OWNERS // 2) + lax.shift_right_logical(b, 1)


def store_relative(ref, lead, value, d):
    n = value.shape[0] // OWNERS
    for b in range(OWNERS):
        spot = pl.multiple_of(place(b ^ d) * n, n)
        ref[lead, pl.ds(spot, n), :] = value[b * n : (b + 1) * n]


def unpacked(tall, i, images, part):
    base = part // 16 * 16
    rest = part - base
    last = tall[images * base :, :].astype(F32)
    row = last[:rest]
    for j in range(1, images):
        row = jnp.where(i == j, last[j * rest : (j + 1) * rest], row)
    most = tall[pl.ds(pl.multiple_of(i * base, base), base), :].astype(F32)
    return jnp.concatenate([most, row], axis=0)


def forward_kernel(
    at, keep, x0, x1, x2, x3, sp, g1, b1, wq, bq, wp, bp, g2, b2,
    xs, a1t, qkv, prob, ot, h, a2, a2t, buf, *, rows, heads,
):
    i = pl.program_id(0)
    d = at[1]
    part = x0.shape[1]
    ns = sp.shape[1]
    width = x0.shape[2]
    buf[...] = jnp.zeros_like(buf)
    buf[0:ns, :] = sp[0].astype(F32)
    came = [x0[0].astype(F32)]
    came += [unpacked(ref, i, x1.shape[0] // part, part) for ref in (x1, x2, x3)]
    for s in range(len(came)):
        k = (at[0] - s) & 3
        near, far = (jnp.where((k & 1) == 0, came[j], came[j + 1]) for j in (0, 2))
        buf[ns + s * part : ns + (s + 1) * part, :] = jnp.where(k < 2, near, far)
    x = buf[...]
    xs[0] = x.astype(BF)
    hat, _ = normalize(x)
    a1 = (hat * g1[...].astype(F32) + b1[...].astype(F32)).astype(BF)
    store_relative(a1t, 0, a1.T, d)
    both = (dot(a1, wq[...]) + bq[...]).astype(BF)
    qkv[0] = both
    padded = x.shape[0]
    low = lax.broadcasted_iota(jnp.int32, (padded, 2 * HEAD_DIM), 1) < HEAD_DIM
    seen = lax.broadcasted_iota(jnp.int32, (2 * padded, padded), 1) < rows
    outs = []
    for j in range(heads // 2):
        c = j * 2 * HEAD_DIM
        q = both[:, c : c + 2 * HEAD_DIM] * BF(HEAD_DIM**-0.5)
        k = both[:, width + c : width + c + 2 * HEAD_DIM]
        v = both[:, 2 * width + c : 2 * width + c + 2 * HEAD_DIM]
        s = jnp.where(seen, dot_nt(both_heads(q, low), k), -1e30)
        e = jnp.exp(s - jnp.max(s, axis=-1, keepdims=True))
        p = (e * (1.0 / jnp.sum(e, axis=-1, keepdims=True))).astype(BF)
        prob[0, j] = p
        pv = dot(p, v)
        outs.append(jnp.where(low, pv[:padded], pv[padded:]))
    o32 = jnp.concatenate(outs, axis=1)
    o = o32.astype(BF)
    store_relative(ot, 0, o.T, d)
    y = dot(o, wp[...]) + bp[...].astype(F32)
    m1 = keep[at[0] * pl.num_programs(0) + i, 0].astype(F32) * KEEP
    hh = x + m1 * y
    h[0] = hh
    hat2, _ = normalize(hh)
    n2 = (hat2 * g2[...].astype(F32) + b2[...].astype(F32)).astype(BF)
    a2[0] = n2
    store_relative(a2t, 0, n2.T, d)


def feed_kernel(
    at, keep, g0, g1, g2, g3, sg, h_any, a2, a2t_any, w1, b1, w2, b2, gain,
    out, dh, dy, w2s, w2k, w1s, w1k, db1, small,
    dout, dz, z, da2, acts, dus, across, h, a2t, sems, *, images,
):
    t = pl.program_id(0)
    fetch_h = pltpu.make_async_copy(h_any, h, sems.at[0])
    fetch_a2t = pltpu.make_async_copy(a2t_any, a2t, sems.at[1])
    part = g0.shape[1] // images
    ns = sg.shape[1]
    padded = h.shape[1]

    @pl.when(t == 0)
    def _():
        fetch_a2t.start()
        fetch_h.start()
        for i in range(images):
            m2 = keep[at[0] * images + i, 1].astype(F32) * KEEP
            r = i * padded
            dout[r : r + padded, :] = jnp.zeros((padded, dout.shape[1]), F32)
            dout[r : r + ns, :] = sg[i].astype(F32)
            for k, ref in enumerate((g0, g1, g2, g3)):
                lo = r + ns + k * part
                dout[lo : lo + part, :] = unpacked(ref.at[0], i, images, part)
            dz[r : r + padded, :] = (dout[r : r + padded, :] * m2).astype(BF)
        z[...] = jnp.zeros_like(z)
        da2[...] = jnp.zeros_like(da2)

    wa = w1[...]
    wb = w2[...]
    bias = b1[...].astype(F32)
    db = None
    for i in range(images):
        r = slice(i * padded, (i + 1) * padded)
        g, slope = gelu_both(dot(a2[i], wa) + bias)
        acts[r, :] = g.astype(BF)
        du = (slope * dot_nt(dz[r, :], wb)).astype(BF)
        dus[r, :] = du
        s = colsum(du.astype(F32))
        db = s if db is None else db + s
    db1[...] = db
    z[...] += dot(acts[...], wb)
    da2[...] += dot_nt(dus[...], wa)

    @pl.when(t == 0)
    def _():
        fetch_a2t.wait()
        for i in range(images):
            across[:, i * padded : (i + 1) * padded] = a2t[i]

    half = across.shape[0] // 2
    w1k[...] = dot(across[:half, :], dus[...]).astype(BF).reshape(w1k.shape)
    w1s[...] = dot(across[half:, :], dus[...]).astype(BF).reshape(w1s.shape)
    half = acts.shape[1] // 2
    for side, ref in enumerate((w2k, w2s)):
        lo = pl.multiple_of(((at[1] & 1) ^ side) * half, half)
        ref[...] = dot_tn(acts[:, pl.ds(lo, half)], dz[...]).astype(BF)

    @pl.when(t == pl.num_programs(0) - 1)
    def _():
        fetch_h.wait()
        gains = gain[...].astype(F32)
        sums = [jnp.zeros((1, dout.shape[1]), F32) for _ in range(4)]
        for i in range(images):
            m1 = keep[at[0] * images + i, 0].astype(F32) * KEEP
            m2 = keep[at[0] * images + i, 1].astype(F32) * KEEP
            r = slice(i * padded, (i + 1) * padded)
            x = h[i]
            z[r, :] = x + m2 * (z[r, :] + b2[...].astype(F32))
            for k in range(out.shape[0] // images):
                lo = i * padded + ns + k * part
                out[k * images + i] = jnp.concatenate(
                    [z[lo : lo + part, :], z[i * padded : i * padded + ns, :]], axis=0
                ).astype(BF)
            hat, inv = normalize(x)
            up = da2[r, :]
            grad = dout[r, :] + norm_back(up, hat, inv, gains)
            dh[i] = grad
            low = (m1 * grad).astype(BF)
            dy[i] = low
            for j, v in enumerate((up * hat, up, dz[r, :].astype(F32), low.astype(F32))):
                sums[j] = sums[j] + colsum(v)
        small[...] = jnp.concatenate(sums, axis=0)


def heads_kernel(
    at, dy, prob, qkv, wp_any, wq_any, xs, dh, gain, a1t_any, ot_any, small2, db1,
    out_any, small, flat, cs_any, ck_any, ds_any, dk_,
    buf, dqkv, dys, wp, wq, a1t, ot, a1, o, cols, cs, ds_, out, ck, sems, *, images, heads, part, ns,
):
    i = pl.program_id(0)
    width = dy.shape[2]
    padded = dy.shape[1]
    fetches = [
        pltpu.make_async_copy(src, dst, sems.at[j])
        for j, (src, dst) in enumerate(((wp_any, wp), (wq_any, wq), (a1t_any, a1t), (ot_any, ot)))
    ]

    @pl.when(i == 0)
    def _():
        for fetch in fetches:
            fetch.start()
        fetches[0].wait()

    @pl.when(i < images)
    def _():
        low = lax.broadcasted_iota(jnp.int32, (padded, 2 * HEAD_DIM), 1) < HEAD_DIM
        mine = pl.ds(pl.multiple_of(i * padded, padded), padded)
        dys[mine, :] = dy[0]
        do = dot_nt(dy[0], wp[...]).astype(BF)
        for j in range(heads // 2):
            c = j * 2 * HEAD_DIM
            q = qkv[0, :, c : c + 2 * HEAD_DIM]
            k = qkv[0, :, width + c : width + c + 2 * HEAD_DIM]
            v = qkv[0, :, 2 * width + c : 2 * width + c + 2 * HEAD_DIM]
            g = both_heads(do[:, c : c + 2 * HEAD_DIM], low)
            p = prob[0, j]
            p32 = p.astype(F32)
            w = p32 * dot_nt(g, v)
            ds = (w - p32 * jnp.sum(w, axis=-1, keepdims=True)).astype(BF)
            dq = dot(ds, k)
            dq = jnp.where(low, dq[:padded], dq[padded:]) * HEAD_DIM**-0.5
            dk = dot_tn(ds, both_heads(q, low)) * HEAD_DIM**-0.5
            dqkv[mine, c : c + 2 * HEAD_DIM] = dq.astype(BF)
            dqkv[mine, width + c : width + c + 2 * HEAD_DIM] = dk.astype(BF)
            dqkv[mine, 2 * width + c : 2 * width + c + 2 * HEAD_DIM] = dot_tn(p, g).astype(BF)

        @pl.when(i == 0)
        def _():
            fetches[1].wait()

        grads = dqkv[mine, :]
        tops = colsum(grads.astype(F32))
        up = dot_nt(grads, wq[...])
        hat, inv = normalize(xs[0].astype(F32))
        buf[...] = dh[0] + norm_back(up, hat, inv, gain[...].astype(F32))
        for k in range(out.shape[0] // images):
            lo = ns + k * part
            out[k * images + i] = jnp.concatenate(
                [buf[lo : lo + part, :], buf[0:ns, :]], axis=0
            ).astype(BF)
        sums = jnp.concatenate([colsum(up * hat), colsum(up)], axis=0)

        @pl.when(i == 0)
        def _():
            flat[...] = tops
            small[...] = sums

        @pl.when(i > 0)
        def _():
            flat[...] += tops
            small[...] += sums

    @pl.when(i == images)
    def _():
        n = width // OWNERS
        per = db1.shape[1] // width
        eight = jnp.concatenate(
            [small[...], flat[:, :width], flat[:, 2 * width :], small2[...]], axis=0
        ).T
        long = jnp.broadcast_to(db1[...], (8, db1.shape[1])).T
        cols[...] = jnp.zeros_like(cols)
        for b in range(OWNERS):
            rows = pl.ds(pl.multiple_of(place(b ^ at[1]) * n, n), n)
            cols[rows, 0:8] = eight[b * n : (b + 1) * n]
            for j in range(per):
                lo = (b * per + j) * n
                cols[rows, 8 + j : 9 + j] = long[lo : lo + n, 0:1]
        fetches[2].wait()
        fetches[3].wait()

    send = [
        pltpu.make_async_copy(cs, cs_any, sems.at[4]),
        pltpu.make_async_copy(ds_, ds_any, sems.at[5]),
        pltpu.make_async_copy(out, out_any, sems.at[6]),
    ]
    send_ck = pltpu.make_async_copy(ck, ck_any, sems.at[7])
    half = cs.shape[0]
    for step, lo, c_ref, d_ref in ((images, half, cs, ds_), (images + 1, 0, ck, dk_)):

        @pl.when(i == step)
        def _(lo=lo, c_ref=c_ref, d_ref=d_ref):
            for n in range(images):
                lanes = slice(n * padded, (n + 1) * padded)
                a1[:, lanes] = a1t[n, lo : lo + half, :]
                o[:, lanes] = ot[n, lo : lo + half, :]
            c_ref[:, : 2 * width] = dot(a1[...], dqkv[:, : 2 * width]).astype(BF)
            c_ref[:, 2 * width :] = jnp.zeros((half, COLUMNS), BF)
            if not lo:
                send_ck.start()
            d_ref[:, :width] = dot(a1[...], dqkv[:, 2 * width :]).astype(BF)
            d_ref[:, width : 2 * width] = dot(o[...], dys[...]).astype(BF)
            d_ref[:, 2 * width :] = cols[lo : lo + half, :].astype(BF)
            for copy in send:
                copy.start() if lo else copy.wait()
            if not lo:
                send_ck.wait()


def settle_kernel(both, rows, specials):
    part = rows.shape[1]
    rows[...] = both[:, :part, :]
    specials[...] = both[:, part:, :]


def sum_kernel(*refs, jobs, pick):
    if pick:
        at, *refs = refs
        even = (at[0] & 1) == 0
    terms = [lead for job in jobs for lead in job]
    count = len(terms)
    arrays, outs, bufs, sems = refs[:count], refs[count : -count - 1], refs[-count - 1 : -1], refs[-1]
    fetches = [
        pltpu.make_async_copy(array.at[lead], buf, sems.at[k])
        for k, (array, lead, buf) in enumerate(zip(arrays, terms, bufs))
    ]
    for fetch in fetches:
        fetch.start()
    for fetch in fetches:
        fetch.wait()
    values = []
    for job in jobs:
        total = None
        for ref in bufs[: len(job)]:
            v = ref[...].astype(F32)
            total = v if total is None else total + v
        bufs = bufs[len(job) :]
        values.append(total)
    if pick:
        values = [jnp.where(even, *values), jnp.where(even, *values[::-1])]
    for ref, v in zip(outs, values):
        ref[...] = v.astype(BF)


def sums(jobs, at=None, mib=63):
    arrays, bufs, out_shapes, leads = [], [], [], []
    for job in jobs:
        leads.append([])
        for v, lead in job:
            index = tuple(slice(None) if j is None else j for j in lead)
            kept = tuple(v.shape[k] for k, j in enumerate(lead) if j is None) + v.shape[len(lead) :]
            leads[-1].append(index)
            arrays.append(v)
            bufs.append(pltpu.VMEM(kept, BF))
        out_shapes.append(struct(*kept))
    specs = [ANY] * len(arrays)
    if at is not None:
        specs.insert(0, pl.BlockSpec(memory_space=pltpu.SMEM))
        arrays.insert(0, at)
    return pl.pallas_call(
        partial(sum_kernel, jobs=leads, pick=at is not None),
        in_specs=specs,
        out_shape=out_shapes,
        scratch_shapes=[*bufs, pltpu.SemaphoreType.DMA((len(bufs),))],
        compiler_params=pltpu.CompilerParams(vmem_limit_bytes=mib * 2**20),
        cost_estimate=cost(2),
        name="sums",
    )(*arrays)


def finish_feed_kernel(at, mine, other, *refs):
    fc1, fc2 = refs[-2:]
    even = (at[0] & 1) == 0
    n = fc1.shape[0]
    width = fc2.shape[1]
    for m in range(mine.shape[0]):
        p, q = mine[m].astype(F32), other[m].astype(F32)
        fc1[:, m * width : (m + 1) * width] = jnp.where(even, p, q)
        fc2[m * n : (m + 1) * n, :] = jnp.where(even, q, p)


def finish_kernel(at, mine, other, qkv, proj, *rest):
    vectors, long = rest[:-1], rest[-1]
    width = proj.shape[1]
    even = (at[0] & 1) == 0
    p, q = mine[...].astype(F32), other[...].astype(F32)
    c, d = jnp.where(even, p, q), jnp.where(even, q, p)
    qkv[:, : 2 * width] = c[:, : 2 * width]
    qkv[:, 2 * width :] = d[:, :width]
    proj[...] = d[:, width : 2 * width]
    n = c.shape[0]
    flat = d[:, 2 * width :].T
    row = 0
    for ref in vectors:
        ref[...] = flat[row : row + ref.shape[0]]
        row += ref.shape[0]
    parts = [flat[row + j : row + j + 1] for j in range(long.shape[0] // n)]
    long[...] = jnp.concatenate(parts, axis=1).reshape(long.shape)


def whole(shape, mode=None):
    return pl.BlockSpec(shape, lambda *_: (0,) * len(shape), pipeline_mode=mode)


def params(mib=63):
    return pltpu.CompilerParams(
        dimension_semantics=("arbitrary",), vmem_limit_bytes=mib * 2**20
    )


def cost(us):
    return pl.CostEstimate(flops=int(us * 1e9 * PACE), bytes_accessed=1, transcendentals=0)


ANY = pl.BlockSpec(memory_space=pl.ANY)


def struct(*shape, dtype=BF):
    return jax.ShapeDtypeStruct(shape, dtype)


def after(v, *others):
    return lax.optimization_barrier((v, *others))[0]


def together(*vs):
    return lax.optimization_barrier(vs)


def swap(v, bit):
    return lax.ppermute(v, "dp", [(s, s ^ bit) for s in range(lax.axis_size("dp"))])


def pack(x, blocks):
    images, part, width = x.shape
    x = x.reshape(blocks, images // blocks, part, width)
    base = part // 16 * 16
    return jnp.concatenate(
        [x[:, :, :base].reshape(blocks, -1, width), x[:, :, base:].reshape(blocks, -1, width)], axis=1
    )


def exchange(x):
    return lax.all_to_all(x, "seq", split_axis=0, concat_axis=0, tiled=True)


def settle(both, ns):
    images, rows, width = both.shape
    n = images // 4
    return pl.pallas_call(
        settle_kernel,
        grid=(images // n,),
        in_specs=[pl.BlockSpec((n, rows, width), lambda i: (i, 0, 0))],
        out_specs=[
            pl.BlockSpec((n, rows - ns, width), lambda i: (i, 0, 0)),
            pl.BlockSpec((n, ns, width), lambda i: (i, 0, 0)),
        ],
        out_shape=[struct(images, rows - ns, width), struct(images, ns, width)],
        compiler_params=params(60),
        cost_estimate=cost(2),
        name="settle",
    )(both)


def shards(
    patches, specials, keep_mask, ln1_gain, ln1_bias, qkv_weight, qv_bias, proj_weight, proj_bias,
    ln2_gain, ln2_bias, fc1_weight, fc1_bias, fc2_weight, fc2_bias, grad_patches, grad_specials,
):
    images, part, width = patches.shape
    ns = specials.shape[1]
    groups = lax.axis_size("seq")
    replicas = lax.axis_size("dp")
    hidden = fc1_weight.shape[1]
    heads = width // HEAD_DIM
    n = images // groups
    rows = ns + groups * part
    padded = -(-rows // 16) * 16
    steps = OWNERS // 2
    chunk = hidden // steps
    half = width // 2
    direct = replicas == OWNERS
    me = lax.axis_index("seq")
    d = lax.axis_index("dp") if direct else jnp.int32(0)
    at = jnp.stack([me, d]).astype(jnp.int32)

    def per_image(lo, *shape):
        return pl.BlockSpec((1, *shape), lambda i, *_: (lo + i,) + (0,) * len(shape))

    moved = []
    for k in range(1, groups):
        block = pack(lax.dynamic_slice_in_dim(patches, n * ((me + k) % groups), n), 1)[0]
        moved.append(lax.ppermute(block, "seq", [(s, (s + k) % groups) for s in range(groups)]))
    moved = together(*moved)
    grads = exchange(after(pack(grad_patches, groups), *moved))
    vectors = (
        fc1_bias, ln1_gain, ln1_bias, qv_bias[0], jnp.zeros_like(proj_bias), qv_bias[1], proj_bias,
        ln2_gain, ln2_bias, fc2_bias,
    )
    vectors = jnp.concatenate([v.astype(F32) for v in vectors]).reshape(1, -1)
    first = hidden // width

    def vector(k, wide=1):
        return pl.BlockSpec((1, wide * width), lambda *_: (0, (first + k) // wide))

    shapes = [
        ((padded, width), BF), ((width, padded), BF), ((padded, 3 * width), BF),
        ((heads // 2, 2 * padded, padded), BF), ((width, padded), BF),
        ((padded, width), F32), ((padded, width), BF), ((width, padded), BF),
    ]

    xs, a1t, qkv, prob, ot, h, a2, a2t = pl.pallas_call(
        partial(forward_kernel, rows=rows, heads=heads),
        grid_spec=pltpu.PrefetchScalarGridSpec(
            num_scalar_prefetch=2,
            grid=(n,),
            in_specs=[
                pl.BlockSpec((1, part, width), lambda i, at, keep: (at[0] * n + i, 0, 0)),
                *[whole((n * part, width))] * (groups - 1),
                pl.BlockSpec((1, ns, width), lambda i, at, keep: (at[0] * n + i, 0, 0)),
                vector(0), vector(1), whole(qkv_weight.shape), vector(2, 3),
                whole(proj_weight.shape), vector(5), vector(6), vector(7),
            ],
            out_specs=[per_image(0, *shape) for shape, _ in shapes],
            scratch_shapes=[pltpu.VMEM((padded, width), F32)],
        ),
        out_shape=[struct(n, *shape, dtype=dtype) for shape, dtype in shapes],
        compiler_params=params(63),
        cost_estimate=cost(15),
        name="attention_forward",
    )(
        at, keep_mask, patches, *moved, specials, vectors, vectors, qkv_weight, vectors, proj_weight,
        vectors, vectors, vectors,
    )

    total = n * padded
    h, grads = together(h, grads)

    def owner(t, at):
        return t ^ lax.shift_right_logical(at[1], 1)

    once = pl.Buffered(1)
    out_rows, dh, dy, w2s, w2k, w1s, w1k, db1, small2 = pl.pallas_call(
        partial(feed_kernel, images=n),
        grid_spec=pltpu.PrefetchScalarGridSpec(
            num_scalar_prefetch=2,
            grid=(steps,),
            in_specs=[
                *[
                    pl.BlockSpec((1, n * part, width), lambda t, at, keep, k=k: (k, 0, 0), pipeline_mode=once)
                    for k in range(groups)
                ],
                pl.BlockSpec((n, ns, width), lambda t, at, keep: (at[0], 0, 0)),
                ANY, whole(a2.shape, once), ANY,
                pl.BlockSpec((width, chunk), lambda t, at, keep: (0, owner(t, at))),
                pl.BlockSpec((1, chunk), lambda t, at, keep: (0, owner(t, at))),
                pl.BlockSpec((chunk, width), lambda t, at, keep: (owner(t, at), 0)),
                vector(8), vector(6),
            ],
            out_specs=[
                whole((images, part + ns, width)),
                whole((n, padded, width)), whole((n, padded, width)),
                *[pl.BlockSpec((chunk // 2, width), lambda t, *_: (t, 0))] * 2,
                *[pl.BlockSpec((steps, 1, width // OWNERS, chunk), lambda t, at, keep: (0, owner(t, at), 0, 0))] * 2,
                pl.BlockSpec((1, chunk), lambda t, at, keep: (0, owner(t, at))),
                whole((4, width)),
            ],
            scratch_shapes=[
                pltpu.VMEM((total, width), F32), pltpu.VMEM((total, width), BF),
                pltpu.VMEM((total, width), F32), pltpu.VMEM((total, width), F32),
                pltpu.VMEM((total, chunk), BF), pltpu.VMEM((total, chunk), BF),
                pltpu.VMEM((width, total), BF), pltpu.VMEM(h.shape, F32), pltpu.VMEM(a2t.shape, BF),
                pltpu.SemaphoreType.DMA((2,)),
            ],
        ),
        out_shape=[
            struct(images, part + ns, width),
            struct(n, padded, width, dtype=F32), struct(n, padded, width),
            *[struct(hidden // 2, width)] * 2, *[struct(steps, steps, width // OWNERS, chunk)] * 2,
            struct(1, hidden, dtype=F32), struct(4, width, dtype=F32),
        ],
        compiler_params=params(63),
        cost_estimate=cost(30),
        name="feed_forward",
    )(
        at, keep_mask, *[grads] * groups, grad_specials, h, a2, a2t, fc1_weight, vectors,
        fc2_weight, vectors, vectors,
    )

    n1 = width // OWNERS
    x_half, y_half = (None, 1), (1, None)
    if direct:
        ra, rb = swap(w1s, 1), swap(w2s, 1)
        ra, rb = together(ra, rb)
        wa, wb, ra, rb = (v.reshape(2, 2, steps, n1, chunk) for v in (w1k, w2k, ra, rb))
        as_, bs = sums([[(wa, x_half), (ra, x_half)], [(wb, y_half), (rb, y_half)]], mib=63)
        dy, as_, bs = together(dy, as_, bs)
        qa, qb = swap(as_, 2), swap(bs, 4)
    out_rows = exchange(out_rows)

    def per_image_last(*shape):
        return pl.BlockSpec(
            (1, *shape), lambda i, *_: (jnp.minimum(i, n - 1),) + (0,) * len(shape)
        )

    wide = 2 * width + COLUMNS
    dx_rows, small1, flat, cs, ck, ds_, dk_ = pl.pallas_call(
        partial(heads_kernel, images=n, heads=heads, part=part, ns=ns),
        grid_spec=pltpu.PrefetchScalarGridSpec(
            num_scalar_prefetch=1,
            grid=(n + 2,),
            in_specs=[
                per_image_last(padded, width), per_image_last(heads // 2, 2 * padded, padded),
                per_image_last(padded, 3 * width), ANY, ANY, per_image_last(padded, width),
                per_image_last(padded, width), vector(0), ANY, ANY, whole((4, width)),
                whole((1, hidden)),
            ],
            out_specs=[
                ANY, whole((2, width)), whole((1, 3 * width)),
                ANY, ANY, ANY, whole((half, wide)),
            ],
            scratch_shapes=[
                pltpu.VMEM((padded, width), F32), pltpu.VMEM((total, 3 * width), BF),
                pltpu.VMEM((total, width), BF), pltpu.VMEM(proj_weight.shape, BF),
                pltpu.VMEM(qkv_weight.shape, BF), pltpu.VMEM(a1t.shape, BF), pltpu.VMEM(ot.shape, BF),
                pltpu.VMEM((half, total), BF), pltpu.VMEM((half, total), BF),
                pltpu.VMEM((width, COLUMNS), F32), pltpu.VMEM((half, wide), BF),
                pltpu.VMEM((half, wide), BF), pltpu.VMEM((images, part + ns, width), BF),
                pltpu.VMEM((half, wide), BF), pltpu.SemaphoreType.DMA((8,)),
            ],
        ),
        out_shape=[
            struct(images, part + ns, width), struct(2, width, dtype=F32),
            struct(1, 3 * width, dtype=F32), *[struct(half, wide)] * 4,
        ],
        compiler_params=params(63),
        cost_estimate=cost(22),
        name="attention_backward",
    )(at, dy, prob, qkv, proj_weight, qkv_weight, xs, dh, vectors, a1t, ot, small2, db1)

    cs, ds_, out_rows = together(cs, ds_, out_rows)
    dx_rows = exchange(dx_rows)

    if not direct:
        out_rows, out_specials = settle(out_rows, ns)
        dx_rows, dx_specials = settle(dx_rows, ns)
        return (
            out_rows, out_specials, dx_rows, dx_specials,
            *natural_sums(
                w1s, w1k, w2s, w2k, cs, ck, ds_, dk_, flat, small1, small2, db1
            ),
        )

    def near(v):
        return lax.ppermute(v, "seq", [(s, s ^ 1) for s in range(groups)])

    def far(v):
        return lax.ppermute(v, "seq", [(s, s ^ 2) for s in range(groups)])

    qa, qb, cs, ds_ = together(qa, qb, cs, ds_)
    as_, bs = sums(
        [[(wa, (1, 0)), (ra, (1, 0)), (qa, (1,))], [(wb, (0, 1)), (rb, (0, 1)), (qb, (1,))]]
    )
    as_, bs, cs, ds_ = together(as_, bs, cs, ds_)
    ta, tb = swap(as_, 4), swap(bs, 2)
    rc, rd = swap(cs, 1), swap(ds_, 1)
    rc, rd, ck, dk_ = together(rc, rd, ck, dk_)
    wc, wd, rc, rd = (v.reshape(2, 2, 2, n1 // 2, -1) for v in (ck, dk_, rc, rd))
    cs, ds_ = sums([[(wc, x_half), (rc, x_half)], [(wd, y_half), (rd, y_half)]])
    qc, qd = swap(cs, 2), swap(ds_, 4)
    ta, tb, cs = together(ta, tb, cs)
    e, es = sums(
        [
            [(wa, (0, 0)), (ra, (0, 0)), (qa, (0,)), (ta, ())],
            [(wb, (0, 0)), (rb, (0, 0)), (qb, (0,)), (tb, ())],
        ],
        at,
    )
    re = near(es)
    out_rows, out_specials = settle(after(out_rows, e), ns)
    qc, qd, e, out_rows = together(qc, qd, e, out_rows)
    cs, ds_ = sums(
        [[(wc, (1, 0)), (rc, (1, 0)), (qc, (1,))], [(wd, (0, 1)), (rd, (0, 1)), (qd, (1,))]],
        mib=60,
    )
    cs, ds_, re = together(cs, ds_, re)
    tc, td = swap(cs, 4), swap(ds_, 2)
    e = e + re
    e, g = e[: steps // 2], e[steps // 2 :]
    re, rg = far(e), far(g)
    e, g, tc, td = together(e, g, tc, td)
    f1, fs = sums(
        [
            [(wc, (0, 0)), (rc, (0, 0)), (qc, (0,)), (tc, ())],
            [(wd, (0, 0)), (rd, (0, 0)), (qd, (0,)), (td, ())],
        ],
        at,
        mib=60,
    )
    rf = near(fs)
    f1, re, e = together(f1, re, e)
    e = e + re
    re = near(e)
    dx_rows, dx_specials = settle(after(dx_rows, e), ns)
    rf, dx_rows = together(rf, dx_rows)
    f1 = f1 + rf
    rf = far(f1)
    f1, rg, g = together(f1, rg, g)
    g = g + rg
    rg = near(g)
    rf, g = together(rf, g)
    f1 = f1 + rf
    rf = near(f1)
    re, f1 = together(re, f1)
    smem = pl.BlockSpec(memory_space=pltpu.SMEM)
    vmem = pl.BlockSpec(memory_space=pltpu.VMEM)

    def finish_feed(k, mine, other, *before):
        return pl.pallas_call(
            finish_feed_kernel,
            grid=(1,),
            in_specs=[smem, whole(mine.shape), whole(other.shape), *[ANY] * len(before)],
            out_specs=[
                pl.BlockSpec((n1, hidden // 2), lambda i: (0, k)),
                pl.BlockSpec((hidden // OWNERS // 2, width), lambda i: (k, 0)),
            ],
            out_shape=[struct(n1, hidden, dtype=F32), struct(hidden // OWNERS, width, dtype=F32)],
            input_output_aliases={3 + j: j for j in range(len(before))},
            compiler_params=params(60),
            cost_estimate=cost(2),
            name="finish_feed",
        )(at, mine, other, *before)

    d_fc1, d_fc2 = finish_feed(0, e, re)
    rg, d_fc1, d_fc2 = together(rg, d_fc1, d_fc2)
    d_fc1, d_fc2 = finish_feed(1, g, rg, d_fc1, d_fc2)
    rf, d_fc1 = together(rf, d_fc1)
    done = pl.pallas_call(
        finish_kernel,
        in_specs=[smem, vmem, vmem],
        out_shape=[
            struct(n1, 3 * width, dtype=F32), struct(n1, width, dtype=F32),
            *[struct(1, n1, dtype=F32)] * 2, struct(2, n1, dtype=F32),
            *[struct(1, n1, dtype=F32)] * 4, struct(hidden // OWNERS, dtype=F32),
        ],
        compiler_params=pltpu.CompilerParams(vmem_limit_bytes=60 * 2**20),
        cost_estimate=cost(2),
        name="finish",
    )(at, f1.reshape(n1, -1), rf.reshape(n1, -1))
    d_qkv, d_proj, gain1, bias1, d_qv, gain2, bias2, d_fc2b, d_projb, d_fc1b = done

    def one(v):
        return v.reshape(-1)

    return (
        out_rows, out_specials, dx_rows, dx_specials,
        one(gain1), one(bias1), d_qkv, d_qv, d_proj, one(d_projb), one(gain2), one(bias2),
        d_fc1, one(d_fc1b), d_fc2, one(d_fc2b),
    )


def natural_sums(w1s, w1k, w2s, w2k, cs, ck, ds_, dk_, flat, small1, small2, db1):
    width = small1.shape[1]
    replicas = lax.axis_size("dp")

    def natural(sent, kept):
        if kept.ndim == 4:
            kept, sent = (v.transpose(0, 2, 1, 3).reshape(width // 2, -1) for v in (kept, sent))
        v = jnp.stack([kept, sent]).reshape(2, OWNERS // 2, -1, kept.shape[1])
        v = v.transpose(1, 0, 2, 3).reshape(-1, kept.shape[1])
        v = lax.psum_scatter(v, "dp", scatter_dimension=0, tiled=True)
        return lax.psum(v, "seq").astype(F32)

    d_fc1, d_fc2 = natural(w1s, w1k), natural(w2s, w2k)
    d_qk, d_vp = natural(cs, ck), natural(ds_, dk_)
    d_qkv = jnp.concatenate([d_qk[:, : 2 * width], d_vp[:, :width]], axis=1)
    d_proj = d_vp[:, width : 2 * width]
    flat = flat.reshape(3, width)
    vectors = jnp.concatenate([small1, flat[0:1], flat[2:3], small2, db1.reshape(-1, width)], axis=0)
    vectors = lax.psum(vectors, ("dp", "seq"))
    mine = lax.axis_index("dp")

    def shard(v):
        size = v.shape[-1] // replicas
        return lax.dynamic_slice_in_dim(v, mine * size, size, axis=v.ndim - 1)

    s = shard(vectors[:8])
    d_fc1b = shard(vectors[8:].reshape(-1))
    return s[0], s[1], d_qkv, s[2:4], d_proj, s[7], s[4], s[5], d_fc1, d_fc1b, d_fc2, s[6]


def solution(mesh):
    rows = P("dp", "seq", None)
    lead = P("dp", None, None)
    flat = P("dp")
    matrix = P("dp", None)
    return jax.shard_map(
        shards,
        mesh=mesh,
        in_specs=(rows, lead, matrix, *[P()] * 12, rows, lead),
        out_specs=(
            rows, lead, rows, lead, flat, flat, matrix, P(None, "dp"), matrix, flat, flat, flat,
            matrix, flat, matrix, flat,
        ),
        check_vma=False,
    )
```
